32 devices in a mesh: dp: 2 (over x), zero: 4 (over z), seq: 4 (over y, core).
Axes of the slice: x: 2, y: 2, z: 4, core: 2. Of those that a mesh axis runs over, the one named last changes fastest.
Arguments:
- inputs: bfloat16 [8, 1024, 2048], P(('dp', 'zero'), 'seq'), may hold values from -8 to 8
- out_grad: bfloat16 [8, 1024, 2048], P(('dp', 'zero'), 'seq'), may hold values from -6 to 6
- vectors: float32 [26624], P(('zero', 'seq')), may hold values from -1 to 1.5
- qkv_weight: float32 [2048, 6144], P(('zero', 'seq')), may hold values from -1 to 1
- dense_weight: float32 [2048, 2048], P(('zero', 'seq')), may hold values from -1.5 to 1.5
- up_weight: float32 [2048, 8192], P(('zero', 'seq')), may hold values from -0.125 to 0.125
- down_weight: float32 [8192, 2048], P(None, ('zero', 'seq')), may hold values from -1 to 1
- vectors_first: float32 [26624], P(('zero', 'seq')), may hold values from -28 to 28
- qkv_first: float32 [2048, 6144], P(('zero', 'seq')), may hold values from -40 to 40
- dense_first: float32 [2048, 2048], P(('zero', 'seq')), may hold values from -6 to 6
- up_first: float32 [2048, 8192], P(('zero', 'seq')), may hold values from -28 to 28
- down_first: float32 [8192, 2048], P(None, ('zero', 'seq')), may hold values from -28 to 28
- vectors_second: float32 [26624], P(('zero', 'seq')), may hold values from 163.84 to 983.04
- qkv_second: float32 [2048, 6144], P(('zero', 'seq')), may hold values from 409.6 to 1638.4
- dense_second: float32 [2048, 2048], P(('zero', 'seq')), may hold values from 3.2 to 16
- up_second: float32 [2048, 8192], P(('zero', 'seq')), may hold values from 163.84 to 819.2
- down_second: float32 [8192, 2048], P(None, ('zero', 'seq')), may hold values from 163.84 to 655.36
Outputs:
- outputs: bfloat16 [8, 1024, 2048], P(('dp', 'zero'), 'seq')
- input_grad: bfloat16 [8, 1024, 2048], P(('dp', 'zero'), 'seq')
- vectors_grad: float32 [26624], P(('zero', 'seq'))
- qkv_grad: float32 [2048, 6144], P(('zero', 'seq'))
- dense_grad: float32 [2048, 2048], P(('zero', 'seq'))
- up_grad: float32 [2048, 8192], P(('zero', 'seq'))
- down_grad: float32 [8192, 2048], P(None, ('zero', 'seq'))
- vectors_new: float32 [26624], P(('zero', 'seq'))
- qkv_new: float32 [2048, 6144], P(('zero', 'seq'))
- dense_new: float32 [2048, 2048], P(('zero', 'seq'))
- up_new: float32 [2048, 8192], P(('zero', 'seq'))
- down_new: float32 [8192, 2048], P(None, ('zero', 'seq'))
- vectors_first_new: float32 [26624], P(('zero', 'seq'))
- qkv_first_new: float32 [2048, 6144], P(('zero', 'seq'))
- dense_first_new: float32 [2048, 2048], P(('zero', 'seq'))
- up_first_new: float32 [2048, 8192], P(('zero', 'seq'))
- down_first_new: float32 [8192, 2048], P(None, ('zero', 'seq'))
- vectors_second_new: float32 [26624], P(('zero', 'seq'))
- qkv_second_new: float32 [2048, 6144], P(('zero', 'seq'))
- dense_second_new: float32 [2048, 2048], P(('zero', 'seq'))
- up_second_new: float32 [2048, 8192], P(('zero', 'seq'))
- down_second_new: float32 [8192, 2048], P(None, ('zero', 'seq'))
The draws below stay inside these ranges and needn't reach their ends.
All inputs are finite; a program needn't handle non-finite values.
Results may differ from the reference program's by a relative error of at most 0.012.
Values may be sent and summed in bfloat16 or wider, within the bound.
A program may use at most 896 MiB of HBM per device.

```python
import math
import jax
import jax.numpy as jnp
from jax import lax

D = 2048
HEADS = 8
HEAD_DIM = 256
FF = 8192
ROT = 64
LENGTH = 1024
ADAM_STEP = 4
BATCH = 8


def draw_inputs(key, part):
    noise_key = jax.random.fold_in(key, 5)
    sample = jax.random.truncated_normal(noise_key, -6.0, 6.0, (BATCH, LENGTH, D), jnp.float32)
    return sample.astype(jnp.bfloat16)


def draw_vectors(key, part):
    element = jnp.arange(9 * D + FF)
    is_gain = (element < D) | (element >= 6 * D) & (element < 7 * D)
    gain_key, shift_key = jax.random.split(jax.random.fold_in(key, 23))
    gain_values = jax.random.uniform(gain_key, (9 * D + FF,), jnp.float32, 0.6, 1.4)
    shifts = 0.25 * jax.random.truncated_normal(shift_key, -3.0, 3.0, (9 * D + FF,), jnp.float32)
    return jnp.where(is_gain, gain_values, shifts)


def draw_qkv_weight(key, part):
    base_key = jax.random.fold_in(key, 17)
    matrix = jax.random.truncated_normal(base_key, -5.0, 5.0, (D, 3 * D), jnp.float32) / math.sqrt(D)
    return matrix


def draw_dense_weight(key, part):
    base_key = jax.random.fold_in(key, 31)
    matrix = jax.random.truncated_normal(base_key, -6.0, 6.0, (D, D), jnp.float32) * math.sqrt(LENGTH / (8.0 * D))
    return matrix


def draw_down_weight(key, part):
    base_key = jax.random.fold_in(key, 37)
    matrix = jax.random.truncated_normal(base_key, -6.0, 6.0, (FF, D), jnp.float32) / math.sqrt(FF)
    return matrix


def level_of(stream_key, dims, shards, least, high):
    level = 1.0
    for dim, blocks in shards:
        draws = jax.random.uniform(jax.random.fold_in(jax.random.fold_in(stream_key, 6), dim), (blocks,), jnp.float32, least / len(shards), high / len(shards))
        level = level * jnp.repeat(jnp.exp(draws), dims[dim] // blocks).reshape((-1,) + (1,) * (len(dims) - 1 - dim))
    return level


def noise(own_key, extent, scale, reach, shards=(), held_as=jnp.bfloat16):
    values = jax.random.normal(own_key, extent, jnp.float32) * scale
    if len(shards) > 0:
        values = level_of(own_key, extent, shards, -0.22, 0.18) * values
    return jnp.clip(values, min=-reach, max=reach).astype(held_as)


def setup_inputs(seed: int = 0) -> dict:
    keys = jax.random.split(jax.random.key(seed), 18)
    return {
        "inputs": draw_inputs(jax.random.fold_in(keys[17], 71), 0),
        "out_grad": noise(keys[1], (BATCH, LENGTH, D), 1.0, 6.0, ((0, 8), (1, 4))),
        "vectors": draw_vectors(jax.random.fold_in(keys[17], 71), 0),
        "qkv_weight": draw_qkv_weight(jax.random.fold_in(keys[17], 71), 0),
        "dense_weight": draw_dense_weight(jax.random.fold_in(keys[17], 71), 0),
        "up_weight": noise(keys[5], (D, FF), D ** -0.5, 0.125, ((0, 16),), jnp.float32),
        "down_weight": draw_down_weight(jax.random.fold_in(keys[17], 71), 0),
        "vectors_first": noise(keys[7], (9 * D + FF,), (0.05 * (BATCH * LENGTH) ** 0.5), 28.0, ((0, 16),), jnp.float32),
        "qkv_first": noise(keys[8], (D, 3 * D), (0.07 * (BATCH * LENGTH) ** 0.5), 40.0, ((0, 16),), jnp.float32),
        "dense_first": noise(keys[9], (D, D), (0.2 * BATCH ** 0.5), 6.0, ((0, 16),), jnp.float32),
        "up_first": noise(keys[10], (D, FF), (0.05 * (BATCH * LENGTH) ** 0.5), 28.0, ((0, 16),), jnp.float32),
        "down_first": noise(keys[11], (FF, D), (0.05 * (BATCH * LENGTH) ** 0.5), 28.0, ((1, 16),), jnp.float32),
        "vectors_second": jnp.clip(jnp.exp(math.log(983.04) - 1.7917595 * jax.random.uniform(keys[12], (9 * D + FF,), jnp.float32) ** level_of(keys[12], (9 * D + FF,), ((0, 16),), -0.2, 0.2)), 163.84, 983.04),
        "qkv_second": jnp.clip(jnp.exp(math.log(1638.4) - 1.3862944 * jax.random.uniform(keys[13], (D, 3 * D), jnp.float32) ** level_of(keys[13], (D, 3 * D), ((0, 16),), -0.2, 0.2)), 409.6, 1638.4),
        "dense_second": jnp.clip(jnp.exp(math.log(16.0) - 1.609438 * jax.random.uniform(keys[14], (D, D), jnp.float32) ** level_of(keys[14], (D, D), ((0, 16),), -0.2, 0.2)), 3.2, 16.0),
        "up_second": jnp.clip(jnp.exp(math.log(819.2) - 1.609438 * jax.random.uniform(keys[15], (D, FF), jnp.float32) ** level_of(keys[15], (D, FF), ((0, 16),), -0.2, 0.2)), 163.84, 819.2),
        "down_second": jnp.clip(jnp.exp(math.log(655.36) - 1.3862944 * jax.random.uniform(keys[16], (FF, D), jnp.float32) ** level_of(keys[16], (FF, D), ((1, 16),), -0.2, 0.2)), 163.84, 655.36),
    }


@jax.custom_vjp
def low(v):
    return lax.optimization_barrier(v.astype(jnp.bfloat16)).astype(jnp.float32)

@jax.custom_vjp
def low_back(v):
    return v

def low_keep(v):
    return (low(v), None)

def low_pass(kept, grad):
    return (grad,)

def back_keep(v):
    return (v, None)

def back_low(kept, grad):
    return (low(grad),)
low.defvjp(low_keep, low_pass)
low_back.defvjp(back_keep, back_low)
HIGHEST = lax.Precision.HIGHEST
BETA_ONE = 0.9
BETA_TWO = 0.95
LEARN_RATE = 0.5
EPSILON = 1e-08
WEIGHT_DECAY = 0.1
NORM_EPSILON = 1e-05
MASKED = -1e+30

def layer_norm(values, gain_vec, bias_vec):
    average = lax.optimization_barrier(jnp.mean(values, axis=-1, keepdims=True))
    centred = values - average
    spread = lax.optimization_barrier(jnp.mean(centred * centred, axis=-1, keepdims=True))
    return centred * lax.rsqrt(spread + NORM_EPSILON) * gain_vec + bias_vec

def gelu_exact(values):
    return 0.5 * values * (1.0 + lax.erf(values * (1.0 / math.sqrt(2.0))))

def split_vectors(wide_vec):
    return (wide_vec[0:D], wide_vec[D:2 * D], wide_vec[2 * D:5 * D], wide_vec[5 * D:6 * D], wide_vec[6 * D:7 * D], wide_vec[7 * D:8 * D], wide_vec[8 * D:8 * D + FF], wide_vec[8 * D + FF:9 * D + FF])

def rotary_tables(positions):
    half_rot = ROT // 2
    exponent = jnp.arange(half_rot, dtype=jnp.float32) * (2.0 / ROT)
    inverse = jnp.power(10000.0, -exponent)
    angles = positions[:, None] * inverse[None, :]
    angles = jnp.concatenate([angles, angles], axis=1)
    return (jnp.cos(angles), jnp.sin(angles))

def apply_rotary(head_values, cosine, sine_table):
    half_rot = ROT // 2
    rot_part = head_values[..., :ROT]
    turned = jnp.concatenate([-rot_part[..., half_rot:], rot_part[..., :half_rot]], axis=-1)
    mixed_part = rot_part * cosine[:, None, :] + turned * sine_table[:, None, :]
    return jnp.concatenate([mixed_part, head_values[..., ROT:]], axis=-1)

def sequence_layer(tokens, vectors, qkv_weight, dense_weight, up_weight, down_weight):
    ln1_gain, ln1_bias, qkv_bias, dense_bias, ln2_gain, ln2_bias, up_bias, down_bias = split_vectors(vectors)
    normed_one = low(layer_norm(tokens, ln1_gain, ln1_bias))
    projected = low_back(jnp.dot(normed_one, qkv_weight, precision=HIGHEST) + qkv_bias)
    positions = jnp.arange(LENGTH).astype(jnp.float32)
    cosine, sine_table = rotary_tables(positions)
    head_shape = (LENGTH, HEADS, HEAD_DIM)
    queries = low(apply_rotary(projected[:, :D].reshape(head_shape), cosine, sine_table))
    keys_rot = low(apply_rotary(projected[:, D:2 * D].reshape(head_shape), cosine, sine_table))
    values_low = low(projected[:, 2 * D:].reshape(head_shape))
    raw_scores = jnp.einsum('qhd,khd->hqk', queries, keys_rot, precision=HIGHEST) * (1.0 / math.sqrt(HEAD_DIM))
    scores = low_back(raw_scores)
    places = jnp.arange(LENGTH)
    allowed = places[:, None] >= places[None, :]
    masked_scores = jnp.where(allowed[None], scores, MASKED)
    top_score = lax.optimization_barrier(jnp.max(masked_scores, axis=-1, keepdims=True))
    exp_scores = jnp.exp(masked_scores - top_score)
    prob_full = exp_scores / lax.optimization_barrier(jnp.sum(exp_scores, axis=-1, keepdims=True))
    prob_low = low(prob_full)
    attended = jnp.einsum('hqk,khd->qhd', prob_low, values_low, precision=HIGHEST).reshape(LENGTH, D)
    attended = low(low_back(attended))
    dense_out = jnp.dot(attended, dense_weight, precision=HIGHEST) + dense_bias
    normed_two = low(layer_norm(tokens, ln2_gain, ln2_bias))
    pre_act = low_back(jnp.dot(normed_two, up_weight, precision=HIGHEST) + up_bias)
    hidden = low(gelu_exact(pre_act))
    mlp_out = jnp.dot(hidden, down_weight, precision=HIGHEST) + down_bias
    return tokens + dense_out + mlp_out

def adam_step(parameter, gradient, first_moment, second, decay_rate):
    first_new = BETA_ONE * first_moment + (1.0 - BETA_ONE) * gradient
    second_new = BETA_TWO * second + (1.0 - BETA_TWO) * gradient * gradient
    first_hat = first_new / (1.0 - BETA_ONE ** ADAM_STEP)
    second_hat = second_new / (1.0 - BETA_TWO ** ADAM_STEP)
    param_new = parameter - LEARN_RATE * (first_hat / (jnp.sqrt(second_hat) + EPSILON) + decay_rate * parameter)
    return (param_new, first_new, second_new)

def reference(inputs, out_grad, vectors, qkv_weight, dense_weight, up_weight, down_weight, vectors_first, qkv_first, dense_first, up_first, down_first, vectors_second, qkv_second, dense_second, up_second, down_second):

    def whole(tokens, vec_param, qkv_param, dense_param, up_param, down_param):
        rounded = (low(vec_param), low(qkv_param), low(dense_param), low(up_param), low(down_param))

        def one_sequence(seq_tokens):
            return sequence_layer(seq_tokens, rounded[0], rounded[1], rounded[2], rounded[3], rounded[4])
        return lax.map(jax.checkpoint(one_sequence), tokens)
    tokens = inputs.astype(jnp.float32)
    result, pullback = jax.vjp(whole, tokens, vectors, qkv_weight, dense_weight, up_weight, down_weight)
    gradients = pullback(out_grad.astype(jnp.float32))
    vec_new = adam_step(vectors, gradients[1], vectors_first, vectors_second, 0.0)
    qkv_upd = adam_step(qkv_weight, gradients[2], qkv_first, qkv_second, WEIGHT_DECAY)
    dense_upd = adam_step(dense_weight, gradients[3], dense_first, dense_second, WEIGHT_DECAY)
    up_upd = adam_step(up_weight, gradients[4], up_first, up_second, WEIGHT_DECAY)
    down_upd = adam_step(down_weight, gradients[5], down_first, down_second, WEIGHT_DECAY)
    return (result.astype(jnp.bfloat16), gradients[0].astype(jnp.bfloat16), gradients[1], gradients[2], gradients[3], gradients[4], gradients[5], vec_new[0], qkv_upd[0], dense_upd[0], up_upd[0], down_upd[0], vec_new[1], qkv_upd[1], dense_upd[1], up_upd[1], down_upd[1], vec_new[2], qkv_upd[2], dense_upd[2], up_upd[2], down_upd[2])
```

```python
import functools
import math

import jax
import jax.numpy as jnp
from jax import lax
from jax.experimental import pallas as pl
from jax.experimental.pallas import tpu as pltpu
from jax.sharding import PartitionSpec as P

D = 2048
HEADS = 8
HEAD_DIM = 256
FF = 8192
ROT = 64
ADAM_STEP = 4

BETA_ONE = 0.9
BETA_TWO = 0.95
LEARN_RATE = 0.5
EPSILON = 1e-08
WEIGHT_DECAY = 0.1
NORM_EPSILON = 1e-05
MASKED = -1e30
BF = jnp.bfloat16
F32 = jnp.float32
NT = (((1,), (1,)), ((), ()))
TN = (((0,), (0,)), ((), ()))


def rotary_tables(positions):
    half_rot = ROT // 2
    exponent = jnp.arange(half_rot, dtype=F32) * (2.0 / ROT)
    inverse = jnp.power(10000.0, -exponent)
    angles = positions[:, None] * inverse[None, :]
    angles = jnp.concatenate([angles, angles], axis=1)
    return (jnp.cos(angles), jnp.sin(angles))


def adam_step(parameter, gradient, first_moment, second, decay_rate):
    first_new = BETA_ONE * first_moment + (1.0 - BETA_ONE) * gradient
    second_new = BETA_TWO * second + (1.0 - BETA_TWO) * gradient * gradient
    first_hat = first_new / (1.0 - BETA_ONE**ADAM_STEP)
    second_hat = second_new / (1.0 - BETA_TWO**ADAM_STEP)
    param_new = parameter - LEARN_RATE * (
        first_hat / (jnp.sqrt(second_hat) + EPSILON) + decay_rate * parameter
    )
    return (param_new, first_new, second_new)


def swap(value, axis, size, bit):
    return lax.ppermute(value, axis, [(i, i ^ bit) for i in range(size)])


def take(value, index, axis):
    return lax.dynamic_index_in_dim(value, index, axis, keepdims=False)


def pair(mine, other, my_bit, axis):
    low = jnp.where(my_bit == 0, mine, other)
    high = jnp.where(my_bit == 0, other, mine)
    return jnp.stack([low, high], axis=axis)


def bits_of(size):
    return [1 << k for k in reversed(range(size.bit_length() - 1))]


def exchange(value, axis, size):
    place = lax.axis_index(axis)
    rest = value.shape[1:]
    for bit in bits_of(size):
        outer = size // (2 * bit)
        split = value.reshape((outer, 2, bit) + rest)
        my_bit = (place // bit) % 2
        mine = take(split, my_bit, 1)
        theirs = take(split, 1 - my_bit, 1)
        got = swap(theirs, axis, size, bit)
        value = pair(mine, got, my_bit, 1).reshape((size,) + rest)
    return value


def line_gather(block, size):
    place = lax.axis_index("zero")
    whole = jnp.zeros((size,) + block.shape, block.dtype)
    whole = lax.dynamic_update_index_in_dim(whole, block, place, 0)
    above, below = block, block
    ups, downs = {}, {}
    for step in range(1, size):
        above = lax.ppermute(above, "zero", [(i, i + 1) for i in range(step - 1, size - 1)])
        below = lax.ppermute(below, "zero", [(i, i - 1) for i in range(1, size - step + 1)])
        ups[step], downs[size - step] = above, below
    for step in range(1, size):
        got = jnp.where(place >= step, ups[step], downs[step])
        whole = lax.dynamic_update_index_in_dim(whole, got, lax.rem(place - step + size, size), 0)
    return whole


def line_scatter(parts, size):
    place = lax.axis_index("zero")
    up_sum, down_sum = None, None
    for step in range(1, size):
        up_at = jnp.clip(size + place - step, 0, size - 1)
        down_at = jnp.clip(place + step - size, 0, size - 1)
        up_own = take(parts, up_at, 0)
        down_own = take(parts, down_at, 0)
        if up_sum is None:
            up_send, down_send = up_own, down_own
        else:
            up_send = (up_own.astype(F32) + up_sum.astype(F32)).astype(BF)
            down_send = (down_own.astype(F32) + down_sum.astype(F32)).astype(BF)
        up_sum = lax.ppermute(up_send, "zero", [(i, i + 1) for i in range(0, step)])
        down_sum = lax.ppermute(down_send, "zero", [(i, i - 1) for i in range(size - step, size)])
    own = take(parts, place, 0)
    return (own.astype(F32) + up_sum.astype(F32) + down_sum.astype(F32)).astype(BF)


def attention_body(scale, projected, cos_ref, sin_ref, d_att_ref, att_ref, d_proj_ref, keys_acc, values_acc):
    length = projected.shape[1]
    tile = min(256, length)
    half = ROT // 2
    cosine = cos_ref[...]
    sine = sin_ref[...]

    def turn(block):
        first = block[:, :128]
        rolled = jnp.concatenate([first[:, half:ROT], first[:, :half], first[:, ROT:]], axis=1)
        return jnp.concatenate([first * cosine + rolled * sine, block[:, 128:]], axis=1)

    def turn_back(block):
        first = block[:, :128]
        scaled = first * sine
        rolled = jnp.concatenate([scaled[:, half:ROT], scaled[:, :half], scaled[:, ROT:]], axis=1)
        return jnp.concatenate([first * cosine + rolled, block[:, 128:]], axis=1)

    queries = turn(projected[0, :, 0:HEAD_DIM]).astype(BF)
    keys = turn(projected[0, :, HEAD_DIM : 2 * HEAD_DIM]).astype(BF)
    values = projected[0, :, 2 * HEAD_DIM :].astype(BF)
    d_att_all = d_att_ref[0]
    keys_acc[...] = jnp.zeros_like(keys_acc)
    values_acc[...] = jnp.zeros_like(values_acc)
    d_queries = []
    for at in range(length // tile):
        rows = slice(at * tile, (at + 1) * tile)
        seen = (at + 1) * tile
        q = queries[rows]
        d_att = d_att_all[rows]
        k, v = keys[:seen], values[:seen]
        scores = lax.dot_general(q, k, NT, preferred_element_type=F32) * scale
        row = lax.broadcasted_iota(jnp.int32, scores.shape, 0) + at * tile
        column = lax.broadcasted_iota(jnp.int32, scores.shape, 1)
        scores = jnp.where(row >= column, scores, MASKED)
        top = jnp.max(scores, axis=1, keepdims=True)
        grown = jnp.exp(scores - top)
        prob = grown * (1.0 / jnp.sum(grown, axis=1, keepdims=True))
        prob_low = prob.astype(BF)
        att_ref[0, rows, :] = jnp.dot(prob_low, v, preferred_element_type=F32).astype(BF)
        d_prob = lax.dot_general(d_att, v, NT, preferred_element_type=F32)
        inner = jnp.sum(d_prob * prob, axis=1, keepdims=True)
        d_scores = (prob * (d_prob - inner)).astype(BF)
        d_queries.append(jnp.dot(d_scores, k, preferred_element_type=F32) * scale)
        keys_acc[:seen, :] += lax.dot_general(d_scores, q, TN, preferred_element_type=F32)
        values_acc[:seen, :] += lax.dot_general(prob_low, d_att, TN, preferred_element_type=F32)
    d_proj_ref[0, :, 0:HEAD_DIM] = turn_back(jnp.concatenate(d_queries, axis=0)).astype(BF)
    d_proj_ref[0, :, HEAD_DIM : 2 * HEAD_DIM] = turn_back(keys_acc[...] * scale).astype(BF)
    d_proj_ref[0, :, 2 * HEAD_DIM :] = values_acc[...].astype(BF)


def attention(projected, d_att):
    seqs, length, _ = projected.shape
    cosine, sine = rotary_tables(jnp.arange(length).astype(F32))
    half = ROT // 2
    sine_turn = jnp.concatenate([-sine[:, :half], sine[:, half:]], axis=1)
    cosine = jnp.concatenate([cosine, jnp.ones((length, 128 - ROT), F32)], axis=1)
    sine_turn = jnp.concatenate([sine_turn, jnp.zeros((length, 128 - ROT), F32)], axis=1)
    whole = pl.BlockSpec((length, 128), lambda s: (0, 0))
    one = lambda width: pl.BlockSpec((1, length, width), lambda s: (s, 0, 0))
    return pl.pallas_call(
        functools.partial(attention_body, 1.0 / math.sqrt(HEAD_DIM)),
        grid=(seqs,),
        in_specs=[one(3 * HEAD_DIM), whole, whole, one(HEAD_DIM)],
        out_specs=[one(HEAD_DIM), one(3 * HEAD_DIM)],
        out_shape=[
            jax.ShapeDtypeStruct((seqs, length, HEAD_DIM), BF),
            jax.ShapeDtypeStruct((seqs, length, 3 * HEAD_DIM), BF),
        ],
        scratch_shapes=[pltpu.VMEM((length, HEAD_DIM), F32), pltpu.VMEM((length, HEAD_DIM), F32)],
        compiler_params=pltpu.CompilerParams(vmem_limit_bytes=48 * 1024 * 1024),
        cost_estimate=pl.CostEstimate(
            flops=seqs * length * length * HEAD_DIM * 9,
            bytes_accessed=seqs * length * HEAD_DIM * 22,
            transcendentals=seqs * length * length,
        ),
        name="attention",
    )(projected, cosine, sine_turn, d_att)


def gelu_parts(values):
    phi_wide = 0.5 * (1.0 + lax.erf(values * (1.0 / math.sqrt(2.0))))
    density = jnp.exp(-0.5 * values * values) * (1.0 / math.sqrt(2.0 * math.pi))
    return values * phi_wide, phi_wide + values * density


def make_body(sizes):
    n_dp, n_zero, n_seq = sizes["dp"], sizes["zero"], sizes["seq"]
    parts = n_dp * n_seq
    head_w = D // parts
    hid_w = FF // parts
    plane = ("dp", "seq")
    dp_bits = [("dp", n_dp, bit) for bit in bits_of(n_dp)]
    seq_bits = [("seq", n_seq, bit) for bit in bits_of(n_seq)]
    far_bits, core_bits = seq_bits[:-1], seq_bits[-1:]

    def plane_gather(value, steps):
        shape = value.shape
        for axis, size, bit in steps:
            got = swap(value, axis, size, bit)
            value = pair(value, got, (lax.axis_index(axis) // bit) % 2, 0)
        order = [parts_index for parts_index in reversed(steps)]
        value = value.reshape((2,) * len(steps) + shape)
        wanted = dp_bits + seq_bits
        perm = [order.index(step) for step in wanted]
        value = jnp.transpose(value, perm + [len(steps) + k for k in range(len(shape))])
        return value.reshape((n_dp, n_seq) + shape)

    def plane_exchange(value):
        rest = value.shape[1:]
        value = value.reshape((n_dp, n_seq) + rest)
        value = jnp.swapaxes(value, 0, 1)
        value = exchange(value, "seq", n_seq)
        value = jnp.swapaxes(value, 0, 1)
        value = exchange(value, "dp", n_dp)
        return value.reshape((parts,) + rest)

    def body(
        inputs,
        out_grad,
        vectors,
        qkv_weight,
        dense_weight,
        up_weight,
        down_weight,
        vectors_first,
        qkv_first,
        dense_first,
        up_first,
        down_first,
        vectors_second,
        qkv_second,
        dense_second,
        up_second,
        down_second,
    ):
        dp_i, zero_i, seq_i = lax.axis_index("dp"), lax.axis_index("zero"), lax.axis_index("seq")
        part_i = dp_i * n_seq + seq_i
        seqs_here, local_len = inputs.shape[0], inputs.shape[1]
        token_rows = seqs_here * local_len
        rows_d = qkv_weight.shape[0]
        block_d = rows_d * n_seq

        vec_all = lax.all_gather(vectors.astype(BF), ("zero", "seq"), axis=0, tiled=True).astype(F32)
        ln1_gain, ln1_bias = vec_all[:D], vec_all[D : 2 * D]
        qkv_bias = vec_all[2 * D : 5 * D].reshape(3, parts, head_w)
        dense_bias = vec_all[5 * D : 6 * D]
        ln2_gain, ln2_bias = vec_all[6 * D : 7 * D], vec_all[7 * D : 8 * D]
        up_bias = vec_all[8 * D : 8 * D + FF].reshape(parts, hid_w)
        down_bias = vec_all[8 * D + FF :]

        half = lambda value, axis: take(
            value.reshape(value.shape[:axis] + (n_dp, n_seq, -1) + value.shape[axis + 1 :]), dp_i, axis
        )
        qkv_low = qkv_weight.astype(BF).reshape(rows_d, 3, n_dp, n_seq, head_w)
        qkv_low = take(qkv_low, dp_i, 2).transpose(2, 0, 1, 3).reshape(n_seq, rows_d, 3 * head_w)
        dense_low = half(dense_weight.astype(BF), 1).transpose(1, 0, 2)
        up_low = half(up_weight.astype(BF), 1).transpose(1, 0, 2)
        down_low = half(down_weight.astype(BF), 0)

        attn_block = exchange(jnp.concatenate([dense_low, qkv_low], axis=2), "seq", n_seq)
        attn_block = attn_block.reshape(block_d, 4 * head_w)
        dense_cols = line_gather(attn_block[:, :head_w], n_zero).reshape(D, head_w)
        qkv_own = line_gather(attn_block[:, head_w:], n_zero).reshape(D, 3 * head_w)
        dense_own = plane_exchange(dense_cols.reshape(parts, head_w, head_w))
        dense_own = dense_own.transpose(1, 0, 2).reshape(head_w, D)
        up_block = exchange(up_low, "seq", n_seq).reshape(block_d, hid_w)
        up_own = line_gather(up_block, n_zero).reshape(D, hid_w)
        down_block = exchange(down_low, "seq", n_seq).transpose(1, 0, 2).reshape(hid_w, block_d)
        down_own = line_gather(down_block, n_zero).transpose(1, 0, 2).reshape(hid_w, D)

        tokens_low = inputs.reshape(token_rows, D)
        grad_low = out_grad.reshape(token_rows, D)
        tokens_all = plane_gather(tokens_low, far_bits + dp_bits + core_bits)
        grad_all = plane_gather(grad_low, dp_bits + far_bits + core_bits)
        order = lambda value: value.reshape(n_dp, n_seq, seqs_here, local_len, D).transpose(
            0, 2, 1, 3, 4
        ).reshape(n_dp * seqs_here * n_seq * local_len, D)
        unorder = lambda value: value.reshape(n_dp, seqs_here, n_seq, local_len, D).transpose(
            0, 2, 1, 3, 4
        ).reshape(n_dp, n_seq, token_rows, D)
        tokens = order(tokens_all)
        grads = order(grad_all)
        seqs = n_dp * seqs_here
        length = n_seq * local_len

        def statistics(values):
            average = jnp.mean(values, axis=-1, keepdims=True)
            centred = values - average
            spread = jnp.mean(centred * centred, axis=-1, keepdims=True)
            return centred, lax.rsqrt(spread + NORM_EPSILON)

        centred, rate = statistics(tokens.astype(F32))
        xhat = centred * rate
        normed_one = (xhat * ln1_gain + ln1_bias).astype(BF)
        normed_two = (xhat * ln2_gain + ln2_bias).astype(BF)

        projected = jnp.dot(normed_one, qkv_own, preferred_element_type=F32)
        projected = projected + take(qkv_bias, part_i, 1).reshape(3 * head_w)
        d_att = lax.dot_general(grads, dense_own, NT, preferred_element_type=F32).astype(BF)
        attended, d_proj = attention(
            projected.reshape(seqs, length, 3 * head_w), d_att.reshape(seqs, length, head_w)
        )
        attended = attended.reshape(seqs * length, head_w)
        d_proj = d_proj.reshape(seqs * length, 3 * head_w)
        d_qkv_bias = jnp.sum(d_proj.astype(F32), axis=0)
        d_normed_one = lax.dot_general(d_proj, qkv_own, NT, preferred_element_type=F32)
        qkv_part = lax.dot_general(normed_one, d_proj, TN, preferred_element_type=F32).astype(BF)
        dense_part = lax.dot_general(attended, grads, TN, preferred_element_type=F32).astype(BF)
        dense_part = plane_exchange(dense_part.reshape(head_w, parts, head_w).transpose(1, 0, 2))
        dense_part = dense_part.reshape(D, head_w)
        attn_parts = jnp.concatenate([dense_part, qkv_part], axis=1).reshape(n_zero, block_d, 4 * head_w)
        attn_sum = line_scatter(attn_parts, n_zero)

        pre_act = jnp.dot(normed_two, up_own, preferred_element_type=F32) + take(up_bias, part_i, 0)
        hidden_wide, slope = gelu_parts(pre_act)
        hidden = hidden_wide.astype(BF)
        down_part = lax.dot_general(hidden, grads, TN, preferred_element_type=F32).astype(BF)
        down_parts = down_part.reshape(hid_w, n_zero, block_d).transpose(1, 0, 2)
        down_sum = line_scatter(down_parts, n_zero)
        d_hidden = lax.dot_general(grads, down_own, NT, preferred_element_type=F32)
        d_pre_wide = (d_hidden * slope).astype(BF)
        d_pre = d_pre_wide
        d_up_bias = jnp.sum(d_pre.astype(F32), axis=0)
        up_part = lax.dot_general(normed_two, d_pre, TN, preferred_element_type=F32).astype(BF)
        up_sum = line_scatter(up_part.reshape(n_zero, block_d, hid_w), n_zero)
        d_normed_two = lax.dot_general(d_pre, up_own, NT, preferred_element_type=F32)

        out_part = jnp.dot(attended, dense_own, preferred_element_type=F32) + jnp.dot(
            hidden, down_own, preferred_element_type=F32
        )
        out_sum = lax.psum_scatter(
            unorder(out_part.astype(BF)).reshape(parts, token_rows, D), plane, scatter_dimension=0
        )
        tokens_wide = tokens_low.astype(F32)
        grad_wide = grad_low.astype(F32)
        outputs = (tokens_wide + out_sum.astype(F32) + dense_bias + down_bias).astype(BF)
        outputs = outputs.reshape(inputs.shape)

        d_gain_one = jnp.sum(d_normed_one * xhat, axis=0)
        d_bias_one = jnp.sum(d_normed_one, axis=0)
        d_gain_two = jnp.sum(d_normed_two * xhat, axis=0)
        d_bias_two = jnp.sum(d_normed_two, axis=0)
        d_xhat = (d_normed_one * ln1_gain + d_normed_two * ln2_gain).astype(BF)
        d_xhat = lax.psum_scatter(
            unorder(d_xhat).reshape(parts, token_rows, D), plane, scatter_dimension=0
        ).astype(F32)
        centred_own, rate_own = statistics(tokens_wide)
        xhat_own = centred_own * rate_own
        d_tokens = rate_own * (
            d_xhat
            - jnp.mean(d_xhat, axis=-1, keepdims=True)
            - xhat_own * jnp.mean(d_xhat * xhat_own, axis=-1, keepdims=True)
        )
        input_grad = (grad_wide + d_tokens).astype(BF).reshape(inputs.shape)

        d_out_bias = jnp.sum(grad_wide, axis=0)
        place_in = lambda value, count: lax.dynamic_update_index_in_dim(
            jnp.zeros((value.shape[0], count, value.shape[1]), F32), value, part_i, 1
        ).reshape(-1)
        vector_local = jnp.concatenate(
            [
                d_gain_one,
                d_bias_one,
                place_in(d_qkv_bias.reshape(3, head_w), parts),
                d_out_bias,
                d_gain_two,
                d_bias_two,
                place_in(d_up_bias.reshape(1, hid_w), parts),
                d_out_bias,
            ]
        )
        vector_sum = lax.psum(vector_local, ("dp", "zero", "seq"))
        vectors_grad = lax.dynamic_slice_in_dim(
            vector_sum, (zero_i * n_seq + seq_i) * vectors.shape[0], vectors.shape[0], 0
        )

        def home(value):
            value = exchange(value, "seq", n_seq)
            return exchange_all(value)

        def exchange_all(value):
            for step in dp_bits:
                got = swap(value, *step)
                value = pair(value, got, (dp_i // step[2]) % 2, 0)
            return value.reshape((n_dp, n_seq) + value.shape[-2:])

        attn_home = home(attn_sum.reshape(n_seq, rows_d, 4 * head_w))
        dense_grad = attn_home[..., :head_w].transpose(2, 0, 1, 3).reshape(rows_d, D).astype(F32)
        qkv_grad = attn_home[..., head_w:].reshape(n_dp, n_seq, rows_d, 3, head_w)
        qkv_grad = qkv_grad.transpose(2, 3, 0, 1, 4).reshape(rows_d, 3 * D).astype(F32)
        down_home = home(down_sum.reshape(hid_w, n_seq, rows_d).transpose(1, 0, 2))
        down_grad = down_home.reshape(FF, rows_d).astype(F32)
        up_home = home(up_sum.reshape(n_seq, rows_d, hid_w))
        up_grad = up_home.transpose(2, 0, 1, 3).reshape(rows_d, FF).astype(F32)

        vec_upd = adam_step(vectors, vectors_grad, vectors_first, vectors_second, 0.0)
        qkv_upd = adam_step(qkv_weight, qkv_grad, qkv_first, qkv_second, WEIGHT_DECAY)
        dense_upd = adam_step(dense_weight, dense_grad, dense_first, dense_second, WEIGHT_DECAY)
        up_upd = adam_step(up_weight, up_grad, up_first, up_second, WEIGHT_DECAY)
        down_upd = adam_step(down_weight, down_grad, down_first, down_second, WEIGHT_DECAY)
        updates = (vec_upd, qkv_upd, dense_upd, up_upd, down_upd)
        return (
            (outputs, input_grad, vectors_grad, qkv_grad, dense_grad, up_grad, down_grad)
            + tuple(update[0] for update in updates)
            + tuple(update[1] for update in updates)
            + tuple(update[2] for update in updates)
        )

    return body


def solution(mesh):
    wide = P(("dp", "zero"), "seq", None)
    vector = P(("zero", "seq"))
    rows = P(("zero", "seq"), None)
    columns = P(None, ("zero", "seq"))
    state = (vector, rows, rows, rows, columns)
    return jax.shard_map(
        make_body(dict(mesh.shape)),
        mesh=mesh,
        in_specs=(wide, wide) + state * 3,
        out_specs=(wide, wide) + state * 4,
        check_vma=False,
    )
```

```python
import functools
import math

import jax
import jax.numpy as jnp
from jax import lax
from jax.experimental import pallas as pl
from jax.experimental.pallas import tpu as pltpu
from jax.sharding import PartitionSpec as P

D = 2048
HEADS = 8
HEAD_DIM = 256
FF = 8192
ROT = 64
ADAM_STEP = 4

BETA_ONE = 0.9
BETA_TWO = 0.95
LEARN_RATE = 0.5
EPSILON = 1e-08
WEIGHT_DECAY = 0.1
NORM_EPSILON = 1e-05
MASKED = -1e30
N_DP = 2
N_SEQ = 4
PARTS = N_DP * N_SEQ
HEAD_W = D // PARTS
HID_W = FF // PARTS
BF = jnp.bfloat16
F32 = jnp.float32
NT = (((1,), (1,)), ((), ()))
TN = (((0,), (0,)), ((), ()))


def rotary_tables(positions):
    half_rot = ROT // 2
    exponent = jnp.arange(half_rot, dtype=F32) * (2.0 / ROT)
    inverse = jnp.power(10000.0, -exponent)
    angles = positions[:, None] * inverse[None, :]
    angles = jnp.concatenate([angles, angles], axis=1)
    return (jnp.cos(angles), jnp.sin(angles))


def adam_step(parameter, gradient, first_moment, second, decay_rate):
    first_new = BETA_ONE * first_moment + (1.0 - BETA_ONE) * gradient
    second_new = BETA_TWO * second + (1.0 - BETA_TWO) * gradient * gradient
    first_hat = first_new / (1.0 - BETA_ONE**ADAM_STEP)
    second_hat = second_new / (1.0 - BETA_TWO**ADAM_STEP)
    param_new = parameter - LEARN_RATE * (
        first_hat / (jnp.sqrt(second_hat) + EPSILON) + decay_rate * parameter
    )
    return (param_new, first_new, second_new)


class Wire:
    def __init__(self, send_sems, recv_sems):
        self.send_sems, self.recv_sems, self.used = send_sems, recv_sems, 0
        self.sent = []

    def slot(self):
        self.used += 1
        return self.used - 1

    def copy(self, slot, source, target, device):
        return pltpu.make_async_remote_copy(
            src_ref=source,
            dst_ref=target,
            send_sem=self.send_sems.at[slot],
            recv_sem=self.recv_sems.at[slot],
            device_id=device,
            device_id_type=pl.DeviceIdType.MESH,
        )

    def send(self, slot, source, target, device, when=None):
        copy = self.copy(slot, source, target, device)
        guarded(when, copy.start)
        self.sent.append((copy, when))

    def receive(self, slot, target, device, when=None):
        copy = self.copy(slot, target, target, device)
        guarded(when, copy.wait_recv)

    def finish(self):
        for copy, when in self.sent:
            guarded(when, copy.wait_send)
        self.sent = []


def guarded(when, action):
    if when is None:
        action()
    else:
        pl.when(when)(action)


class Place:
    def __init__(self, n_zero):
        self.n = n_zero
        self.dp, self.z, self.s = (lax.axis_index(a) for a in ("dp", "zero", "seq"))
        flip = lambda value, bit: jnp.bitwise_xor(value, bit)
        self.dp_far, self.s_far, self.s_core = 1 - self.dp, flip(self.s, 2), flip(self.s, 1)
        self.s_both = flip(self.s, 3)
        self.across = {"dp": self.dp_far}
        self.far = {"seq": self.s_far}
        self.core = {"seq": self.s_core}
        self.above, self.below = {"zero": self.z + 1}, {"zero": self.z - 1}
        self.part = self.dp * N_SEQ + self.s

    def others(self):
        for step in range(1, N_DP * N_SEQ):
            at = lax.rem(self.part + step, N_DP * N_SEQ)
            dp, s = lax.div(at, N_SEQ), lax.rem(at, N_SEQ)
            yield step, dp, s, {"dp": dp, "seq": s}

    def barrier(self):
        gate = pltpu.get_barrier_semaphore()
        signal = lambda device: pl.semaphore_signal(
            gate, inc=1, device_id=device, device_id_type=pl.DeviceIdType.MESH
        )
        for _, _, _, device in self.others():
            signal(device)
        pl.when(self.z < self.n - 1)(lambda: signal(self.above))
        pl.when(self.z > 0)(lambda: signal(self.below))
        ends = (self.z < self.n - 1).astype(jnp.int32) + (self.z > 0).astype(jnp.int32)
        pl.semaphore_wait(gate, N_DP * N_SEQ - 1 + ends)


class LineGather:
    def __init__(self, wire, place, whole, rows):
        self.wire, self.place, self.whole, self.rows = wire, place, whole, rows
        self.ups = [wire.slot() for _ in range(place.n - 1)]
        self.downs = [wire.slot() for _ in range(place.n - 1)]

    def block(self, index):
        return self.whole.at[pl.ds(pl.multiple_of(index * self.rows, self.rows), self.rows)]

    def take(self, step):
        p = self.place
        self.wire.receive(self.ups[step - 1], self.block(jnp.maximum(p.z - step, 0)), p.below, p.z >= step)
        self.wire.receive(
            self.downs[step - 1], self.block(jnp.minimum(p.z + step, p.n - 1)), p.above, p.z + step < p.n
        )

    def pass_on(self, step):
        p = self.place
        up, down = jnp.maximum(p.z - step + 1, 0), jnp.minimum(p.z + step - 1, p.n - 1)
        self.wire.send(
            self.ups[step - 1], self.block(up), self.block(up), p.above, (p.z < p.n - 1) & (p.z >= step - 1)
        )
        self.wire.send(
            self.downs[step - 1], self.block(down), self.block(down), p.below, (p.z > 0) & (p.z + step <= p.n)
        )


class SeqExchange:
    def __init__(self, wire, place, send, whole, rows):
        self.wire, self.place, self.out, self.whole, self.rows = wire, place, send, whole, rows
        self.slots = [wire.slot() for _ in range(1, N_SEQ)]

    def target(self, s):
        row = (self.place.z * N_SEQ + s) * self.rows
        return self.whole.at[pl.ds(pl.multiple_of(row, self.rows), self.rows)]

    def start(self, local_sem):
        p = self.place
        for step in range(1, N_SEQ):
            to = lax.rem(p.s + step, N_SEQ)
            self.wire.send(self.slots[step - 1], self.out.at[to], self.target(p.s), {"seq": to})
        own = pltpu.make_async_copy(self.out.at[p.s], self.target(p.s), local_sem)
        own.start()
        self.own = own

    def wait(self):
        p = self.place
        for step in range(1, N_SEQ):
            source = lax.rem(p.s - step + N_SEQ, N_SEQ)
            self.wire.receive(self.slots[step - 1], self.target(source), {"seq": source})
        self.own.wait()


class PlaneGather:
    def __init__(self, wire, place, block, whole):
        self.wire, self.place, self.own, self.whole = wire, place, block, whole
        self.slots = {name: wire.slot() for name in ("far", "across", "both0", "both1", "c0", "c1", "c2", "c3")}
        self.half = block.shape[0] // 2

    def start(self, local_sem):
        p, w, slots = self.place, self.wire, self.slots
        mine = self.whole.at[p.dp, p.s]
        w.send(slots["far"], self.own, mine, p.far)
        w.send(slots["across"], self.own, mine, p.across)
        w.send(slots["c0"], self.own, mine, p.core)
        self.copied = pltpu.make_async_copy(self.own, mine, local_sem)
        self.copied.start()

    def turn(self):
        p, w, slots, h = self.place, self.wire, self.slots, self.half
        far, across = self.whole.at[p.dp, p.s_far], self.whole.at[p.dp_far, p.s]
        w.receive(slots["far"], far, p.far)
        w.send(slots["both0"], far.at[pl.ds(0, h)], far.at[pl.ds(0, h)], p.across)
        w.send(slots["c1"], far, far, p.core)
        w.receive(slots["across"], across, p.across)
        w.send(slots["both1"], across.at[pl.ds(h, h)], across.at[pl.ds(h, h)], p.far)
        w.send(slots["c2"], across, across, p.core)

    def turn_again(self):
        p, w, slots, h = self.place, self.wire, self.slots, self.half
        both = self.whole.at[p.dp_far, p.s_far]
        w.receive(slots["both0"], both.at[pl.ds(0, h)], p.across)
        w.receive(slots["both1"], both.at[pl.ds(h, h)], p.far)
        w.send(slots["c3"], both, both, p.core)

    def wait(self):
        p, w, slots = self.place, self.wire, self.slots
        w.receive(slots["c0"], self.whole.at[p.dp, p.s_core], p.core)
        w.receive(slots["c1"], self.whole.at[p.dp, p.s_both], p.core)
        w.receive(slots["c2"], self.whole.at[p.dp_far, p.s_core], p.core)
        w.receive(slots["c3"], self.whole.at[p.dp_far, p.s_both], p.core)
        self.copied.wait()


def add_rows(target, *sources):
    rows = target.shape[0]
    tile = 32 if rows % 32 == 0 else 16

    def one(i, carry):
        at = pl.ds(pl.multiple_of(i * tile, tile), tile)
        total = sources[0][at, :].astype(F32)
        for source in sources[1:]:
            total = total + source[at, :].astype(F32)
        target[at, :] = total.astype(target.dtype)
        return carry

    lax.fori_loop(0, rows // tile, one, 0)


class LineScatter:
    def __init__(self, wire, place, parts, ups, downs, total, own, rows, sem):
        self.wire, self.place, self.parts, self.rows = wire, place, parts, rows
        self.ups, self.downs, self.total, self.own, self.sem = ups, downs, total, own, sem
        self.up_slots = [wire.slot() for _ in range(place.n)]
        self.down_slots = [wire.slot() for _ in range(place.n)]

    def part(self, j):
        return self.parts.at[pl.ds(pl.multiple_of(j * self.rows, self.rows), self.rows)]

    def fetch(self, j, target):
        copy = pltpu.make_async_copy(self.part(j), target, self.sem)
        copy.start()
        copy.wait()

    def step(self, k):
        p = self.place
        j = p.n - 1 - k
        self.hop(j, self.ups, self.up_slots[j], p.above, p.below, p.z < j, p.z == 0)
        j = k
        self.hop(j, self.downs, self.down_slots[j], p.below, p.above, p.z > j, p.z == p.n - 1)

    def hop(self, j, held, slot, onto, source, active, first):
        def go():
            pl.when(first)(lambda: self.fetch(j, held.at[j]))

            @pl.when(jnp.logical_not(first))
            def _():
                self.fetch(j, self.own)
                self.wire.receive(slot, held.at[j], source)
                add_rows(held.at[j], held.at[j], self.own)

        pl.when(active)(go)
        self.wire.send(slot, held.at[j], held.at[j], onto, active)

    def last(self):
        p = self.place
        self.fetch(p.z, self.own)
        up, down = self.ups.at[p.z], self.downs.at[p.z]

        @pl.when(p.z == 0)
        def _():
            self.arrive(self.downs, self.down_slots, p.above)
            add_rows(self.total, self.own, down)

        @pl.when(p.z == p.n - 1)
        def _():
            self.arrive(self.ups, self.up_slots, p.below)
            add_rows(self.total, self.own, up)

        @pl.when((p.z > 0) & (p.z < p.n - 1))
        def _():
            self.arrive(self.ups, self.up_slots, p.below)
            self.arrive(self.downs, self.down_slots, p.above)
            add_rows(self.total, self.own, up, down)

    def arrive(self, held, slots, source):
        self.wire.receive(slots[0] + self.place.z, held.at[self.place.z], source)


class Home:
    def __init__(self, wire, place, total, home, rows):
        self.wire, self.place, self.total, self.home, self.rows = wire, place, total, home, rows
        self.slots = [wire.slot() for _ in range(1, N_DP * N_SEQ)]

    def start(self, local_sem):
        p = self.place
        piece = lambda s: self.total.at[pl.ds(pl.multiple_of(s * self.rows, self.rows), self.rows)]
        for step, dp, s, device in p.others():
            self.wire.send(self.slots[step - 1], piece(s), self.home.at[p.dp, p.s], device)
        self.copied = pltpu.make_async_copy(piece(p.s), self.home.at[p.dp, p.s], local_sem)
        self.copied.start()

    def wait(self):
        p = self.place
        parts = N_DP * N_SEQ
        for step in range(1, parts):
            at = lax.rem(p.part - step + parts, parts)
            dp, s = lax.div(at, N_SEQ), lax.rem(at, N_SEQ)
            self.wire.receive(self.slots[step - 1], self.home.at[dp, s], {"dp": dp, "seq": s})
        self.copied.wait()


class DenseExchange:
    def __init__(self, wire, place, source, target):
        self.wire, self.place, self.source, self.target = wire, place, source, target
        self.slots = [wire.slot() for _ in range(1, N_DP * N_SEQ)]

    def start(self, local_sem):
        p = self.place
        for step, dp, s, device in p.others():
            self.wire.send(self.slots[step - 1], self.source(dp * N_SEQ + s), self.target(p.part), device)
        self.copied = pltpu.make_async_copy(self.source(p.part), self.target(p.part), local_sem)
        self.copied.start()

    def wait(self):
        p = self.place
        parts = N_DP * N_SEQ
        for step in range(1, parts):
            at = lax.rem(p.part - step + parts, parts)
            device = {"dp": lax.div(at, N_SEQ), "seq": lax.rem(at, N_SEQ)}
            self.wire.receive(self.slots[step - 1], self.target(at), device)
        self.copied.wait()


class PlaneScatter:
    def __init__(self, wire, place, parts, mate, from_far, from_across, turned, total, own, sem):
        self.wire, self.place, self.parts, self.mate, self.sums = wire, place, parts, mate, mate
        self.from_far, self.from_across, self.turned = from_far, from_across, turned
        self.total, self.own, self.sem = total, own, sem
        self.half = total.shape[0] // 2
        self.core_slots = [[wire.slot() for _ in range(2)] for _ in range(2)]
        names = ("turn_across", "turn_far", "far0", "far1", "across0", "across1")
        self.slots = {name: wire.slot() for name in names}

    def start(self):
        p = self.place
        core = lax.rem(p.s_core, 2)
        for dp in range(2):
            for y in range(2):
                self.wire.send(
                    self.core_slots[dp][y], self.parts.at[dp, 2 * y + core], self.mate.at[dp, y], p.core
                )

    def combine(self, dp, y):
        p = self.place
        core = lax.rem(p.s, 2)
        for d in range(2):
            for v in range(2):

                @pl.when((dp == d) & (y == v))
                def _(d=d, v=v):
                    copy = pltpu.make_async_copy(self.parts.at[d, 2 * v + core], self.own, self.sem)
                    copy.start()
                    self.wire.receive(self.core_slots[d][v], self.mate.at[d, v], p.core)
                    copy.wait()
                    add_rows(self.sums.at[d, v], self.own, self.mate.at[d, v])

    def turn(self):
        p, w, h, slots = self.place, self.wire, self.half, self.slots
        y = lax.div(p.s, 2)
        y_far = 1 - y
        low, high = pl.ds(0, h), pl.ds(h, h)
        self.combine(p.dp_far, y_far)
        both = self.sums.at[p.dp_far, y_far]
        w.send(slots["turn_across"], both.at[low], self.turned.at[low], p.across)
        w.send(slots["turn_far"], both.at[high], self.turned.at[high], p.far)
        self.combine(p.dp, y_far)
        far = self.sums.at[p.dp, y_far]
        w.send(slots["far1"], far.at[high], self.from_far.at[high], p.far)
        self.combine(p.dp_far, y)
        across = self.sums.at[p.dp_far, y]
        w.send(slots["across0"], across.at[low], self.from_across.at[low], p.across)
        self.combine(p.dp, y)

    def turn_again(self):
        p, w, h, slots = self.place, self.wire, self.half, self.slots
        y = lax.div(p.s, 2)
        low, high = pl.ds(0, h), pl.ds(h, h)
        far, across = self.sums.at[p.dp, 1 - y], self.sums.at[p.dp_far, y]
        w.receive(slots["turn_across"], self.turned.at[low], p.across)
        add_rows(far.at[low], far.at[low], self.turned.at[low])
        w.send(slots["far0"], far.at[low], self.from_far.at[low], p.far)
        w.receive(slots["turn_far"], self.turned.at[high], p.far)
        add_rows(across.at[high], across.at[high], self.turned.at[high])
        w.send(slots["across1"], across.at[high], self.from_across.at[high], p.across)

    def last(self):
        p, w, h, slots = self.place, self.wire, self.half, self.slots
        low, high = pl.ds(0, h), pl.ds(h, h)
        w.receive(slots["far1"], self.from_far.at[high], p.far)
        w.receive(slots["far0"], self.from_far.at[low], p.far)
        w.receive(slots["across0"], self.from_across.at[low], p.across)
        w.receive(slots["across1"], self.from_across.at[high], p.across)
        add_rows(self.total, self.sums.at[p.dp, lax.div(p.s, 2)], self.from_far, self.from_across)


def attention_body(scale, projected, cos_ref, sin_ref, d_att_ref, att_ref, d_proj_ref, keys_acc, values_acc):
    length = projected.shape[1]
    tile = min(256, length)
    half = ROT // 2
    cosine = cos_ref[...]
    sine = sin_ref[...]

    def turn(block):
        first = block[:, :128]
        rolled = jnp.concatenate([first[:, half:ROT], first[:, :half], first[:, ROT:]], axis=1)
        return jnp.concatenate([first * cosine + rolled * sine, block[:, 128:]], axis=1)

    def turn_back(block):
        first = block[:, :128]
        scaled = first * sine
        rolled = jnp.concatenate([scaled[:, half:ROT], scaled[:, :half], scaled[:, ROT:]], axis=1)
        return jnp.concatenate([first * cosine + rolled, block[:, 128:]], axis=1)

    queries = turn(projected[0, :, 0:HEAD_DIM]).astype(BF)
    keys = turn(projected[0, :, HEAD_DIM : 2 * HEAD_DIM]).astype(BF)
    values = projected[0, :, 2 * HEAD_DIM :].astype(BF)
    d_att_all = d_att_ref[0]
    keys_acc[...] = jnp.zeros_like(keys_acc)
    values_acc[...] = jnp.zeros_like(values_acc)
    d_queries = []
    for at in range(length // tile):
        rows = slice(at * tile, (at + 1) * tile)
        seen = (at + 1) * tile
        q = queries[rows]
        d_att = d_att_all[rows]
        k, v = keys[:seen], values[:seen]
        scores = lax.dot_general(q, k, NT, preferred_element_type=F32) * scale
        row = lax.broadcasted_iota(jnp.int32, scores.shape, 0) + at * tile
        column = lax.broadcasted_iota(jnp.int32, scores.shape, 1)
        scores = jnp.where(row >= column, scores, MASKED)
        top = jnp.max(scores, axis=1, keepdims=True)
        grown = jnp.exp(scores - top)
        prob = grown * (1.0 / jnp.sum(grown, axis=1, keepdims=True))
        prob_low = prob.astype(BF)
        att_ref[0, rows, :] = jnp.dot(prob_low, v, preferred_element_type=F32).astype(BF)
        d_prob = lax.dot_general(d_att, v, NT, preferred_element_type=F32)
        inner = jnp.sum(d_prob * prob, axis=1, keepdims=True)
        d_scores = (prob * (d_prob - inner)).astype(BF)
        d_queries.append(jnp.dot(d_scores, k, preferred_element_type=F32) * scale)
        keys_acc[:seen, :] += lax.dot_general(d_scores, q, TN, preferred_element_type=F32)
        values_acc[:seen, :] += lax.dot_general(prob_low, d_att, TN, preferred_element_type=F32)
    d_proj_ref[0, :, 0:HEAD_DIM] = turn_back(jnp.concatenate(d_queries, axis=0)).astype(BF)
    d_proj_ref[0, :, HEAD_DIM : 2 * HEAD_DIM] = turn_back(keys_acc[...] * scale).astype(BF)
    d_proj_ref[0, :, 2 * HEAD_DIM :] = values_acc[...].astype(BF)


def attention(projected, d_att):
    seqs, length, _ = projected.shape
    cosine, sine = rotary_tables(jnp.arange(length).astype(F32))
    half = ROT // 2
    sine_turn = jnp.concatenate([-sine[:, :half], sine[:, half:]], axis=1)
    cosine = jnp.concatenate([cosine, jnp.ones((length, 128 - ROT), F32)], axis=1)
    sine_turn = jnp.concatenate([sine_turn, jnp.zeros((length, 128 - ROT), F32)], axis=1)
    whole = pl.BlockSpec((length, 128), lambda s: (0, 0))
    one = lambda width: pl.BlockSpec((1, length, width), lambda s: (s, 0, 0))
    return pl.pallas_call(
        functools.partial(attention_body, 1.0 / math.sqrt(HEAD_DIM)),
        grid=(seqs,),
        in_specs=[one(3 * HEAD_DIM), whole, whole, one(HEAD_DIM)],
        out_specs=[one(HEAD_DIM), one(3 * HEAD_DIM)],
        out_shape=[
            jax.ShapeDtypeStruct((seqs, length, HEAD_DIM), BF),
            jax.ShapeDtypeStruct((seqs, length, 3 * HEAD_DIM), BF),
        ],
        scratch_shapes=[pltpu.VMEM((length, HEAD_DIM), F32), pltpu.VMEM((length, HEAD_DIM), F32)],
        compiler_params=pltpu.CompilerParams(vmem_limit_bytes=48 * 1024 * 1024),
        cost_estimate=pl.CostEstimate(
            flops=seqs * length * length * HEAD_DIM * 9,
            bytes_accessed=seqs * length * HEAD_DIM * 22,
            transcendentals=seqs * length * length,
        ),
        name="attention",
    )(projected, cosine, sine_turn, d_att)


def gelu_parts(values):
    phi_wide = 0.5 * (1.0 + lax.erf(values * (1.0 / math.sqrt(2.0))))
    density = jnp.exp(-0.5 * values * values) * (1.0 / math.sqrt(2.0 * math.pi))
    return values * phi_wide, phi_wide + values * density


def any_spec(count):
    return [pl.BlockSpec(memory_space=pl.ANY)] * count


def slots_needed(n_zero):
    return 8 * n_zero + 96


def gather_body(
    n_zero,
    rows,
    x_ref,
    g_ref,
    dn_ref,
    qk_ref,
    up_ref,
    wt_ref,
    x_all,
    g_all,
    dn_all,
    dense_own,
    qk_all,
    up_all,
    wt_all,
    send_sems,
    recv_sems,
    local_sems,
):
    place = Place(n_zero)
    wire = Wire(send_sems, recv_sems)
    block = rows * N_SEQ
    pairs = ((dn_ref, dn_all), (qk_ref, qk_all), (up_ref, up_all), (wt_ref, wt_all))
    exchanges = [SeqExchange(wire, place, send, whole, rows) for send, whole in pairs]
    dn, qk, up, wt = [LineGather(wire, place, whole, block) for _, whole in pairs]
    x = PlaneGather(wire, place, x_ref, x_all)
    g = PlaneGather(wire, place, g_ref, g_all)
    dense = DenseExchange(
        wire,
        place,
        lambda c: dn_all.at[pl.ds(pl.multiple_of(c * HEAD_W, HEAD_W), HEAD_W)],
        lambda c: dense_own.at[:, pl.ds(pl.multiple_of(c * HEAD_W, HEAD_W), HEAD_W)],
    )
    place.barrier()
    for k, exchange in enumerate(exchanges):
        exchange.start(local_sems.at[k])
        if k == 1:
            x.start(local_sems.at[4])
            g.start(local_sems.at[5])
    exchanges[0].wait()
    dn.pass_on(1)
    exchanges[1].wait()
    qk.pass_on(1)
    exchanges[2].wait()
    up.pass_on(1)
    exchanges[3].wait()
    x.turn()
    g.turn()
    for line in (dn, qk, up, wt):
        for k in range(2, n_zero):
            line.take(k - 1)
            line.pass_on(k)
        line.take(n_zero - 1)
        if line is dn:
            dense.start(local_sems.at[6])
            x.turn_again()
            g.turn_again()
        if line is qk:
            wt.pass_on(1)
            x.wait()
            g.wait()
            dense.wait()
    wire.finish()


def gather(n_zero, rows, x, g, dn, qk, up, wt):
    shape = lambda *dims: jax.ShapeDtypeStruct(dims, BF)
    slots = slots_needed(n_zero)
    return pl.pallas_call(
        functools.partial(gather_body, n_zero, rows),
        in_specs=any_spec(6),
        out_specs=any_spec(7),
        out_shape=[
            shape(N_DP, N_SEQ, *x.shape),
            shape(N_DP, N_SEQ, *g.shape),
            shape(D, HEAD_W),
            shape(HEAD_W, D),
            shape(D, 3 * HEAD_W),
            shape(D, HID_W),
            shape(D, HID_W),
        ],
        scratch_shapes=[
            pltpu.SemaphoreType.DMA((slots,)),
            pltpu.SemaphoreType.DMA((slots,)),
            pltpu.SemaphoreType.DMA((8,)),
        ],
        compiler_params=pltpu.CompilerParams(collective_id=0, has_side_effects=True),
        name="gather",
    )(x, g, dn, qk, up, wt)


def scatter_body(n_zero, rows, *refs):
    out_parts, tok_parts, dn_part, qk_part, up_part, wt_part = refs[:6]
    out_sum, tok_sum, dn_home, qk_home, up_home, wt_home, dn_cols = refs[6:13]
    send_sems, recv_sems, local_sems = refs[13:16]
    scratch = list(refs[16:])
    take = lambda count: [scratch.pop(0) for _ in range(count)]
    place = Place(n_zero)
    wire = Wire(send_sems, recv_sems)
    block = rows * N_SEQ
    plane = []
    for k, (parts, result) in enumerate(((out_parts, out_sum), (tok_parts, tok_sum))):
        mate, far, across, turned, total, own = take(6)
        sem = local_sems.at[k]
        plane.append((PlaneScatter(wire, place, parts, mate, far, across, turned, total, own, sem), result))
    lines = []
    pairs = ((dn_cols, dn_home), (qk_part, qk_home), (up_part, up_home), (wt_part, wt_home))
    for k, (parts, home) in enumerate(pairs):
        ups, downs, total, own = take(4)
        line = LineScatter(wire, place, parts, ups, downs, total, own, block, local_sems.at[2 + k])
        lines.append((line, Home(wire, place, total, home, rows), k))
    dense = DenseExchange(
        wire,
        place,
        lambda c: dn_part.at[:, pl.ds(pl.multiple_of(c * HEAD_W, HEAD_W), HEAD_W)],
        lambda c: dn_cols.at[pl.ds(pl.multiple_of(c * HEAD_W, HEAD_W), HEAD_W)],
    )
    place.barrier()
    dense.start(local_sems.at[6])
    for scatter, _ in plane:
        scatter.start()
    dn, qk, up, wt = lines
    todo = [(line, k) for line in (wt, up, qk, dn) for k in range(n_zero - 1)]
    for index, (line, k) in enumerate(todo):
        if index == 2:
            for scatter, _ in plane:
                scatter.turn()
        if index == 4:
            for scatter, _ in plane:
                scatter.turn_again()
        if line is dn and k == 0:
            dense.wait()
        line[0].step(k)
        if k == n_zero - 2:
            line[0].last()
            line[1].start(local_sems.at[7 + line[2]])
    for scatter, result in plane:
        scatter.last()
        copy = pltpu.make_async_copy(scatter.total, result, scatter.sem)
        copy.start()
        copy.wait()
    for _, home, _ in lines:
        home.wait()
    wire.finish()


def scatter(n_zero, rows, out_parts, tok_parts, dn_part, qk_part, up_part, wt_part):
    tokens = out_parts.shape[2]
    block = rows * N_SEQ
    slots = slots_needed(n_zero)
    vmem = lambda *dims: pltpu.VMEM(dims, BF)
    widths = (HEAD_W, 3 * HEAD_W, HID_W, HID_W)
    scratch = []
    for _ in range(2):
        scratch += [vmem(2, 2, tokens, D), vmem(tokens, D), vmem(tokens, D), vmem(tokens, D)]
        scratch += [pltpu.VMEM((tokens, D), F32), vmem(tokens, D)]
    for width in widths:
        scratch += [vmem(n_zero, block, width), vmem(n_zero, block, width)]
        scratch += [vmem(block, width), vmem(block, width)]
    return pl.pallas_call(
        functools.partial(scatter_body, n_zero, rows),
        in_specs=any_spec(6),
        out_specs=any_spec(7),
        out_shape=[jax.ShapeDtypeStruct((tokens, D), F32)] * 2
        + [jax.ShapeDtypeStruct((N_DP, N_SEQ, rows, width), BF) for width in widths]
        + [jax.ShapeDtypeStruct((D, HEAD_W), BF)],
        scratch_shapes=[
            pltpu.SemaphoreType.DMA((slots,)),
            pltpu.SemaphoreType.DMA((slots,)),
            pltpu.SemaphoreType.DMA((12,)),
        ]
        + scratch,
        compiler_params=pltpu.CompilerParams(
            collective_id=1, has_side_effects=True, vmem_limit_bytes=60 * 1024 * 1024
        ),
        name="scatter",
    )(out_parts, tok_parts, dn_part, qk_part, up_part, wt_part)


def adam_body(decay, flipped, home, param, first, second, new, first_new, second_new, grad_out):
    gradient = home[0, 0].astype(F32)
    if flipped:
        gradient = gradient.T
    updated = adam_step(param[...], gradient, first[...], second[...], decay)
    new[...], first_new[...], second_new[...] = updated
    grad_out[...] = gradient


def adam(home, pieces, param, first, second, flipped=False):
    rows, width = home.shape[2], home.shape[3] // pieces
    if flipped:
        block = pl.BlockSpec((width, rows), lambda c, t: (t * PARTS + c, 0))
    else:
        block = pl.BlockSpec((rows, width), lambda c, t: (0, t * PARTS + c))
    return pl.pallas_call(
        functools.partial(adam_body, WEIGHT_DECAY, flipped),
        grid=(PARTS, pieces),
        in_specs=[
            pl.BlockSpec((1, 1, rows, width), lambda c, t: (c // N_SEQ, c % N_SEQ, 0, t)),
            block,
            block,
            block,
        ],
        out_specs=[block] * 4,
        out_shape=[jax.ShapeDtypeStruct(param.shape, F32)] * 4,
        compiler_params=pltpu.CompilerParams(vmem_limit_bytes=48 * 1024 * 1024),
        name="adam",
    )(home, param, first, second)


def make_body(sizes):
    n_zero = sizes["zero"]
    everywhere = ("dp", "zero", "seq")

    def body(
        inputs,
        out_grad,
        vectors,
        qkv_weight,
        dense_weight,
        up_weight,
        down_weight,
        vectors_first,
        qkv_first,
        dense_first,
        up_first,
        down_first,
        vectors_second,
        qkv_second,
        dense_second,
        up_second,
        down_second,
    ):
        dp_i, zero_i, seq_i = (lax.axis_index(axis) for axis in everywhere)
        part_i = dp_i * N_SEQ + seq_i
        seqs_here, local_len = inputs.shape[0], inputs.shape[1]
        token_rows = seqs_here * local_len
        rows = qkv_weight.shape[0]
        pick = lambda value, index, axis: lax.dynamic_index_in_dim(value, index, axis, keepdims=False)

        vec_all = lax.all_gather(vectors.astype(BF), ("zero", "seq"), axis=0, tiled=True).astype(F32)
        ln1_gain, ln1_bias = vec_all[:D], vec_all[D : 2 * D]
        qkv_bias = vec_all[2 * D : 5 * D].reshape(3, PARTS, HEAD_W)
        dense_bias = vec_all[5 * D : 6 * D]
        ln2_gain, ln2_bias = vec_all[6 * D : 7 * D], vec_all[7 * D : 8 * D]
        up_bias = vec_all[8 * D : 8 * D + FF].reshape(PARTS, HID_W)
        down_bias = vec_all[8 * D + FF :]

        def columns(value, width):
            wide = value.shape[1] // N_DP
            half = lax.dynamic_slice_in_dim(value, dp_i * wide, wide, 1).astype(BF)
            return half.reshape(rows, N_SEQ, width).transpose(1, 0, 2)

        qk_low = jnp.concatenate(
            [columns(qkv_weight[:, t * D : (t + 1) * D], HEAD_W) for t in range(3)], axis=2
        )
        dn_low = columns(dense_weight, HEAD_W)
        up_low = columns(up_weight, HID_W)
        wt_low = lax.dynamic_slice_in_dim(down_weight, dp_i * (FF // N_DP), FF // N_DP, 0).astype(BF)
        wt_low = wt_low.reshape(N_SEQ, HID_W, rows).transpose(0, 2, 1)

        tokens_low = inputs.reshape(token_rows, D)
        grad_low = out_grad.reshape(token_rows, D)
        tokens_all, grad_all, _, dense_own, qkv_own, up_own, wt_own = gather(
            n_zero, rows, tokens_low, grad_low, dn_low, qk_low, up_low, wt_low
        )
        seqs = N_DP * seqs_here
        length = N_SEQ * local_len
        order = lambda value: value.reshape(N_DP, N_SEQ, seqs_here, local_len, -1).transpose(
            0, 2, 1, 3, 4
        ).reshape(seqs * length, -1)
        unorder = lambda value: value.reshape(N_DP, seqs_here, N_SEQ, local_len, D).transpose(
            0, 2, 1, 3, 4
        ).reshape(N_DP, N_SEQ, token_rows, D)
        tokens = order(tokens_all)
        grads = order(grad_all)

        def statistics(values):
            average = jnp.mean(values, axis=-1, keepdims=True)
            centred = values - average
            spread = jnp.mean(centred * centred, axis=-1, keepdims=True)
            return centred, lax.rsqrt(spread + NORM_EPSILON)

        centred, rate = statistics(tokens.astype(F32))
        xhat = centred * rate
        normed_one = (xhat * ln1_gain + ln1_bias).astype(BF)
        normed_two = (xhat * ln2_gain + ln2_bias).astype(BF)

        projected = jnp.dot(normed_one, qkv_own, preferred_element_type=F32)
        projected = projected + pick(qkv_bias, part_i, 1).reshape(3 * HEAD_W)
        d_att = lax.dot_general(grads, dense_own, NT, preferred_element_type=F32).astype(BF)
        attended, d_proj = attention(
            projected.reshape(seqs, length, 3 * HEAD_W), d_att.reshape(seqs, length, HEAD_W)
        )
        attended = attended.reshape(seqs * length, HEAD_W)
        d_proj = d_proj.reshape(seqs * length, 3 * HEAD_W)
        d_qkv_bias = jnp.sum(d_proj.astype(F32), axis=0)
        d_normed_one = lax.dot_general(d_proj, qkv_own, NT, preferred_element_type=F32)
        qk_part = lax.dot_general(normed_one, d_proj, TN, preferred_element_type=F32).astype(BF)
        dn_part = lax.dot_general(attended, grads, TN, preferred_element_type=F32).astype(BF)

        pre_act = jnp.dot(normed_two, up_own, preferred_element_type=F32) + pick(up_bias, part_i, 0)
        hidden_wide, slope = gelu_parts(pre_act)
        hidden = hidden_wide.astype(BF)
        wt_part = lax.dot_general(grads, hidden, TN, preferred_element_type=F32).astype(BF)
        d_hidden = jnp.dot(grads, wt_own, preferred_element_type=F32)
        d_pre = (d_hidden * slope).astype(BF)
        d_up_bias = jnp.sum(d_pre.astype(F32), axis=0)
        up_part = lax.dot_general(normed_two, d_pre, TN, preferred_element_type=F32).astype(BF)
        d_normed_two = lax.dot_general(d_pre, up_own, NT, preferred_element_type=F32)

        out_part = jnp.dot(attended, dense_own, preferred_element_type=F32) + lax.dot_general(
            hidden, wt_own, NT, preferred_element_type=F32
        )
        d_gain_one = jnp.sum(d_normed_one * xhat, axis=0)
        d_bias_one = jnp.sum(d_normed_one, axis=0)
        d_gain_two = jnp.sum(d_normed_two * xhat, axis=0)
        d_bias_two = jnp.sum(d_normed_two, axis=0)
        tok_part = d_normed_one * ln1_gain + d_normed_two * ln2_gain

        out_sum, d_xhat, dn_home, qk_home, up_home, wt_home, _ = scatter(
            n_zero,
            rows,
            unorder(out_part.astype(BF)),
            unorder(tok_part.astype(BF)),
            dn_part,
            qk_part,
            up_part,
            wt_part,
        )

        tokens_wide = tokens_low.astype(F32)
        grad_wide = grad_low.astype(F32)
        outputs = (tokens_wide + out_sum + dense_bias + down_bias).astype(BF).reshape(inputs.shape)
        centred_own, rate_own = statistics(tokens_wide)
        xhat_own = centred_own * rate_own
        d_tokens = rate_own * (
            d_xhat
            - jnp.mean(d_xhat, axis=-1, keepdims=True)
            - xhat_own * jnp.mean(d_xhat * xhat_own, axis=-1, keepdims=True)
        )
        input_grad = (grad_wide + d_tokens).astype(BF).reshape(inputs.shape)

        d_out_bias = jnp.sum(grad_wide, axis=0)
        place_in = lambda value, count: lax.dynamic_update_index_in_dim(
            jnp.zeros((value.shape[0], count, value.shape[1]), F32), value, part_i, 1
        ).reshape(-1)
        vector_local = jnp.concatenate(
            [
                d_gain_one,
                d_bias_one,
                place_in(d_qkv_bias.reshape(3, HEAD_W), PARTS),
                d_out_bias,
                d_gain_two,
                d_bias_two,
                place_in(d_up_bias.reshape(1, HID_W), PARTS),
                d_out_bias,
            ]
        )
        vector_sum = lax.psum(vector_local, everywhere)
        vectors_grad = lax.dynamic_slice_in_dim(
            vector_sum, (zero_i * N_SEQ + seq_i) * vectors.shape[0], vectors.shape[0], 0
        )

        vec_upd = adam_step(vectors, vectors_grad, vectors_first, vectors_second, 0.0) + (vectors_grad,)
        qkv_upd = adam(qk_home, 3, qkv_weight, qkv_first, qkv_second)
        dense_upd = adam(dn_home, 1, dense_weight, dense_first, dense_second)
        up_upd = adam(up_home, 1, up_weight, up_first, up_second)
        down_upd = adam(wt_home, 1, down_weight, down_first, down_second, flipped=True)
        updates = (vec_upd, qkv_upd, dense_upd, up_upd, down_upd)
        picked = lambda k: tuple(update[k] for update in updates)
        return (outputs, input_grad) + picked(3) + picked(0) + picked(1) + picked(2)

    return body


def solution(mesh):
    wide = P(("dp", "zero"), "seq", None)
    vector = P(("zero", "seq"))
    rows = P(("zero", "seq"), None)
    columns = P(None, ("zero", "seq"))
    state = (vector, rows, rows, rows, columns)
    return jax.shard_map(
        make_body(dict(mesh.shape)),
        mesh=mesh,
        in_specs=(wide, wide) + state * 3,
        out_specs=(wide, wide) + state * 4,
        check_vma=False,
    )
```

```python
import functools
import math

import jax
import jax.numpy as jnp
from jax import lax
from jax.experimental import pallas as pl
from jax.experimental.pallas import tpu as pltpu
from jax.sharding import PartitionSpec as P

D = 2048
HEADS = 8
HEAD_DIM = 256
FF = 8192
ROT = 64
ADAM_STEP = 4

BETA_ONE = 0.9
BETA_TWO = 0.95
LEARN_RATE = 0.5
EPSILON = 1e-08
WEIGHT_DECAY = 0.1
NORM_EPSILON = 1e-05
MASKED = -1e30
N_DP = 2
N_SEQ = 4
PARTS = N_DP * N_SEQ
HEAD_W = D // PARTS
HID_W = FF // PARTS
BF = jnp.bfloat16
F32 = jnp.float32
NT = (((1,), (1,)), ((), ()))
TN = (((0,), (0,)), ((), ()))


def rotary_tables(positions):
    half_rot = ROT // 2
    exponent = jnp.arange(half_rot, dtype=F32) * (2.0 / ROT)
    inverse = jnp.power(10000.0, -exponent)
    angles = positions[:, None] * inverse[None, :]
    angles = jnp.concatenate([angles, angles], axis=1)
    return (jnp.cos(angles), jnp.sin(angles))


def adam_step(parameter, gradient, first_moment, second, decay_rate):
    first_new = BETA_ONE * first_moment + (1.0 - BETA_ONE) * gradient
    second_new = BETA_TWO * second + (1.0 - BETA_TWO) * gradient * gradient
    first_hat = first_new / (1.0 - BETA_ONE**ADAM_STEP)
    second_hat = second_new / (1.0 - BETA_TWO**ADAM_STEP)
    param_new = parameter - LEARN_RATE * (
        first_hat / (jnp.sqrt(second_hat) + EPSILON) + decay_rate * parameter
    )
    return (param_new, first_new, second_new)


class Wire:
    def __init__(self, send_sems, recv_sems):
        self.send_sems, self.recv_sems, self.used = send_sems, recv_sems, 0
        self.sent = []

    def slot(self):
        self.used += 1
        return self.used - 1

    def copy(self, slot, source, target, device):
        return pltpu.make_async_remote_copy(
            src_ref=source,
            dst_ref=target,
            send_sem=self.send_sems.at[slot],
            recv_sem=self.recv_sems.at[slot],
            device_id=device,
            device_id_type=pl.DeviceIdType.MESH,
        )

    def send(self, slot, source, target, device, when=None):
        copy = self.copy(slot, source, target, device)
        guarded(when, copy.start)
        self.sent.append((copy, when))

    def receive(self, slot, target, device, when=None):
        copy = self.copy(slot, target, target, device)
        guarded(when, copy.wait_recv)

    def finish(self):
        for copy, when in self.sent:
            guarded(when, copy.wait_send)
        self.sent = []


def guarded(when, action):
    if when is None:
        action()
    else:
        pl.when(when)(action)


class Place:
    def __init__(self, n_zero):
        self.n = n_zero
        self.dp, self.z, self.s = (lax.axis_index(a) for a in ("dp", "zero", "seq"))
        flip = lambda value, bit: jnp.bitwise_xor(value, bit)
        self.dp_far, self.s_far, self.s_core = 1 - self.dp, flip(self.s, 2), flip(self.s, 1)
        self.s_both = flip(self.s, 3)
        self.across = {"dp": self.dp_far}
        self.far = {"seq": self.s_far}
        self.core = {"seq": self.s_core}
        self.above, self.below = {"zero": self.z + 1}, {"zero": self.z - 1}
        self.part = self.dp * N_SEQ + self.s

    def others(self):
        for step in range(1, N_DP * N_SEQ):
            at = lax.rem(self.part + step, N_DP * N_SEQ)
            dp, s = lax.div(at, N_SEQ), lax.rem(at, N_SEQ)
            yield step, dp, s, {"dp": dp, "seq": s}

    def barrier(self):
        gate = pltpu.get_barrier_semaphore()
        signal = lambda device: pl.semaphore_signal(
            gate, inc=1, device_id=device, device_id_type=pl.DeviceIdType.MESH
        )
        for _, _, _, device in self.others():
            signal(device)
        pl.when(self.z < self.n - 1)(lambda: signal(self.above))
        pl.when(self.z > 0)(lambda: signal(self.below))
        ends = (self.z < self.n - 1).astype(jnp.int32) + (self.z > 0).astype(jnp.int32)
        pl.semaphore_wait(gate, N_DP * N_SEQ - 1 + ends)


class LineGather:
    def __init__(self, wire, place, whole, rows):
        self.wire, self.place, self.whole, self.rows = wire, place, whole, rows
        self.ups = [wire.slot() for _ in range(place.n - 1)]
        self.downs = [wire.slot() for _ in range(place.n - 1)]

    def block(self, index):
        return self.whole.at[pl.ds(pl.multiple_of(index * self.rows, self.rows), self.rows)]

    def take(self, step):
        p = self.place
        self.wire.receive(self.ups[step - 1], self.block(jnp.maximum(p.z - step, 0)), p.below, p.z >= step)
        self.wire.receive(
            self.downs[step - 1], self.block(jnp.minimum(p.z + step, p.n - 1)), p.above, p.z + step < p.n
        )

    def pass_on(self, step):
        p = self.place
        up, down = jnp.maximum(p.z - step + 1, 0), jnp.minimum(p.z + step - 1, p.n - 1)
        self.wire.send(
            self.ups[step - 1], self.block(up), self.block(up), p.above, (p.z < p.n - 1) & (p.z >= step - 1)
        )
        self.wire.send(
            self.downs[step - 1], self.block(down), self.block(down), p.below, (p.z > 0) & (p.z + step <= p.n)
        )


class SeqExchange:
    def __init__(self, wire, place, send, whole, rows):
        self.wire, self.place, self.out, self.whole, self.rows = wire, place, send, whole, rows
        self.slots = [wire.slot() for _ in range(1, N_SEQ)]

    def target(self, s):
        row = (self.place.z * N_SEQ + s) * self.rows
        return self.whole.at[pl.ds(pl.multiple_of(row, self.rows), self.rows)]

    def start(self, local_sem):
        p = self.place
        for step in range(1, N_SEQ):
            to = lax.rem(p.s + step, N_SEQ)
            self.wire.send(self.slots[step - 1], self.out.at[to], self.target(p.s), {"seq": to})
        own = pltpu.make_async_copy(self.out.at[p.s], self.target(p.s), local_sem)
        own.start()
        self.own = own

    def wait(self):
        p = self.place
        for step in range(1, N_SEQ):
            source = lax.rem(p.s - step + N_SEQ, N_SEQ)
            self.wire.receive(self.slots[step - 1], self.target(source), {"seq": source})
        self.own.wait()


class PlaneGather:
    def __init__(self, wire, place, block, whole):
        self.wire, self.place, self.own, self.whole = wire, place, block, whole
        self.slots = {name: wire.slot() for name in ("far", "across", "both0", "both1", "c0", "c1", "c2", "c3")}
        self.rows = block.shape[0]
        self.half = self.rows // 2

    def at(self, dp, s):
        row = (dp * N_SEQ + s) * self.rows
        return self.whole.at[pl.ds(pl.multiple_of(row, self.rows), self.rows)]

    def start(self, local_sem):
        p, w, slots = self.place, self.wire, self.slots
        mine = self.at(p.dp, p.s)
        w.send(slots["far"], self.own, mine, p.far)
        w.send(slots["across"], self.own, mine, p.across)
        w.send(slots["c0"], self.own, mine, p.core)
        self.copied = pltpu.make_async_copy(self.own, mine, local_sem)
        self.copied.start()

    def turn(self):
        p, w, slots, h = self.place, self.wire, self.slots, self.half
        far, across = self.at(p.dp, p.s_far), self.at(p.dp_far, p.s)
        w.receive(slots["far"], far, p.far)
        w.send(slots["both0"], far.at[pl.ds(0, h)], far.at[pl.ds(0, h)], p.across)
        w.send(slots["c1"], far, far, p.core)
        w.receive(slots["across"], across, p.across)
        w.send(slots["both1"], across.at[pl.ds(h, h)], across.at[pl.ds(h, h)], p.far)
        w.send(slots["c2"], across, across, p.core)

    def turn_again(self):
        p, w, slots, h = self.place, self.wire, self.slots, self.half
        both = self.at(p.dp_far, p.s_far)
        w.receive(slots["both0"], both.at[pl.ds(0, h)], p.across)
        w.receive(slots["both1"], both.at[pl.ds(h, h)], p.far)
        w.send(slots["c3"], both, both, p.core)

    def wait(self):
        p, w, slots = self.place, self.wire, self.slots
        w.receive(slots["c0"], self.at(p.dp, p.s_core), p.core)
        w.receive(slots["c1"], self.at(p.dp, p.s_both), p.core)
        w.receive(slots["c2"], self.at(p.dp_far, p.s_core), p.core)
        w.receive(slots["c3"], self.at(p.dp_far, p.s_both), p.core)
        self.copied.wait()


def add_rows(target, *sources):
    rows = target.shape[0]
    tile = 32 if rows % 32 == 0 else 16

    def one(i, carry):
        at = pl.ds(pl.multiple_of(i * tile, tile), tile)
        total = sources[0][at, :].astype(F32)
        for source in sources[1:]:
            total = total + source[at, :].astype(F32)
        target[at, :] = total.astype(target.dtype)
        return carry

    lax.fori_loop(0, rows // tile, one, 0)


class LineScatter:
    def __init__(self, wire, place, parts, held, total, own, rows, sem):
        self.wire, self.place, self.parts, self.rows = wire, place, parts, rows
        self.held, self.total, self.own, self.sem, self.slot = held, total, own, sem, 0
        self.up_slots = [wire.slot() for _ in range(place.n)]
        self.down_slots = [wire.slot() for _ in range(place.n)]

    def part(self, j):
        return self.parts.at[pl.ds(pl.multiple_of(j * self.rows, self.rows), self.rows)]

    def fetch(self, j, target):
        return pltpu.make_async_copy(self.part(j), target, self.sem)

    def advance(self):
        p, slot = self.place, self.slot
        self.slot = slot + 1
        top = p.n - 1
        up = jnp.minimum(top - slot + p.z, top)
        self.hop(up, up + 1, self.up_slots[0] + up, p.above, p.below, p.z <= slot, p.z == 0)
        down = jnp.maximum(slot - top + p.z, 0)
        self.hop(down, down, self.down_slots[0] + down, p.below, p.above, top - p.z <= slot, p.z == top)

    def hop(self, j, index, slot, onto, source, active, first):
        held = self.held.at[index]

        def go():
            @pl.when(first)
            def _():
                copy = self.fetch(j, held)
                copy.start()
                copy.wait()

            @pl.when(jnp.logical_not(first))
            def _():
                copy = self.fetch(j, self.own)
                copy.start()
                self.wire.receive(slot, held, source)
                copy.wait()
                add_rows(held, held, self.own)

        pl.when(active)(go)
        self.wire.send(slot, held, held, onto, active)

    def last(self):
        p = self.place
        while self.slot < p.n - 1:
            self.advance()
        copy = self.fetch(p.z, self.own)
        copy.start()
        copy.wait()
        up, down = self.held.at[p.z + 1], self.held.at[p.z]

        @pl.when(p.z == 0)
        def _():
            self.arrive(down, self.down_slots, p.above)
            add_rows(self.total, self.own, down)

        @pl.when(p.z == p.n - 1)
        def _():
            self.arrive(up, self.up_slots, p.below)
            add_rows(self.total, self.own, up)

        @pl.when((p.z > 0) & (p.z < p.n - 1))
        def _():
            self.arrive(up, self.up_slots, p.below)
            self.arrive(down, self.down_slots, p.above)
            add_rows(self.total, self.own, up, down)

    def arrive(self, held, slots, source):
        self.wire.receive(slots[0] + self.place.z, held, source)


class Home:
    def __init__(self, wire, place, total, home, rows):
        self.wire, self.place, self.total, self.home, self.rows = wire, place, total, home, rows
        self.slots = [wire.slot() for _ in range(1, N_DP * N_SEQ)]

    def start(self, local_sem):
        p = self.place
        piece = lambda s: self.total.at[pl.ds(pl.multiple_of(s * self.rows, self.rows), self.rows)]
        for step, dp, s, device in p.others():
            self.wire.send(self.slots[step - 1], piece(s), self.home.at[p.dp, p.s], device)
        self.copied = pltpu.make_async_copy(piece(p.s), self.home.at[p.dp, p.s], local_sem)
        self.copied.start()

    def wait(self):
        p = self.place
        parts = N_DP * N_SEQ
        for step in range(1, parts):
            at = lax.rem(p.part - step + parts, parts)
            dp, s = lax.div(at, N_SEQ), lax.rem(at, N_SEQ)
            self.wire.receive(self.slots[step - 1], self.home.at[dp, s], {"dp": dp, "seq": s})
        self.copied.wait()


class DenseExchange:
    def __init__(self, wire, place, source, target):
        self.wire, self.place, self.source, self.target = wire, place, source, target
        self.slots = [wire.slot() for _ in range(1, N_DP * N_SEQ)]

    def start(self, local_sem):
        p = self.place
        for step, dp, s, device in p.others():
            self.wire.send(self.slots[step - 1], self.source(dp * N_SEQ + s), self.target(p.part), device)
        self.copied = pltpu.make_async_copy(self.source(p.part), self.target(p.part), local_sem)
        self.copied.start()

    def wait(self):
        p = self.place
        parts = N_DP * N_SEQ
        for step in range(1, parts):
            at = lax.rem(p.part - step + parts, parts)
            device = {"dp": lax.div(at, N_SEQ), "seq": lax.rem(at, N_SEQ)}
            self.wire.receive(self.slots[step - 1], self.target(at), device)
        self.copied.wait()


class PlaneScatter:
    def __init__(self, wire, place, parts, mate, from_far, from_across, turned, total, own, sem):
        self.wire, self.place, self.parts, self.mate, self.sums = wire, place, parts, mate, mate
        self.from_far, self.from_across, self.turned = from_far, from_across, turned
        self.total, self.own, self.sem = total, own, sem
        self.rows = total.shape[0]
        self.half = self.rows // 2
        self.core_slots = [[wire.slot() for _ in range(2)] for _ in range(2)]
        names = ("turn_across", "turn_far", "far0", "far1", "across0", "across1")
        self.slots = {name: wire.slot() for name in names}

    def part(self, dp, s):
        row = (dp * N_SEQ + s) * self.rows
        return self.parts.at[pl.ds(pl.multiple_of(row, self.rows), self.rows)]

    def start(self):
        p = self.place
        core = lax.rem(p.s_core, 2)
        for dp in range(2):
            for y in range(2):
                self.wire.send(
                    self.core_slots[dp][y], self.part(dp, 2 * y + core), self.mate.at[dp, y], p.core
                )

    def combine(self, dp, y):
        p = self.place
        core = lax.rem(p.s, 2)
        for d in range(2):
            for v in range(2):

                @pl.when((dp == d) & (y == v))
                def _(d=d, v=v):
                    copy = pltpu.make_async_copy(self.part(d, 2 * v + core), self.own, self.sem)
                    copy.start()
                    self.wire.receive(self.core_slots[d][v], self.mate.at[d, v], p.core)
                    copy.wait()
                    add_rows(self.sums.at[d, v], self.own, self.mate.at[d, v])

    def turn(self):
        p, w, h, slots = self.place, self.wire, self.half, self.slots
        y = lax.div(p.s, 2)
        y_far = 1 - y
        low, high = pl.ds(0, h), pl.ds(h, h)
        self.combine(p.dp_far, y_far)
        both = self.sums.at[p.dp_far, y_far]
        w.send(slots["turn_across"], both.at[low], self.turned.at[low], p.across)
        w.send(slots["turn_far"], both.at[high], self.turned.at[high], p.far)
        self.combine(p.dp, y_far)
        far = self.sums.at[p.dp, y_far]
        w.send(slots["far1"], far.at[high], self.from_far.at[high], p.far)
        self.combine(p.dp_far, y)
        across = self.sums.at[p.dp_far, y]
        w.send(slots["across0"], across.at[low], self.from_across.at[low], p.across)
        self.combine(p.dp, y)

    def turn_again(self):
        p, w, h, slots = self.place, self.wire, self.half, self.slots
        y = lax.div(p.s, 2)
        low, high = pl.ds(0, h), pl.ds(h, h)
        far, across = self.sums.at[p.dp, 1 - y], self.sums.at[p.dp_far, y]
        w.receive(slots["turn_across"], self.turned.at[low], p.across)
        add_rows(far.at[low], far.at[low], self.turned.at[low])
        w.send(slots["far0"], far.at[low], self.from_far.at[low], p.far)
        w.receive(slots["turn_far"], self.turned.at[high], p.far)
        add_rows(across.at[high], across.at[high], self.turned.at[high])
        w.send(slots["across1"], across.at[high], self.from_across.at[high], p.across)

    def last(self):
        p, w, h, slots = self.place, self.wire, self.half, self.slots
        low, high = pl.ds(0, h), pl.ds(h, h)
        w.receive(slots["far1"], self.from_far.at[high], p.far)
        w.receive(slots["far0"], self.from_far.at[low], p.far)
        w.receive(slots["across0"], self.from_across.at[low], p.across)
        w.receive(slots["across1"], self.from_across.at[high], p.across)
        add_rows(self.total, self.sums.at[p.dp, lax.div(p.s, 2)], self.from_far, self.from_across)


def gelu_parts(values):
    phi_wide = 0.5 * (1.0 + lax.erf(values * (1.0 / math.sqrt(2.0))))
    density = jnp.exp(-0.5 * values * values) * (1.0 / math.sqrt(2.0 * math.pi))
    return values * phi_wide, phi_wide + values * density


TILE = 256


def pipe(body, grid, ins, outs, refs):
    pltpu.emit_pipeline(
        body, grid=(grid,), in_specs=[spec for spec in ins], out_specs=[spec for spec in outs]
    )(*refs)


def tall(width, tile=TILE):
    return pl.BlockSpec((tile, width), lambda i: (i, 0))


def slim(height, tile=TILE):
    return pl.BlockSpec((height, tile), lambda i: (0, i))


def fixed(height, width):
    return pl.BlockSpec((height, width), lambda i: (0, 0), pipeline_mode=pl.Buffered(1))


def column_sums(total, values):
    rows, width = values.shape
    total[...] += jnp.sum(values.reshape(rows // 8, 8, width), axis=0)


def rotate(block, cosine, sine):
    half = ROT // 2
    first = block[:, :128]
    rolled = jnp.concatenate([first[:, half:ROT], first[:, :half], first[:, ROT:]], axis=1)
    return jnp.concatenate([first * cosine + rolled * sine, block[:, 128:]], axis=1)


def rotate_back(block, cosine, sine):
    half = ROT // 2
    first = block[:, :128]
    scaled = first * sine
    rolled = jnp.concatenate([scaled[:, half:ROT], scaled[:, :half], scaled[:, ROT:]], axis=1)
    return jnp.concatenate([first * cosine + rolled, block[:, 128:]], axis=1)


class Layer:
    def __init__(self, refs):
        self.__dict__.update(refs)
        self.tokens = self.x.shape[0]
        self.length = self.tokens // N_DP
        self.tiles = self.tokens // TILE

    def clear(self):
        for total in (self.gain1, self.bias1, self.gain2, self.bias2, self.qkv_total, self.up_total):
            total[...] = jnp.zeros_like(total)

    def normalise(self, part, of):
        count = self.tokens // of
        rows = pl.ds(part * count, count)

        def body(x, n1, n2, xh):
            def some(i, carry):
                at = pl.ds(pl.multiple_of(i * 32, 32), 32)
                values = x[at, :].astype(F32)
                centred = values - jnp.mean(values, axis=1, keepdims=True)
                spread = jnp.mean(centred * centred, axis=1, keepdims=True)
                xhat = centred * lax.rsqrt(spread + NORM_EPSILON)
                xh[at, :] = xhat.astype(BF)
                n1[at, :] = (xhat * self.vec[0:1, :] + self.vec[1:2, :]).astype(BF)
                n2[at, :] = (xhat * self.vec[2:3, :] + self.vec[3:4, :]).astype(BF)
                return carry

            lax.fori_loop(0, TILE // 32, some, 0)

        pipe(
            body,
            count // TILE,
            [tall(D)],
            [tall(D)] * 3,
            [ref.at[rows] for ref in (self.x, self.n1, self.n2, self.xhat)],
        )

    def attend(self, seq):
        scale = 1.0 / math.sqrt(HEAD_DIM)
        length = self.length

        def project(q_refs, n1, qkv, g, dense):
            at = pl.ds(pl.multiple_of(pl.program_id(0) * TILE, TILE), TILE)
            cosine, sine = self.cos[at, :], self.sin[at, :]
            wide = jnp.dot(n1[...], qkv[...], preferred_element_type=F32) + self.qkv_bias[...]
            q_refs[0][at, :] = rotate(wide[:, :HEAD_W], cosine, sine).astype(BF)
            q_refs[1][at, :] = rotate(wide[:, HEAD_W : 2 * HEAD_W], cosine, sine).astype(BF)
            q_refs[2][at, :] = wide[:, 2 * HEAD_W :].astype(BF)
            q_refs[3][at, :] = lax.dot_general(g[...], dense[...], NT, preferred_element_type=F32).astype(BF)

        def one(q_ref, k_ref, v_ref, d_att_ref, k_total, v_total):
            base = seq * length
            rows = pl.ds(base, length)
            pipe(
                functools.partial(project, (q_ref, k_ref, v_ref, d_att_ref)),
                length // TILE,
                [tall(D), fixed(D, 3 * HEAD_W), tall(D), fixed(HEAD_W, D)],
                [],
                (self.n1.at[rows], self.qkv, self.g.at[rows], self.dense),
            )
            k_total[...] = jnp.zeros_like(k_total)
            v_total[...] = jnp.zeros_like(v_total)
            for i in range(length // TILE):
                seen = (i + 1) * TILE
                here = pl.ds(i * TILE, TILE)
                there = pl.ds(base + i * TILE, TILE)
                q, d_att = q_ref[here, :], d_att_ref[here, :]
                k, v = k_ref[:seen, :], v_ref[:seen, :]
                scores = lax.dot_general(q, k, NT, preferred_element_type=F32) * scale
                row = lax.broadcasted_iota(jnp.int32, scores.shape, 0) + i * TILE
                column = lax.broadcasted_iota(jnp.int32, scores.shape, 1)
                scores = jnp.where(row >= column, scores, MASKED)
                grown = jnp.exp(scores - jnp.max(scores, axis=1, keepdims=True))
                prob = grown * (1.0 / jnp.sum(grown, axis=1, keepdims=True))
                prob_low = prob.astype(BF)
                self.att[there, :] = jnp.dot(prob_low, v, preferred_element_type=F32).astype(BF)
                d_prob = lax.dot_general(d_att, v, NT, preferred_element_type=F32)
                inner = jnp.sum(d_prob * prob, axis=1, keepdims=True)
                d_scores = (prob * (d_prob - inner)).astype(BF)
                d_q = jnp.dot(d_scores, k, preferred_element_type=F32) * scale
                d_q = rotate_back(d_q, self.cos[here, :], self.sin[here, :]).astype(BF)
                self.d_proj[there, :HEAD_W] = d_q
                k_total[:seen, :] += lax.dot_general(d_scores, q, TN, preferred_element_type=F32)
                v_total[:seen, :] += lax.dot_general(prob_low, d_att, TN, preferred_element_type=F32)
            for i in range(length // TILE):
                here = pl.ds(i * TILE, TILE)
                there = pl.ds(base + i * TILE, TILE)
                d_k = rotate_back(k_total[here, :] * scale, self.cos[here, :], self.sin[here, :])
                self.d_proj[there, HEAD_W : 2 * HEAD_W] = d_k.astype(BF)
                self.d_proj[there, 2 * HEAD_W :] = v_total[here, :].astype(BF)
                column_sums(self.qkv_total, self.d_proj[there, :].astype(F32))

        low, wide = pltpu.VMEM((length, HEAD_W), BF), pltpu.VMEM((length, HEAD_W), F32)
        pl.run_scoped(one, low, low, low, low, wide, wide)

    def dense_gradient(self):
        def body(g, part):
            part[...] = lax.dot_general(self.att[...], g[...], TN, preferred_element_type=F32).astype(BF)

        pipe(body, D // 512, [slim(self.tokens, 512)], [slim(HEAD_W, 512)], (self.g, self.dn_part))

    def qkv_gradient(self):
        def body(n1, part):
            part[...] = lax.dot_general(n1[...], self.d_proj[...], TN, preferred_element_type=F32).astype(BF)

        pipe(body, D // TILE, [slim(self.tokens)], [tall(3 * HEAD_W)], (self.n1, self.qk_part))

    def back_one(self):
        def body(qkv, xh, part):
            at = pl.ds(pl.multiple_of(pl.program_id(0) * TILE, TILE), TILE)
            d_n = lax.dot_general(self.d_proj[at, :], qkv[...], NT, preferred_element_type=F32)
            part[...] = (d_n * self.vec[0:1, :]).astype(BF)
            column_sums(self.bias1, d_n)
            column_sums(self.gain1, d_n * xh[...].astype(F32))

        pipe(body, self.tiles, [fixed(D, 3 * HEAD_W), tall(D)], [tall(D)], (self.qkv, self.xhat, self.s1))

    def expand(self):
        def body(n2, up, hidden, slope):
            pre = jnp.dot(n2[...], up[...], preferred_element_type=F32) + self.up_bias[...]
            value, rise = gelu_parts(pre)
            hidden[...] = value.astype(BF)
            slope[...] = rise.astype(BF)

        pipe(
            body,
            self.tiles,
            [tall(D), fixed(D, HID_W)],
            [tall(HID_W)] * 2,
            (self.n2, self.up, self.hidden, self.slope),
        )

    def down_gradient(self):
        def body(g, hidden, part):
            part[...] = lax.dot_general(g[...], hidden[...], TN, preferred_element_type=F32).astype(BF)

        pipe(
            body,
            D // TILE,
            [slim(self.tokens), fixed(self.tokens, HID_W)],
            [tall(HID_W)],
            (self.g, self.hidden, self.wt_part),
        )

    def contract_back(self):
        def body(g, wt, slope, d_pre):
            d_hidden = jnp.dot(g[...], wt[...], preferred_element_type=F32)
            low = (d_hidden * slope[...].astype(F32)).astype(BF)
            d_pre[...] = low
            column_sums(self.up_total, low.astype(F32))

        pipe(
            body,
            self.tiles,
            [tall(D), fixed(D, HID_W), tall(HID_W)],
            [tall(HID_W)],
            (self.g, self.wt, self.slope, self.d_pre),
        )

    def up_gradient(self):
        def body(n2, d_pre, part):
            part[...] = lax.dot_general(n2[...], d_pre[...], TN, preferred_element_type=F32).astype(BF)

        pipe(
            body,
            D // TILE,
            [slim(self.tokens), fixed(self.tokens, HID_W)],
            [tall(HID_W)],
            (self.n2, self.d_pre, self.up_part),
        )

    def back_two(self):
        def body(d_pre, up, xh, s1, part):
            d_n = lax.dot_general(d_pre[...], up[...], NT, preferred_element_type=F32)
            part[...] = (s1[...].astype(F32) + d_n * self.vec[2:3, :]).astype(BF)
            column_sums(self.bias2, d_n)
            column_sums(self.gain2, d_n * xh[...].astype(F32))

        pipe(
            body,
            self.tiles,
            [tall(HID_W), fixed(D, HID_W), tall(D), tall(D)],
            [tall(D)],
            (self.d_pre, self.up, self.xhat, self.s1, self.tok_parts),
        )

    def output(self):
        def body(hidden, dense, wt, part):
            at = pl.ds(pl.multiple_of(pl.program_id(0) * TILE, TILE), TILE)
            total = jnp.dot(self.att[at, :], dense[...], preferred_element_type=F32)
            total = total + lax.dot_general(hidden[...], wt[...], NT, preferred_element_type=F32)
            part[...] = total.astype(BF)

        pipe(
            body,
            self.tiles,
            [tall(HID_W), fixed(HEAD_W, D), fixed(D, HID_W)],
            [tall(D)],
            (self.hidden, self.dense, self.wt, self.out_parts),
        )


def any_spec(count):
    return [pl.BlockSpec(memory_space=pl.ANY)] * count


def slots_needed(n_zero):
    return 16 * n_zero + 100


INPUTS = ("x_own", "g_own", "dn_low", "qk_low", "up_low", "wt_low", "vec", "qkv_bias", "up_bias", "cos", "sin")
RESULTS = ("out_sum", "tok_sum", "dn_home", "qk_home", "up_home", "wt_home")
TOTALS = (("gain1", D), ("bias1", D), ("gain2", D), ("bias2", D), ("qkv_total", 3 * HEAD_W), ("up_total", HID_W))
WIDTHS = (HEAD_W, 3 * HEAD_W, HID_W, HID_W)


def buffers(tokens):
    square = ("x", "g", "n1", "n2", "xhat", "s1", "tok_parts", "out_parts")
    shapes = {name: (tokens, D) for name in square}
    shapes.update({name: (tokens, HID_W) for name in ("hidden", "slope", "d_pre")})
    shapes.update(dense=(HEAD_W, D), dn_part=(HEAD_W, D), dn_all=(D, HEAD_W), dn_cols=(D, HEAD_W))
    shapes.update(qkv=(D, 3 * HEAD_W), qk_part=(D, 3 * HEAD_W))
    shapes.update({name: (D, HID_W) for name in ("up", "wt", "up_part", "wt_part")})
    return shapes


def layer_body(n_zero, rows, tokens, *refs):
    names = INPUTS + RESULTS + tuple(name for name, _ in TOTALS) + tuple(buffers(tokens))
    names += ("att", "d_proj", "send_sems", "recv_sems", "local_sems", "own", "total")
    held = dict(zip(names, refs))
    scratch = list(refs[len(names) :])
    take = lambda count: [scratch.pop(0) for _ in range(count)]
    layer = Layer(held)
    place = Place(n_zero)
    wire = Wire(layer.send_sems, layer.recv_sems)
    local = lambda index: layer.local_sems.at[index]
    block = rows * N_SEQ
    chunk = lambda c: pl.ds(pl.multiple_of(c * HEAD_W, HEAD_W), HEAD_W)

    sources = (layer.dn_low, layer.qk_low, layer.up_low, layer.wt_low)
    wholes = (layer.dn_all, layer.qkv, layer.up, layer.wt)
    exchanges = [SeqExchange(wire, place, low, whole, rows) for low, whole in zip(sources, wholes)]
    dn, qk, up, wt = [LineGather(wire, place, whole, block) for whole in wholes]
    x = PlaneGather(wire, place, layer.x_own, layer.x)
    g = PlaneGather(wire, place, layer.g_own, layer.g)
    dense_in = DenseExchange(
        wire, place, lambda c: layer.dn_all.at[chunk(c)], lambda c: layer.dense.at[:, chunk(c)]
    )
    dense_out = DenseExchange(
        wire, place, lambda c: layer.dn_part.at[:, chunk(c)], lambda c: layer.dn_cols.at[chunk(c)]
    )
    planes = []
    for k, parts in enumerate((layer.out_parts, layer.tok_parts)):
        mate, far, across, turned = take(4)
        planes.append(
            PlaneScatter(wire, place, parts, mate, far, across, turned, layer.total, layer.own, local(k))
        )
    out, tok = planes
    sums, homes = [], []
    parts = (layer.dn_cols, layer.qk_part, layer.up_part, layer.wt_part)
    results = (layer.dn_home, layer.qk_home, layer.up_home, layer.wt_home)
    for k, width in enumerate(WIDTHS):
        ring, total = take(2)
        own = take(1)[0]
        sums.append(LineScatter(wire, place, parts[k], ring, total, own, block, local(2 + k)))
        homes.append(Home(wire, place, total, results[k], rows))
    dn_sum, qk_sum, up_sum, wt_sum = sums

    def ahead(line, step):
        line.take(step)
        if step + 1 < n_zero:
            line.pass_on(step + 1)

    def rest(line, start):
        for step in range(start, n_zero):
            ahead(line, step)

    def finish(k):
        sums[k].last()
        homes[k].start(local(6 + k))

    def store(scatter, result):
        scatter.last()
        copy = pltpu.make_async_copy(scatter.total, result, scatter.sem)
        copy.start()
        copy.wait()

    place.barrier()
    layer.clear()
    exchanges[0].start(local(6))
    exchanges[1].start(local(7))
    x.start(local(10))
    g.start(local(11))
    exchanges[2].start(local(8))
    exchanges[3].start(local(9))
    exchanges[0].wait()
    dn.pass_on(1)
    exchanges[1].wait()
    qk.pass_on(1)
    rest(dn, 1)
    dense_in.start(local(6))
    x.turn()
    g.turn()
    ahead(qk, 1)
    exchanges[2].wait()
    up.pass_on(1)
    x.turn_again()
    g.turn_again()
    x.wait()
    layer.normalise(0, 2)
    ahead(qk, 2) if n_zero > 3 else None
    layer.normalise(1, 2)
    rest(qk, min(3, n_zero - 1))
    exchanges[3].wait()
    g.wait()
    dense_in.wait()
    layer.attend(0)
    ahead(up, 1)
    wt.pass_on(1)
    layer.attend(1)
    layer.dense_gradient()
    dense_out.start(local(7))
    ahead(up, 2) if n_zero > 3 else None
    layer.qkv_gradient()
    qk_sum.advance()
    layer.back_one()
    rest(up, min(3, n_zero - 1))
    ahead(wt, 1)
    dense_out.wait()
    dn_sum.advance()
    layer.expand()
    ahead(wt, 2) if n_zero > 3 else None
    qk_sum.advance()
    dn_sum.advance()
    layer.down_gradient()
    wt_sum.advance()
    rest(wt, min(3, n_zero - 1))
    qk_sum.advance()
    dn_sum.advance()
    layer.contract_back()
    wt_sum.advance()
    finish(0)
    finish(1)
    layer.up_gradient()
    up_sum.advance()
    wt_sum.advance()
    layer.output()
    out.start()
    up_sum.advance()
    finish(3)
    layer.back_two()
    tok.start()
    out.turn()
    up_sum.advance()
    tok.turn()
    out.turn_again()
    finish(2)
    tok.turn_again()
    store(out, layer.out_sum)
    store(tok, layer.tok_sum)
    for home in homes:
        home.wait()
    wire.finish()


def layer_call(n_zero, rows, tokens, *operands):
    local = tokens // PARTS
    block = rows * N_SEQ
    slots = slots_needed(n_zero)
    vmem = lambda *dims: pltpu.VMEM(dims, BF)
    scratch = [
        vmem(tokens, HEAD_W),
        vmem(tokens, 3 * HEAD_W),
        pltpu.SemaphoreType.DMA((slots,)),
        pltpu.SemaphoreType.DMA((slots,)),
        pltpu.SemaphoreType.DMA((12,)),
        vmem(local, D),
        pltpu.VMEM((local, D), F32),
    ]
    for _ in range(2):
        scratch += [vmem(2, 2, local, D), vmem(local, D), vmem(local, D), vmem(local, D)]
    for width in WIDTHS:
        scratch += [vmem(n_zero + 1, block, width), vmem(block, width), vmem(block, width)]
    homes = [jax.ShapeDtypeStruct((N_DP, N_SEQ, rows, width), BF) for width in WIDTHS]
    anywhere = pl.BlockSpec(memory_space=pl.ANY)
    vector = pl.BlockSpec(memory_space=pltpu.VMEM)
    held = buffers(tokens)
    return pl.pallas_call(
        functools.partial(layer_body, n_zero, rows, tokens),
        in_specs=[anywhere] * 6 + [vector] * 5,
        out_specs=[anywhere] * len(RESULTS) + [vector] * len(TOTALS) + [anywhere] * len(held),
        out_shape=[jax.ShapeDtypeStruct((local, D), F32)] * 2
        + homes
        + [jax.ShapeDtypeStruct((8, width), F32) for _, width in TOTALS]
        + [jax.ShapeDtypeStruct(shape, BF) for shape in held.values()],
        scratch_shapes=scratch,
        compiler_params=pltpu.CompilerParams(
            collective_id=0, has_side_effects=True, vmem_limit_bytes=62 * 1024 * 1024
        ),
        name="layer",
    )(*operands)


def adam_body(decay, flipped, home, param, first, second, new, first_new, second_new, grad_out):
    gradient = home[0, 0].astype(F32)
    if flipped:
        gradient = gradient.T
    updated = adam_step(param[...], gradient, first[...], second[...], decay)
    new[...], first_new[...], second_new[...] = updated
    grad_out[...] = gradient


def adam(home, pieces, param, first, second, flipped=False):
    rows, width = home.shape[2], home.shape[3] // pieces
    if flipped:
        block = pl.BlockSpec((width, rows), lambda c, t: (t * PARTS + c, 0))
    else:
        block = pl.BlockSpec((rows, width), lambda c, t: (0, t * PARTS + c))
    return pl.pallas_call(
        functools.partial(adam_body, WEIGHT_DECAY, flipped),
        grid=(PARTS, pieces),
        in_specs=[
            pl.BlockSpec((1, 1, rows, width), lambda c, t: (c // N_SEQ, c % N_SEQ, 0, t)),
            block,
            block,
            block,
        ],
        out_specs=[block] * 4,
        out_shape=[jax.ShapeDtypeStruct(param.shape, F32)] * 4,
        compiler_params=pltpu.CompilerParams(vmem_limit_bytes=48 * 1024 * 1024),
        name="adam",
    )(home, param, first, second)


def make_body(sizes):
    n_zero = sizes["zero"]
    everywhere = ("dp", "zero", "seq")

    def body(
        inputs,
        out_grad,
        vectors,
        qkv_weight,
        dense_weight,
        up_weight,
        down_weight,
        vectors_first,
        qkv_first,
        dense_first,
        up_first,
        down_first,
        vectors_second,
        qkv_second,
        dense_second,
        up_second,
        down_second,
    ):
        dp_i, zero_i, seq_i = (lax.axis_index(axis) for axis in everywhere)
        part_i = dp_i * N_SEQ + seq_i
        seqs_here, local_len = inputs.shape[0], inputs.shape[1]
        token_rows = seqs_here * local_len
        rows = qkv_weight.shape[0]
        pick = lambda value, index, axis: lax.dynamic_index_in_dim(value, index, axis, keepdims=False)

        vec_all = lax.all_gather(vectors.astype(BF), ("zero", "seq"), axis=0, tiled=True).astype(F32)
        ln1_gain, ln1_bias = vec_all[:D], vec_all[D : 2 * D]
        qkv_bias = vec_all[2 * D : 5 * D].reshape(3, PARTS, HEAD_W)
        dense_bias = vec_all[5 * D : 6 * D]
        ln2_gain, ln2_bias = vec_all[6 * D : 7 * D], vec_all[7 * D : 8 * D]
        up_bias = vec_all[8 * D : 8 * D + FF].reshape(PARTS, HID_W)
        down_bias = vec_all[8 * D + FF :]

        def columns(value, width):
            wide = value.shape[1] // N_DP
            half = lax.dynamic_slice_in_dim(value, dp_i * wide, wide, 1).astype(BF)
            return half.reshape(rows, N_SEQ, width).transpose(1, 0, 2)

        qk_low = jnp.concatenate(
            [columns(qkv_weight[:, t * D : (t + 1) * D], HEAD_W) for t in range(3)], axis=2
        )
        dn_low = columns(dense_weight, HEAD_W)
        up_low = columns(up_weight, HID_W)
        wt_low = lax.dynamic_slice_in_dim(down_weight, dp_i * (FF // N_DP), FF // N_DP, 0).astype(BF)
        wt_low = wt_low.reshape(N_SEQ, HID_W, rows).transpose(0, 2, 1)

        tokens_low = inputs.reshape(token_rows, D)
        grad_low = out_grad.reshape(token_rows, D)
        tokens = N_DP * N_SEQ * token_rows
        cosine, sine = rotary_tables(jnp.arange(tokens // N_DP).astype(F32))
        half = ROT // 2
        cosine = jnp.concatenate([cosine, jnp.ones((tokens // N_DP, 128 - ROT), F32)], axis=1)
        sine = jnp.concatenate(
            [-sine[:, :half], sine[:, half:], jnp.zeros((tokens // N_DP, 128 - ROT), F32)], axis=1
        )
        results = layer_call(
            n_zero,
            rows,
            tokens,
            tokens_low,
            grad_low,
            dn_low,
            qk_low,
            up_low,
            wt_low,
            jnp.stack([ln1_gain, ln1_bias, ln2_gain, ln2_bias]),
            pick(qkv_bias, part_i, 1).reshape(1, 3 * HEAD_W),
            pick(up_bias, part_i, 0).reshape(1, HID_W),
            cosine,
            sine,
        )
        out_sum, d_xhat, dn_home, qk_home, up_home, wt_home = results[: len(RESULTS)]
        totals = [jnp.sum(total, axis=0) for total in results[len(RESULTS) : len(RESULTS) + len(TOTALS)]]
        d_gain_one, d_bias_one, d_gain_two, d_bias_two, d_qkv_bias, d_up_bias = totals

        def statistics(values):
            average = jnp.mean(values, axis=-1, keepdims=True)
            centred = values - average
            spread = jnp.mean(centred * centred, axis=-1, keepdims=True)
            return centred, lax.rsqrt(spread + NORM_EPSILON)

        tokens_wide = tokens_low.astype(F32)
        grad_wide = grad_low.astype(F32)
        outputs = (tokens_wide + out_sum + dense_bias + down_bias).astype(BF).reshape(inputs.shape)
        centred_own, rate_own = statistics(tokens_wide)
        xhat_own = centred_own * rate_own
        d_tokens = rate_own * (
            d_xhat
            - jnp.mean(d_xhat, axis=-1, keepdims=True)
            - xhat_own * jnp.mean(d_xhat * xhat_own, axis=-1, keepdims=True)
        )
        input_grad = (grad_wide + d_tokens).astype(BF).reshape(inputs.shape)

        d_out_bias = jnp.sum(grad_wide, axis=0)
        place_in = lambda value, count: lax.dynamic_update_index_in_dim(
            jnp.zeros((value.shape[0], count, value.shape[1]), F32), value, part_i, 1
        ).reshape(-1)
        vector_local = jnp.concatenate(
            [
                d_gain_one,
                d_bias_one,
                place_in(d_qkv_bias.reshape(3, HEAD_W), PARTS),
                d_out_bias,
                d_gain_two,
                d_bias_two,
                place_in(d_up_bias.reshape(1, HID_W), PARTS),
                d_out_bias,
            ]
        )
        vector_sum = lax.psum(vector_local, everywhere)
        vectors_grad = lax.dynamic_slice_in_dim(
            vector_sum, (zero_i * N_SEQ + seq_i) * vectors.shape[0], vectors.shape[0], 0
        )

        vec_upd = adam_step(vectors, vectors_grad, vectors_first, vectors_second, 0.0) + (vectors_grad,)
        qkv_upd = adam(qk_home, 3, qkv_weight, qkv_first, qkv_second)
        dense_upd = adam(dn_home, 1, dense_weight, dense_first, dense_second)
        up_upd = adam(up_home, 1, up_weight, up_first, up_second)
        down_upd = adam(wt_home, 1, down_weight, down_first, down_second, flipped=True)
        updates = (vec_upd, qkv_upd, dense_upd, up_upd, down_upd)
        picked = lambda k: tuple(update[k] for update in updates)
        return (outputs, input_grad) + picked(3) + picked(0) + picked(1) + picked(2)

    return body


def solution(mesh):
    wide = P(("dp", "zero"), "seq", None)
    vector = P(("zero", "seq"))
    rows = P(("zero", "seq"), None)
    columns = P(None, ("zero", "seq"))
    state = (vector, rows, rows, rows, columns)
    return jax.shard_map(
        make_body(dict(mesh.shape)),
        mesh=mesh,
        in_specs=(wide, wide) + state * 3,
        out_specs=(wide, wide) + state * 4,
        check_vma=False,
    )
```

```python
import functools
import math

import jax
import jax.numpy as jnp
import numpy as np
from jax import lax
from jax.experimental import pallas as pl
from jax.experimental.pallas import tpu as pltpu
from jax.sharding import PartitionSpec as P

D = 2048
HEADS = 8
HEAD_DIM = 256
FF = 8192
ROT = 64
ADAM_STEP = 4

BETA_ONE = 0.9
BETA_TWO = 0.95
LEARN_RATE = 0.5
EPSILON = 1e-08
WEIGHT_DECAY = 0.1
NORM_EPSILON = 1e-05
MASKED = -1e30
N_DP = 2
N_SEQ = 4
PARTS = N_DP * N_SEQ
HEAD_W = D // PARTS
HID_W = FF // PARTS
BF = jnp.bfloat16
F32 = jnp.float32
NT = (((1,), (1,)), ((), ()))
TN = (((0,), (0,)), ((), ()))


def adam_step(parameter, gradient, first_moment, second, decay_rate):
    first_new = BETA_ONE * first_moment + (1.0 - BETA_ONE) * gradient
    second_new = BETA_TWO * second + (1.0 - BETA_TWO) * gradient * gradient
    first_hat = first_new / (1.0 - BETA_ONE**ADAM_STEP)
    second_hat = second_new / (1.0 - BETA_TWO**ADAM_STEP)
    param_new = parameter - LEARN_RATE * (
        first_hat / (jnp.sqrt(second_hat) + EPSILON) + decay_rate * parameter
    )
    return (param_new, first_new, second_new)


class Wire:
    def __init__(self, send_sems, recv_sems):
        self.send_sems, self.recv_sems, self.used = send_sems, recv_sems, 0
        self.sent = []

    def slot(self):
        self.used += 1
        return self.used - 1

    def copy(self, slot, source, target, device):
        return pltpu.make_async_remote_copy(
            src_ref=source,
            dst_ref=target,
            send_sem=self.send_sems.at[slot],
            recv_sem=self.recv_sems.at[slot],
            device_id=device,
            device_id_type=pl.DeviceIdType.MESH,
        )

    def send(self, slot, source, target, device, when=None):
        copy = self.copy(slot, source, target, device)
        guarded(when, copy.start)
        self.sent.append((copy, when))

    def receive(self, slot, target, device, when=None):
        copy = self.copy(slot, target, target, device)
        guarded(when, copy.wait_recv)

    def finish(self):
        for copy, when in self.sent:
            guarded(when, copy.wait_send)
        self.sent = []


def guarded(when, action):
    if when is None:
        action()
    else:
        pl.when(when)(action)


class Place:
    def __init__(self, n_zero):
        self.n = n_zero
        self.dp, self.z, self.s = (lax.axis_index(a) for a in ("dp", "zero", "seq"))
        flip = lambda value, bit: jnp.bitwise_xor(value, bit)
        self.dp_far, self.s_far, self.s_core = 1 - self.dp, flip(self.s, 2), flip(self.s, 1)
        self.s_both = flip(self.s, 3)
        self.across = {"dp": self.dp_far}
        self.far = {"seq": self.s_far}
        self.core = {"seq": self.s_core}
        self.above, self.below = {"zero": self.z + 1}, {"zero": self.z - 1}
        self.part = self.dp * N_SEQ + self.s

    def others(self):
        for step in range(1, N_DP * N_SEQ):
            at = lax.rem(self.part + step, N_DP * N_SEQ)
            dp, s = lax.div(at, N_SEQ), lax.rem(at, N_SEQ)
            yield step, dp, s, {"dp": dp, "seq": s}

    def barrier(self):
        gate = pltpu.get_barrier_semaphore()
        signal = lambda device: pl.semaphore_signal(
            gate, inc=1, device_id=device, device_id_type=pl.DeviceIdType.MESH
        )
        for _, _, _, device in self.others():
            signal(device)
        pl.when(self.z < self.n - 1)(lambda: signal(self.above))
        pl.when(self.z > 0)(lambda: signal(self.below))
        ends = (self.z < self.n - 1).astype(jnp.int32) + (self.z > 0).astype(jnp.int32)
        pl.semaphore_wait(gate, N_DP * N_SEQ - 1 + ends)


class LineGather:
    def __init__(self, wire, place, whole, rows):
        self.wire, self.place, self.whole, self.rows = wire, place, whole, rows
        self.ups = [wire.slot() for _ in range(place.n - 1)]
        self.downs = [wire.slot() for _ in range(place.n - 1)]

    def block(self, index):
        return self.whole.at[pl.ds(pl.multiple_of(index * self.rows, self.rows), self.rows)]

    def send_up(self, step, block, when):
        self.wire.send(self.ups[step - 1], block, block, self.place.above, when)

    def send_down(self, step, block, when):
        self.wire.send(self.downs[step - 1], block, block, self.place.below, when)

    def own_from_ends(self):
        p = self.place
        self.send_up(1, self.block(p.z), p.z == 0)
        self.send_down(1, self.block(p.z), p.z == p.n - 1)

    def own_from_middle(self):
        p = self.place
        middle = (p.z > 0) & (p.z < p.n - 1)
        self.send_up(1, self.block(p.z), middle)
        self.send_down(1, self.block(p.z), middle)

    def ahead(self, step):
        p = self.place
        up, down = self.block(jnp.maximum(p.z - step, 0)), self.block(jnp.minimum(p.z + step, p.n - 1))
        self.wire.receive(self.ups[step - 1], up, p.below, p.z >= step)
        if step + 1 < p.n:
            self.send_up(step + 1, up, (p.z < p.n - 1) & (p.z >= step))
        self.wire.receive(self.downs[step - 1], down, p.above, p.z + step < p.n)
        if step + 1 < p.n:
            self.send_down(step + 1, down, (p.z > 0) & (p.z + step < p.n))


class SeqExchange:
    def __init__(self, wire, place, send, whole, rows):
        self.wire, self.place, self.out, self.whole, self.rows = wire, place, send, whole, rows
        self.slots = [wire.slot() for _ in range(1, N_SEQ)]

    def target(self, s):
        row = (self.place.z * N_SEQ + s) * self.rows
        return self.whole.at[pl.ds(pl.multiple_of(row, self.rows), self.rows)]

    def start(self, local_sem):
        p = self.place
        for step in range(1, N_SEQ):
            to = lax.rem(p.s + step, N_SEQ)
            self.wire.send(self.slots[step - 1], self.out.at[to], self.target(p.s), {"seq": to})
        own = pltpu.make_async_copy(self.out.at[p.s], self.target(p.s), local_sem)
        own.start()
        self.own = own

    def wait(self):
        p = self.place
        for step in range(1, N_SEQ):
            source = lax.rem(p.s - step + N_SEQ, N_SEQ)
            self.wire.receive(self.slots[step - 1], self.target(source), {"seq": source})
        self.own.wait()


class PlaneGather:
    def __init__(self, wire, place, block, whole):
        self.wire, self.place, self.own, self.whole = wire, place, block, whole
        self.slots = {name: wire.slot() for name in ("far", "across", "both0", "both1", "c0", "c1", "c2", "c3")}
        self.rows = block.shape[0]
        self.half = self.rows // 2

    def at(self, dp, s):
        row = (dp * N_SEQ + s) * self.rows
        return self.whole.at[pl.ds(pl.multiple_of(row, self.rows), self.rows)]

    def start(self, local_sem):
        p, w, slots = self.place, self.wire, self.slots
        mine = self.at(p.dp, p.s)
        w.send(slots["far"], self.own, mine, p.far)
        w.send(slots["across"], self.own, mine, p.across)
        w.send(slots["c0"], self.own, mine, p.core)
        self.copied = pltpu.make_async_copy(self.own, mine, local_sem)
        self.copied.start()

    def turn(self):
        p, w, slots, h = self.place, self.wire, self.slots, self.half
        far, across = self.at(p.dp, p.s_far), self.at(p.dp_far, p.s)
        w.receive(slots["far"], far, p.far)
        w.send(slots["both0"], far.at[pl.ds(0, h)], far.at[pl.ds(0, h)], p.across)
        w.send(slots["c1"], far, far, p.core)
        w.receive(slots["across"], across, p.across)
        w.send(slots["both1"], across.at[pl.ds(h, h)], across.at[pl.ds(h, h)], p.far)
        w.send(slots["c2"], across, across, p.core)

    def turn_again(self):
        p, w, slots, h = self.place, self.wire, self.slots, self.half
        both = self.at(p.dp_far, p.s_far)
        w.receive(slots["both0"], both.at[pl.ds(0, h)], p.across)
        w.receive(slots["both1"], both.at[pl.ds(h, h)], p.far)
        w.send(slots["c3"], both, both, p.core)

    def wait(self):
        p, w, slots = self.place, self.wire, self.slots
        w.receive(slots["c0"], self.at(p.dp, p.s_core), p.core)
        w.receive(slots["c1"], self.at(p.dp, p.s_both), p.core)
        w.receive(slots["c2"], self.at(p.dp_far, p.s_core), p.core)
        w.receive(slots["c3"], self.at(p.dp_far, p.s_both), p.core)
        self.copied.wait()


def add_rows(target, *sources):
    rows = target.shape[0]
    tile = 32 if rows % 32 == 0 else 16

    def one(i, carry):
        at = pl.ds(pl.multiple_of(i * tile, tile), tile)
        total = sources[0][at, :].astype(F32)
        for source in sources[1:]:
            total = total + source[at, :].astype(F32)
        target[at, :] = total.astype(target.dtype)
        return carry

    lax.fori_loop(0, rows // tile, one, 0)


class LineScatter:
    def __init__(self, wire, place, parts, held, total, own, rows, sem):
        self.wire, self.place, self.parts, self.rows = wire, place, parts, rows
        self.held, self.total, self.own, self.sem = held, total, own, sem
        self.launched, self.advanced = 0, 1
        self.up_slots = [wire.slot() for _ in range(place.n)]
        self.down_slots = [wire.slot() for _ in range(place.n)]

    def part(self, j):
        return self.parts.at[pl.ds(pl.multiple_of(j * self.rows, self.rows), self.rows)]

    def fetch(self, j, target):
        return pltpu.make_async_copy(self.part(j), target, self.sem)

    def launch(self, k):
        p = self.place
        top = p.n - 1
        up, down = top - k, k
        self.wire.send(
            self.up_slots[up], self.part(up), self.held.at[up + 1], p.above, p.z == 0
        )
        self.wire.send(
            self.down_slots[down], self.part(down), self.held.at[down], p.below, p.z == top
        )
        self.launched = k + 1

    def advance(self, k):
        p = self.place
        top = p.n - 1
        up = jnp.minimum(top - k + p.z, top)
        self.hop(up, up + 1, self.up_slots[0] + up, p.above, p.below, (p.z > 0) & (p.z <= k))
        down = jnp.maximum(k - top + p.z, 0)
        self.hop(down, down, self.down_slots[0] + down, p.below, p.above, (p.z < top) & (top - p.z <= k))
        self.advanced = k + 1

    def hop(self, j, index, slot, onto, source, active):
        held = self.held.at[index]

        def go():
            copy = self.fetch(j, self.own)
            copy.start()
            self.wire.receive(slot, held, source)
            copy.wait()
            add_rows(held, held, self.own)

        pl.when(active)(go)
        self.wire.send(slot, held, held, onto, active)

    def last(self):
        p = self.place
        for k in range(self.launched, p.n - 1):
            self.launch(k)
        for k in range(self.advanced, p.n - 1):
            self.advance(k)
        copy = self.fetch(p.z, self.own)
        copy.start()
        copy.wait()
        up, down = self.held.at[p.z + 1], self.held.at[p.z]

        @pl.when(p.z == 0)
        def _():
            self.arrive(down, self.down_slots, p.above)
            add_rows(self.total, self.own, down)

        @pl.when(p.z == p.n - 1)
        def _():
            self.arrive(up, self.up_slots, p.below)
            add_rows(self.total, self.own, up)

        @pl.when((p.z > 0) & (p.z < p.n - 1))
        def _():
            self.arrive(up, self.up_slots, p.below)
            self.arrive(down, self.down_slots, p.above)
            add_rows(self.total, self.own, up, down)

    def arrive(self, held, slots, source):
        self.wire.receive(slots[0] + self.place.z, held, source)


class Home:
    def __init__(self, wire, place, total, home, rows):
        self.wire, self.place, self.total, self.home, self.rows = wire, place, total, home, rows
        self.slots = [wire.slot() for _ in range(1, N_DP * N_SEQ)]

    def start(self, local_sem):
        p = self.place
        piece = lambda s: self.total.at[pl.ds(pl.multiple_of(s * self.rows, self.rows), self.rows)]
        for step, dp, s, device in p.others():
            self.wire.send(self.slots[step - 1], piece(s), self.home.at[p.dp, p.s], device)
        self.copied = pltpu.make_async_copy(piece(p.s), self.home.at[p.dp, p.s], local_sem)
        self.copied.start()

    def wait(self):
        p = self.place
        parts = N_DP * N_SEQ
        for step in range(1, parts):
            at = lax.rem(p.part - step + parts, parts)
            dp, s = lax.div(at, N_SEQ), lax.rem(at, N_SEQ)
            self.wire.receive(self.slots[step - 1], self.home.at[dp, s], {"dp": dp, "seq": s})
        self.copied.wait()


class DenseExchange:
    def __init__(self, wire, place, source, target):
        self.wire, self.place, self.source, self.target = wire, place, source, target
        self.slots = [wire.slot() for _ in range(1, N_DP * N_SEQ)]

    def start(self, local_sem):
        p = self.place
        for step, dp, s, device in p.others():
            self.wire.send(self.slots[step - 1], self.source(dp * N_SEQ + s), self.target(p.part), device)
        self.copied = pltpu.make_async_copy(self.source(p.part), self.target(p.part), local_sem)
        self.copied.start()

    def wait(self):
        p = self.place
        parts = N_DP * N_SEQ
        for step in range(1, parts):
            at = lax.rem(p.part - step + parts, parts)
            device = {"dp": lax.div(at, N_SEQ), "seq": lax.rem(at, N_SEQ)}
            self.wire.receive(self.slots[step - 1], self.target(at), device)
        self.copied.wait()


class PlaneScatter:
    def __init__(self, wire, place, parts, mate, from_far, from_across, turned, total, own, sem):
        self.wire, self.place, self.parts, self.mate, self.sums = wire, place, parts, mate, mate
        self.from_far, self.from_across, self.turned = from_far, from_across, turned
        self.total, self.own, self.sem = total, own, sem
        self.rows = total.shape[0]
        self.half = self.rows // 2
        self.core_slots = [[wire.slot() for _ in range(2)] for _ in range(2)]
        names = ("turn_across", "turn_far", "far0", "far1", "across0", "across1")
        self.slots = {name: wire.slot() for name in names}

    def part(self, dp, s):
        row = (dp * N_SEQ + s) * self.rows
        return self.parts.at[pl.ds(pl.multiple_of(row, self.rows), self.rows)]

    def start(self):
        p = self.place
        core = lax.rem(p.s_core, 2)
        for dp in range(2):
            for y in range(2):
                self.wire.send(
                    self.core_slots[dp][y], self.part(dp, 2 * y + core), self.mate.at[dp, y], p.core
                )

    def combine(self, dp, y):
        p = self.place
        core = lax.rem(p.s, 2)
        for d in range(2):
            for v in range(2):

                @pl.when((dp == d) & (y == v))
                def _(d=d, v=v):
                    copy = pltpu.make_async_copy(self.part(d, 2 * v + core), self.own, self.sem)
                    copy.start()
                    self.wire.receive(self.core_slots[d][v], self.mate.at[d, v], p.core)
                    copy.wait()
                    add_rows(self.sums.at[d, v], self.own, self.mate.at[d, v])

    def turn(self):
        p, w, h, slots = self.place, self.wire, self.half, self.slots
        y = lax.div(p.s, 2)
        y_far = 1 - y
        low, high = pl.ds(0, h), pl.ds(h, h)
        self.combine(p.dp_far, y_far)
        both = self.sums.at[p.dp_far, y_far]
        w.send(slots["turn_across"], both.at[low], self.turned.at[low], p.across)
        w.send(slots["turn_far"], both.at[high], self.turned.at[high], p.far)
        self.combine(p.dp, y_far)
        far = self.sums.at[p.dp, y_far]
        w.send(slots["far1"], far.at[high], self.from_far.at[high], p.far)
        self.combine(p.dp_far, y)
        across = self.sums.at[p.dp_far, y]
        w.send(slots["across0"], across.at[low], self.from_across.at[low], p.across)
        self.combine(p.dp, y)

    def turn_again(self):
        p, w, h, slots = self.place, self.wire, self.half, self.slots
        y = lax.div(p.s, 2)
        low, high = pl.ds(0, h), pl.ds(h, h)
        far, across = self.sums.at[p.dp, 1 - y], self.sums.at[p.dp_far, y]
        w.receive(slots["turn_across"], self.turned.at[low], p.across)
        add_rows(far.at[low], far.at[low], self.turned.at[low])
        w.send(slots["far0"], far.at[low], self.from_far.at[low], p.far)
        w.receive(slots["turn_far"], self.turned.at[high], p.far)
        add_rows(across.at[high], across.at[high], self.turned.at[high])
        w.send(slots["across1"], across.at[high], self.from_across.at[high], p.across)

    def last(self):
        p, w, h, slots = self.place, self.wire, self.half, self.slots
        low, high = pl.ds(0, h), pl.ds(h, h)
        w.receive(slots["far1"], self.from_far.at[high], p.far)
        w.receive(slots["far0"], self.from_far.at[low], p.far)
        w.receive(slots["across0"], self.from_across.at[low], p.across)
        w.receive(slots["across1"], self.from_across.at[high], p.across)
        add_rows(self.total, self.sums.at[p.dp, lax.div(p.s, 2)], self.from_far, self.from_across)


def gelu_parts(values):
    phi_wide = 0.5 * (1.0 + lax.erf(values * (1.0 / math.sqrt(2.0))))
    density = jnp.exp(-0.5 * values * values) * (1.0 / math.sqrt(2.0 * math.pi))
    return values * phi_wide, phi_wide + values * density


TILE = 256


def pipe(body, grid, ins, outs, refs):
    pltpu.emit_pipeline(
        body, grid=(grid,), in_specs=[spec for spec in ins], out_specs=[spec for spec in outs]
    )(*refs)


def tall(width, tile=TILE):
    return pl.BlockSpec((tile, width), lambda i: (i, 0))


def slim(height, tile=TILE):
    return pl.BlockSpec((height, tile), lambda i: (0, i))


def fixed(height, width):
    return pl.BlockSpec((height, width), lambda i: (0, 0), pipeline_mode=pl.Buffered(1))


def column_sums(total, values):
    rows, width = values.shape
    total[...] += jnp.sum(values.reshape(rows // 8, 8, width), axis=0)


def rotate(block, cosine, sine):
    half = ROT // 2
    first = block[:, :128]
    rolled = jnp.concatenate([first[:, half:ROT], first[:, :half], first[:, ROT:]], axis=1)
    return jnp.concatenate([first * cosine + rolled * sine, block[:, 128:]], axis=1)


def rotate_back(block, cosine, sine):
    half = ROT // 2
    first = block[:, :128]
    scaled = first * sine
    rolled = jnp.concatenate([scaled[:, half:ROT], scaled[:, :half], scaled[:, ROT:]], axis=1)
    return jnp.concatenate([first * cosine + rolled, block[:, 128:]], axis=1)


class Layer:
    def __init__(self, refs):
        self.__dict__.update(refs)
        self.tokens = self.x.shape[0]
        self.length = self.tokens // N_DP
        self.tiles = self.tokens // TILE

    def clear(self):
        for total in (self.gain1, self.bias1, self.gain2, self.bias2, self.qkv_total, self.up_total):
            total[...] = jnp.zeros_like(total)

    def normalise(self, part, of):
        count = self.tokens // of
        rows = pl.ds(part * count, count)

        def body(x, n1, n2, xh):
            def some(i, carry):
                at = pl.ds(pl.multiple_of(i * 32, 32), 32)
                values = x[at, :].astype(F32)
                centred = values - jnp.mean(values, axis=1, keepdims=True)
                spread = jnp.mean(centred * centred, axis=1, keepdims=True)
                xhat = centred * lax.rsqrt(spread + NORM_EPSILON)
                xh[at, :] = xhat.astype(BF)
                n1[at, :] = (xhat * self.vec[0:1, :] + self.vec[1:2, :]).astype(BF)
                n2[at, :] = (xhat * self.vec[2:3, :] + self.vec[3:4, :]).astype(BF)
                return carry

            lax.fori_loop(0, TILE // 32, some, 0, unroll=4)

        pipe(
            body,
            count // TILE,
            [tall(D)],
            [tall(D)] * 3,
            [ref.at[rows] for ref in (self.x, self.n1, self.n2, self.xhat)],
        )

    def attend(self, seq):
        scale = 1.0 / math.sqrt(HEAD_DIM)
        length = self.length

        def project(q_refs, n1, qkv, g, dense):
            at = pl.ds(pl.multiple_of(pl.program_id(0) * TILE, TILE), TILE)
            cosine, sine = self.cos[at, :], self.sin[at, :]
            wide = jnp.dot(n1[...], qkv[...], preferred_element_type=F32) + self.qkv_bias[...]
            q_refs[0][at, :] = rotate(wide[:, :HEAD_W], cosine, sine).astype(BF)
            q_refs[1][at, :] = rotate(wide[:, HEAD_W : 2 * HEAD_W], cosine, sine).astype(BF)
            q_refs[2][at, :] = wide[:, 2 * HEAD_W :].astype(BF)
            q_refs[3][at, :] = lax.dot_general(g[...], dense[...], NT, preferred_element_type=F32).astype(BF)

        def one(q_ref, k_ref, v_ref, d_att_ref, k_total, v_total):
            base = seq * length
            rows = pl.ds(base, length)
            pipe(
                functools.partial(project, (q_ref, k_ref, v_ref, d_att_ref)),
                length // TILE,
                [tall(D), fixed(D, 3 * HEAD_W), tall(D), fixed(HEAD_W, D)],
                [],
                (self.n1.at[rows], self.qkv, self.g.at[rows], self.dense),
            )
            k_total[...] = jnp.zeros_like(k_total)
            v_total[...] = jnp.zeros_like(v_total)
            for i in range(length // TILE):
                seen = (i + 1) * TILE
                here = pl.ds(i * TILE, TILE)
                there = pl.ds(base + i * TILE, TILE)
                q, d_att = q_ref[here, :], d_att_ref[here, :]
                k, v = k_ref[:seen, :], v_ref[:seen, :]
                scores = lax.dot_general(q, k, NT, preferred_element_type=F32) * scale
                row = lax.broadcasted_iota(jnp.int32, scores.shape, 0) + i * TILE
                column = lax.broadcasted_iota(jnp.int32, scores.shape, 1)
                scores = jnp.where(row >= column, scores, MASKED)
                grown = jnp.exp(scores - jnp.max(scores, axis=1, keepdims=True))
                prob = grown * (1.0 / jnp.sum(grown, axis=1, keepdims=True))
                prob_low = prob.astype(BF)
                self.att[there, :] = jnp.dot(prob_low, v, preferred_element_type=F32).astype(BF)
                d_prob = lax.dot_general(d_att, v, NT, preferred_element_type=F32)
                inner = jnp.sum(d_prob * prob, axis=1, keepdims=True)
                d_scores = (prob * (d_prob - inner)).astype(BF)
                d_q = jnp.dot(d_scores, k, preferred_element_type=F32) * scale
                d_q = rotate_back(d_q, self.cos[here, :], self.sin[here, :]).astype(BF)
                self.d_proj[there, :HEAD_W] = d_q
                k_total[:seen, :] += lax.dot_general(d_scores, q, TN, preferred_element_type=F32)
                v_total[:seen, :] += lax.dot_general(prob_low, d_att, TN, preferred_element_type=F32)
            for i in range(length // TILE):
                here = pl.ds(i * TILE, TILE)
                there = pl.ds(base + i * TILE, TILE)
                d_k = rotate_back(k_total[here, :] * scale, self.cos[here, :], self.sin[here, :])
                self.d_proj[there, HEAD_W : 2 * HEAD_W] = d_k.astype(BF)
                self.d_proj[there, 2 * HEAD_W :] = v_total[here, :].astype(BF)
                column_sums(self.qkv_total, self.d_proj[there, :].astype(F32))

        low, wide = pltpu.VMEM((length, HEAD_W), BF), pltpu.VMEM((length, HEAD_W), F32)
        pl.run_scoped(one, low, low, low, low, wide, wide)

    def dense_gradient(self):
        def body(g, part):
            part[...] = lax.dot_general(self.att[...], g[...], TN, preferred_element_type=F32).astype(BF)

        pipe(body, D // 512, [slim(self.tokens, 512)], [slim(HEAD_W, 512)], (self.g, self.dn_part))

    def qkv_gradient(self):
        def body(n1, part):
            part[...] = lax.dot_general(n1[...], self.d_proj[...], TN, preferred_element_type=F32).astype(BF)

        pipe(body, D // TILE, [slim(self.tokens)], [tall(3 * HEAD_W)], (self.n1, self.qk_part))

    def back_one(self):
        def body(qkv, xh, part):
            at = pl.ds(pl.multiple_of(pl.program_id(0) * TILE, TILE), TILE)
            d_n = lax.dot_general(self.d_proj[at, :], qkv[...], NT, preferred_element_type=F32)
            part[...] = (d_n * self.vec[0:1, :]).astype(BF)
            column_sums(self.bias1, d_n)
            column_sums(self.gain1, d_n * xh[...].astype(F32))

        pipe(body, self.tiles, [fixed(D, 3 * HEAD_W), tall(D)], [tall(D)], (self.qkv, self.xhat, self.s1))

    def expand(self):
        def body(n2, up, hidden, slope):
            pre = jnp.dot(n2[...], up[...], preferred_element_type=F32) + self.up_bias[...]
            value, rise = gelu_parts(pre)
            hidden[...] = value.astype(BF)
            slope[...] = rise.astype(BF)

        pipe(
            body,
            self.tiles,
            [tall(D), fixed(D, HID_W)],
            [tall(HID_W)] * 2,
            (self.n2, self.up, self.hidden, self.slope),
        )

    def down_gradient(self):
        def body(g, hidden, part):
            part[...] = lax.dot_general(g[...], hidden[...], TN, preferred_element_type=F32).astype(BF)

        pipe(
            body,
            D // TILE,
            [slim(self.tokens), fixed(self.tokens, HID_W)],
            [tall(HID_W)],
            (self.g, self.hidden, self.wt_part),
        )

    def contract_back(self):
        def body(g, wt, slope, d_pre):
            d_hidden = jnp.dot(g[...], wt[...], preferred_element_type=F32)
            low = (d_hidden * slope[...].astype(F32)).astype(BF)
            d_pre[...] = low
            column_sums(self.up_total, low.astype(F32))

        pipe(
            body,
            self.tiles,
            [tall(D), fixed(D, HID_W), tall(HID_W)],
            [tall(HID_W)],
            (self.g, self.wt, self.slope, self.d_pre),
        )

    def up_gradient(self):
        def body(n2, d_pre, part):
            part[...] = lax.dot_general(n2[...], d_pre[...], TN, preferred_element_type=F32).astype(BF)

        pipe(
            body,
            D // TILE,
            [slim(self.tokens), fixed(self.tokens, HID_W)],
            [tall(HID_W)],
            (self.n2, self.d_pre, self.up_part),
        )

    def back_two(self):
        def body(d_pre, up, xh, s1, part):
            d_n = lax.dot_general(d_pre[...], up[...], NT, preferred_element_type=F32)
            part[...] = (s1[...].astype(F32) + d_n * self.vec[2:3, :]).astype(BF)
            column_sums(self.bias2, d_n)
            column_sums(self.gain2, d_n * xh[...].astype(F32))

        pipe(
            body,
            self.tiles,
            [tall(HID_W), fixed(D, HID_W), tall(D), tall(D)],
            [tall(D)],
            (self.d_pre, self.up, self.xhat, self.s1, self.tok_parts),
        )

    def output(self):
        def body(hidden, dense, wt, part):
            at = pl.ds(pl.multiple_of(pl.program_id(0) * TILE, TILE), TILE)
            total = jnp.dot(self.att[at, :], dense[...], preferred_element_type=F32)
            total = total + lax.dot_general(hidden[...], wt[...], NT, preferred_element_type=F32)
            part[...] = total.astype(BF)

        pipe(
            body,
            self.tiles,
            [tall(HID_W), fixed(HEAD_W, D), fixed(D, HID_W)],
            [tall(D)],
            (self.hidden, self.dense, self.wt, self.out_parts),
        )


def any_spec(count):
    return [pl.BlockSpec(memory_space=pl.ANY)] * count


def slots_needed(n_zero):
    return 20 * n_zero + 120


INPUTS = ("x_own", "g_own", "dn_low", "qk_low", "up_low", "wt_low", "vec_own", "out_bias", "cos", "sin")
RESULTS = ("out_sum", "tok_sum", "dn_home", "qk_home", "up_home", "wt_home", "vec_all", "vec_sums")
TOTALS = (("gain1", D), ("bias1", D), ("gain2", D), ("bias2", D), ("qkv_total", 3 * HEAD_W), ("up_total", HID_W))
WIDTHS = (HEAD_W, 3 * HEAD_W, HID_W, HID_W)


def buffers(tokens):
    square = ("x", "g", "n1", "n2", "xhat", "s1", "tok_parts", "out_parts")
    shapes = {name: (tokens, D) for name in square}
    shapes.update({name: (tokens, HID_W) for name in ("hidden", "slope", "d_pre")})
    shapes.update(dense=(HEAD_W, D), dn_part=(HEAD_W, D), dn_all=(D, HEAD_W), dn_cols=(D, HEAD_W))
    shapes.update(qkv=(D, 3 * HEAD_W), qk_part=(D, 3 * HEAD_W))
    shapes.update({name: (D, HID_W) for name in ("up", "wt", "up_part", "wt_part")})
    return shapes


VEC_ROWS = 16
CHUNK = 128


class VectorGather:
    def __init__(self, wire, place, own, whole):
        self.wire, self.place, self.own, self.whole = wire, place, own, whole
        self.slots = [wire.slot() for _ in range(1, N_SEQ)]
        self.line = LineGather(wire, place, whole, N_SEQ)

    def target(self, s):
        return self.whole.at[pl.ds(self.place.z * N_SEQ + s, 1)]

    def start(self, local_sem):
        p = self.place
        for step in range(1, N_SEQ):
            self.wire.send(self.slots[step - 1], self.own, self.target(p.s), {"seq": lax.rem(p.s + step, N_SEQ)})
        self.copied = pltpu.make_async_copy(self.own, self.target(p.s), local_sem)
        self.copied.start()

    def wait(self):
        p = self.place
        for step in range(1, N_SEQ):
            source = lax.rem(p.s - step + N_SEQ, N_SEQ)
            self.wire.receive(self.slots[step - 1], self.target(source), {"seq": source})
        self.copied.wait()


def lay_out_vectors(layer, place):
    rows = layer.vec_all.shape[1]


    def piece(q):
        shard, row = (q // rows, q % rows) if isinstance(q, int) else (lax.div(q, rows), lax.rem(q, rows))
        return layer.vec_all[shard, pl.ds(row, 1), :]

    count = D // CHUNK
    for row, first in enumerate((0, count, 6 * count, 7 * count)):
        for i in range(count):
            layer.vec[row : row + 1, i * CHUNK : (i + 1) * CHUNK] = piece(first + i)
    each = HEAD_W // CHUNK
    for t in range(3):
        for i in range(each):
            at = t * HEAD_W + i * CHUNK
            layer.qkv_bias[:, at : at + CHUNK] = piece((2 + t) * count + place.part * each + i)
    each = HID_W // CHUNK
    for i in range(each):
        layer.up_bias[:, i * CHUNK : (i + 1) * CHUNK] = piece(8 * count + place.part * each + i)


def partial_vectors(layer):
    fold = lambda total: jnp.sum(total[...], axis=0, keepdims=True)
    rows = [fold(total) for total in (layer.gain1, layer.bias1, layer.gain2, layer.bias2)]
    rows.append(layer.out_bias[...])
    wide = jnp.concatenate(rows + [jnp.zeros((3, D), F32)], axis=0)
    for c in range(PARTS):
        layer.pieces_out[c] = wide[:, c * HEAD_W : (c + 1) * HEAD_W]


def own_vectors(layer, own):
    total = layer.pieces_in[0]
    for c in range(1, PARTS):
        total = total + layer.pieces_in[c]
    own[pl.ds(0, 8), :] = total
    qkv = jnp.sum(layer.qkv_total[...], axis=0, keepdims=True)
    up = jnp.sum(layer.up_total[...], axis=0, keepdims=True)
    cut = lambda row, count: [row[:, i * HEAD_W : (i + 1) * HEAD_W] for i in range(count)]
    rows = cut(qkv, 3) + cut(up, 4) + [jnp.zeros((1, HEAD_W), F32)]
    own[pl.ds(8, 8), :] = jnp.concatenate(rows, axis=0)


def layer_body(n_zero, rows, tokens, *refs):
    names = INPUTS + RESULTS + tuple(buffers(tokens))
    names += ("att", "d_proj", "send_sems", "recv_sems", "local_sems", "own", "total")
    names += ("vec", "qkv_bias", "up_bias", "pieces_out", "pieces_in", "vec_line", "vec_total")
    names += tuple(name for name, _ in TOTALS)
    held = dict(zip(names, refs))
    scratch = list(refs[len(names) :])
    take = lambda count: [scratch.pop(0) for _ in range(count)]
    layer = Layer(held)
    place = Place(n_zero)
    wire = Wire(layer.send_sems, layer.recv_sems)
    local = lambda index: layer.local_sems.at[index]
    block = rows * N_SEQ
    chunk = lambda c: pl.ds(pl.multiple_of(c * HEAD_W, HEAD_W), HEAD_W)

    sources = (layer.dn_low, layer.qk_low, layer.up_low, layer.wt_low)
    wholes = (layer.dn_all, layer.qkv, layer.up, layer.wt)
    exchanges = [SeqExchange(wire, place, low, whole, rows) for low, whole in zip(sources, wholes)]
    dn, qk, up, wt = [LineGather(wire, place, whole, block) for whole in wholes]
    x = PlaneGather(wire, place, layer.x_own, layer.x)
    g = PlaneGather(wire, place, layer.g_own, layer.g)
    dense_in = DenseExchange(
        wire, place, lambda c: layer.dn_all.at[chunk(c)], lambda c: layer.dense.at[:, chunk(c)]
    )
    dense_out = DenseExchange(
        wire, place, lambda c: layer.dn_part.at[:, chunk(c)], lambda c: layer.dn_cols.at[chunk(c)]
    )
    planes = []
    for k, parts in enumerate((layer.out_parts, layer.tok_parts)):
        mate, far, across, turned = take(4)
        planes.append(
            PlaneScatter(wire, place, parts, mate, far, across, turned, layer.total, layer.own, local(k))
        )
    out, tok = planes
    sums, homes = [], []
    parts = (layer.dn_cols, layer.qk_part, layer.up_part, layer.wt_part)
    results = (layer.dn_home, layer.qk_home, layer.up_home, layer.wt_home)
    for k, width in enumerate(WIDTHS):
        ring, total = take(2)
        own = take(1)[0]
        sums.append(LineScatter(wire, place, parts[k], ring, total, own, block, local(2 + k)))
        homes.append(Home(wire, place, total, results[k], rows))
    dn_sum, qk_sum, up_sum, wt_sum = sums

    def finish(k):
        sums[k].last()
        homes[k].start(local(6 + k))

    def store(scatter, result):
        scatter.last()
        copy = pltpu.make_async_copy(scatter.total, result, scatter.sem)
        copy.start()
        copy.wait()

    alone = layer.vec_all.shape[0] == 1
    gather = None if alone else VectorGather(wire, place, layer.vec_own, layer.vec_all)

    def vector_in_start():
        if not alone:
            gather.start(local(18))

    def vector_in_pass():
        if not alone:
            gather.wait()
            gather.line.own_from_ends()
            gather.line.own_from_middle()

    def vector_in_rest():
        if alone:
            copy = pltpu.make_async_copy(layer.vec_own, layer.vec_all, local(18))
            copy.start()
            copy.wait()
        else:
            for step in range(1, n_zero):
                gather.line.ahead(step)
        lay_out_vectors(layer, place)

    pieces = DenseExchange(
        wire, place, lambda c: layer.pieces_out.at[c], lambda c: layer.pieces_in.at[c]
    )
    vector_line = LineGather(wire, place, layer.vec_line, VEC_ROWS)
    vector_spread = DenseExchange(
        wire, place, lambda c: layer.vec_total, lambda c: layer.vec_sums.at[c]
    )

    def vector_out_start():
        partial_vectors(layer)
        pieces.start(local(18))

    def vector_out_pass():
        pieces.wait()
        own = vector_line.block(place.z)
        own_vectors(layer, own)
        vector_line.own_from_ends()
        vector_line.own_from_middle()

    def vector_out_spread():
        total = layer.vec_line[pl.ds(0, VEC_ROWS), :]
        for j in range(1, n_zero):
            total = total + layer.vec_line[pl.ds(j * VEC_ROWS, VEC_ROWS), :]
        layer.vec_total[...] = total
        vector_spread.start(local(19))

    place.barrier()
    layer.clear()
    exchanges[0].start(local(12))
    vector_in_start()
    exchanges[2].start(local(14))
    x.start(local(10))
    exchanges[0].wait()
    dn.own_from_ends()
    dn.own_from_middle()
    vector_in_pass()
    dn.ahead(1)
    exchanges[2].wait()
    up.own_from_ends()
    exchanges[1].start(local(13))
    up.own_from_middle()
    dn.ahead(2)
    x.turn()
    g.start(local(11))
    up.ahead(1)
    exchanges[3].start(local(15))
    vector_in_rest()
    x.turn_again()
    up.ahead(2)
    x.wait()
    layer.normalise(0, 2)
    exchanges[1].wait()
    qk.own_from_ends()
    qk.own_from_middle()
    for step in range(3, n_zero):
        dn.ahead(step)
    layer.normalise(1, 2)
    g.turn()
    for step in range(3, n_zero):
        up.ahead(step)
    layer.expand()
    exchanges[3].wait()
    wt.own_from_ends()
    qk.ahead(1)
    g.turn_again()
    g.wait()
    layer.down_gradient()
    dense_in.start(local(16))
    qk.ahead(2)
    wt_sum.launch(0)
    for step in range(3, n_zero):
        qk.ahead(step)
    wt.own_from_middle()
    dense_in.wait()
    layer.attend(0)
    wt_sum.launch(1)
    wt.ahead(1)
    wt_sum.launch(2)
    layer.attend(1)
    wt_sum.advance(1)
    layer.qkv_gradient()
    layer.dense_gradient()
    qk_sum.launch(0)
    qk_sum.launch(1)
    wt.ahead(2)
    qk_sum.launch(2)
    dense_out.start(local(17))
    layer.back_one()
    for step in range(3, n_zero):
        wt.ahead(step)
    dense_out.wait()
    wt_sum.advance(2)
    layer.contract_back()
    layer.output()
    dn_sum.launch(0)
    out.start()
    finish(3)
    layer.up_gradient()
    up_sum.launch(0)
    out.turn()
    qk_sum.advance(1)
    dn_sum.launch(1)
    layer.back_two()
    up_sum.launch(1)
    out.turn_again()
    homes[3].wait()
    dn_sum.advance(1)
    tok.start()
    qk_sum.advance(2)
    tok.turn()
    vector_out_start()
    dn_sum.launch(2)
    up_sum.advance(1)
    dn_sum.advance(2)
    tok.turn_again()
    up_sum.launch(2)
    up_sum.advance(2)
    store(out, layer.out_sum)
    vector_out_pass()
    finish(1)
    finish(0)
    store(tok, layer.tok_sum)
    finish(2)
    vector_line.ahead(1)
    for step in range(2, n_zero):
        vector_line.ahead(step)
    vector_out_spread()
    homes[2].wait()
    homes[0].wait()
    homes[1].wait()
    vector_spread.wait()
    wire.finish()


def layer_call(n_zero, rows, tokens, *operands):
    local = tokens // PARTS
    block = rows * N_SEQ
    slots = slots_needed(n_zero)
    shards = (9 * D + FF) // (operands[6].shape[1] * CHUNK)
    vmem = lambda *dims: pltpu.VMEM(dims, BF)
    scratch = [
        vmem(tokens, HEAD_W),
        vmem(tokens, 3 * HEAD_W),
        pltpu.SemaphoreType.DMA((slots,)),
        pltpu.SemaphoreType.DMA((slots,)),
        pltpu.SemaphoreType.DMA((20,)),
        vmem(local, D),
        pltpu.VMEM((local, D), F32),
    ]
    wide = lambda *dims: pltpu.VMEM(dims, F32)
    scratch += [wide(4, D), wide(1, 3 * HEAD_W), wide(1, HID_W), wide(PARTS, 8, HEAD_W)]
    scratch += [wide(PARTS, 8, HEAD_W), wide(n_zero * VEC_ROWS, HEAD_W), wide(VEC_ROWS, HEAD_W)]
    scratch += [wide(8, width) for _, width in TOTALS]
    for _ in range(2):
        scratch += [vmem(2, 2, local, D), vmem(local, D), vmem(local, D), vmem(local, D)]
    for width in WIDTHS:
        scratch += [vmem(n_zero + 1, block, width), vmem(block, width), vmem(block, width)]
    homes = [jax.ShapeDtypeStruct((N_DP, N_SEQ, rows, width), BF) for width in WIDTHS]
    anywhere = pl.BlockSpec(memory_space=pl.ANY)
    vector = pl.BlockSpec(memory_space=pltpu.VMEM)
    held = buffers(tokens)
    return pl.pallas_call(
        functools.partial(layer_body, n_zero, rows, tokens),
        in_specs=[anywhere] * 7 + [vector] * 3,
        out_specs=[anywhere] * (len(RESULTS) - 2) + [vector] * 2 + [anywhere] * len(held),
        out_shape=[jax.ShapeDtypeStruct((local, D), F32)] * 2
        + homes
        + [
            jax.ShapeDtypeStruct((shards,) + operands[6].shape[1:], F32),
            jax.ShapeDtypeStruct((PARTS, VEC_ROWS, HEAD_W), F32),
        ]
        + [jax.ShapeDtypeStruct(shape, BF) for shape in held.values()],
        scratch_shapes=scratch,
        compiler_params=pltpu.CompilerParams(
            collective_id=0, has_side_effects=True, vmem_limit_bytes=62 * 1024 * 1024
        ),
        name="layer",
    )(*operands)


def adam_body(decay, flipped, home, param, first, second, new, first_new, second_new, grad_out):
    if flipped:
        gradient = home[0, 0].astype(F32).T
    else:
        gradient = jnp.concatenate([home[0, k] for k in range(home.shape[1])], axis=1).astype(F32)
    updated = adam_step(param[...], gradient, first[...], second[...], decay)
    new[...], first_new[...], second_new[...] = updated
    grad_out[...] = gradient


def adam(home, pieces, param, first, second, flipped=False):
    rows, width = home.shape[2], home.shape[3] // pieces
    together = max(1, min(N_SEQ, HID_W // width))
    groups = PARTS // together
    if flipped:
        block = pl.BlockSpec((width, rows), lambda c, t: (c, 0))
    else:
        block = pl.BlockSpec((rows, width * together), lambda c, t: (0, t * groups + c))
    each = N_SEQ // together
    return pl.pallas_call(
        functools.partial(adam_body, WEIGHT_DECAY, flipped),
        grid=(groups, pieces),
        in_specs=[
            pl.BlockSpec((1, together, rows, width), lambda c, t: (c // each, c % each, 0, t)),
            block,
            block,
            block,
        ],
        out_specs=[block] * 4,
        out_shape=[jax.ShapeDtypeStruct(param.shape, F32)] * 4,
        compiler_params=pltpu.CompilerParams(vmem_limit_bytes=48 * 1024 * 1024),
        name="adam",
    )(home, param, first, second)


def rotary_rows(length):
    exponent = np.arange(ROT // 2, dtype=np.float32) * np.float32(2.0 / ROT)
    inverse = np.power(np.float32(10000.0), -exponent)
    angles = np.arange(length, dtype=np.float32)[:, None] * inverse[None, :]
    cosine, sine = np.cos(angles), np.sin(angles)
    ones = np.ones((length, 128 - ROT), np.float32)
    cosine = np.concatenate([cosine, cosine, ones], axis=1)
    sine = np.concatenate([-sine, sine, 0.0 * ones], axis=1)
    return jnp.asarray(cosine), jnp.asarray(sine)


def make_body(sizes):
    n_zero = sizes["zero"]
    everywhere = ("dp", "zero", "seq")

    def body(
        inputs,
        out_grad,
        vectors,
        qkv_weight,
        dense_weight,
        up_weight,
        down_weight,
        vectors_first,
        qkv_first,
        dense_first,
        up_first,
        down_first,
        vectors_second,
        qkv_second,
        dense_second,
        up_second,
        down_second,
    ):
        dp_i, zero_i, seq_i = (lax.axis_index(axis) for axis in everywhere)
        seqs_here, local_len = inputs.shape[0], inputs.shape[1]
        token_rows = seqs_here * local_len
        rows = qkv_weight.shape[0]

        def columns(value, width):
            wide = value.shape[1] // N_DP
            half = lax.dynamic_slice_in_dim(value, dp_i * wide, wide, 1).astype(BF)
            return half.reshape(rows, N_SEQ, width).transpose(1, 0, 2)

        qk_low = jnp.concatenate(
            [columns(qkv_weight[:, t * D : (t + 1) * D], HEAD_W) for t in range(3)], axis=2
        )
        dn_low = columns(dense_weight, HEAD_W)
        up_low = columns(up_weight, HID_W)
        wt_low = lax.dynamic_slice_in_dim(down_weight, dp_i * (FF // N_DP), FF // N_DP, 0).astype(BF)
        wt_low = wt_low.reshape(N_SEQ, HID_W, rows).transpose(0, 2, 1)

        tokens_low = inputs.reshape(token_rows, D)
        grad_low = out_grad.reshape(token_rows, D)
        tokens = N_DP * N_SEQ * token_rows
        grad_wide = grad_low.astype(F32)
        d_out_bias = jnp.sum(grad_wide, axis=0, keepdims=True)
        vec_low = lax.reduce_precision(vectors, exponent_bits=8, mantissa_bits=7)
        if vectors.shape[0] % CHUNK == 0:
            vec_low = vec_low.reshape(1, -1, CHUNK)
        else:
            vec_low = lax.all_gather(vec_low, ("zero", "seq"), axis=0, tiled=True).reshape(1, -1, CHUNK)
        results = layer_call(
            n_zero,
            rows,
            tokens,
            tokens_low,
            grad_low,
            dn_low,
            qk_low,
            up_low,
            wt_low,
            vec_low,
            d_out_bias,
            *rotary_rows(tokens // N_DP),
        )
        out_sum, d_xhat, dn_home, qk_home, up_home, wt_home, vec_all, vec_sums = results[: len(RESULTS)]
        vec_flat = vec_all.reshape(-1)
        dense_bias, down_bias = vec_flat[5 * D : 6 * D], vec_flat[8 * D + FF : 9 * D + FF]

        def statistics(values):
            average = jnp.mean(values, axis=-1, keepdims=True)
            centred = values - average
            spread = jnp.mean(centred * centred, axis=-1, keepdims=True)
            return centred, lax.rsqrt(spread + NORM_EPSILON)

        tokens_wide = tokens_low.astype(F32)
        outputs = (tokens_wide + out_sum + dense_bias + down_bias).astype(BF).reshape(inputs.shape)
        centred_own, rate_own = statistics(tokens_wide)
        xhat_own = centred_own * rate_own
        d_tokens = rate_own * (
            d_xhat
            - jnp.mean(d_xhat, axis=-1, keepdims=True)
            - xhat_own * jnp.mean(d_xhat * xhat_own, axis=-1, keepdims=True)
        )
        input_grad = (grad_wide + d_tokens).astype(BF).reshape(inputs.shape)

        row = lambda k: vec_sums[:, k].reshape(-1)
        vector_sum = jnp.concatenate(
            [
                row(0),
                row(1),
                vec_sums[:, 8:11].transpose(1, 0, 2).reshape(-1),
                row(4),
                row(2),
                row(3),
                vec_sums[:, 11:15].reshape(-1),
                row(4),
            ]
        )
        vectors_grad = lax.dynamic_slice_in_dim(
            vector_sum, (zero_i * N_SEQ + seq_i) * vectors.shape[0], vectors.shape[0], 0
        )

        vec_upd = adam_step(vectors, vectors_grad, vectors_first, vectors_second, 0.0) + (vectors_grad,)
        qkv_upd = adam(qk_home, 3, qkv_weight, qkv_first, qkv_second)
        dense_upd = adam(dn_home, 1, dense_weight, dense_first, dense_second)
        up_upd = adam(up_home, 1, up_weight, up_first, up_second)
        down_upd = adam(wt_home, 1, down_weight, down_first, down_second, flipped=True)
        updates = (vec_upd, qkv_upd, dense_upd, up_upd, down_upd)
        picked = lambda k: tuple(update[k] for update in updates)
        return (outputs, input_grad) + picked(3) + picked(0) + picked(1) + picked(2)

    return body


def solution(mesh):
    wide = P(("dp", "zero"), "seq", None)
    vector = P(("zero", "seq"))
    rows = P(("zero", "seq"), None)
    columns = P(None, ("zero", "seq"))
    state = (vector, rows, rows, rows, columns)
    return jax.shard_map(
        make_body(dict(mesh.shape)),
        mesh=mesh,
        in_specs=(wide, wide) + state * 3,
        out_specs=(wide, wide) + state * 4,
        check_vma=False,
    )
```

```python
import functools
import math

import jax
import jax.numpy as jnp
import numpy as np
from jax import lax
from jax.experimental import pallas as pl
from jax.experimental.pallas import tpu as pltpu
from jax.sharding import PartitionSpec as P

D = 2048
HEADS = 8
HEAD_DIM = 256
FF = 8192
ROT = 64
ADAM_STEP = 4

BETA_ONE = 0.9
BETA_TWO = 0.95
LEARN_RATE = 0.5
EPSILON = 1e-08
WEIGHT_DECAY = 0.1
NORM_EPSILON = 1e-05
MASKED = -1e30
N_DP = 2
N_SEQ = 4
PARTS = N_DP * N_SEQ
HEAD_W = D // PARTS
HID_W = FF // PARTS
BF = jnp.bfloat16
F32 = jnp.float32
NT = (((1,), (1,)), ((), ()))
TN = (((0,), (0,)), ((), ()))


def adam_step(parameter, gradient, first_moment, second, decay_rate):
    first_new = BETA_ONE * first_moment + (1.0 - BETA_ONE) * gradient
    second_new = BETA_TWO * second + (1.0 - BETA_TWO) * gradient * gradient
    first_hat = first_new / (1.0 - BETA_ONE**ADAM_STEP)
    second_hat = second_new / (1.0 - BETA_TWO**ADAM_STEP)
    param_new = parameter - LEARN_RATE * (
        first_hat / (jnp.sqrt(second_hat) + EPSILON) + decay_rate * parameter
    )
    return (param_new, first_new, second_new)


class Wire:
    def __init__(self, send_sems, recv_sems):
        self.send_sems, self.recv_sems, self.used = send_sems, recv_sems, 0
        self.sent = []

    def slot(self):
        self.used += 1
        return self.used - 1

    def copy(self, slot, source, target, device):
        return pltpu.make_async_remote_copy(
            src_ref=source,
            dst_ref=target,
            send_sem=self.send_sems.at[slot],
            recv_sem=self.recv_sems.at[slot],
            device_id=device,
            device_id_type=pl.DeviceIdType.MESH,
        )

    def send(self, slot, source, target, device, when=None):
        copy = self.copy(slot, source, target, device)
        guarded(when, copy.start)
        self.sent.append((copy, when))

    def receive(self, slot, target, device, when=None):
        copy = self.copy(slot, target, target, device)
        guarded(when, copy.wait_recv)

    def finish(self):
        for copy, when in self.sent:
            guarded(when, copy.wait_send)
        self.sent = []


def guarded(when, action):
    if when is None:
        action()
    else:
        pl.when(when)(action)


class Place:
    def __init__(self, n_zero):
        self.n = n_zero
        self.dp, self.z, self.s = (lax.axis_index(a) for a in ("dp", "zero", "seq"))
        flip = lambda value, bit: jnp.bitwise_xor(value, bit)
        self.dp_far, self.s_far, self.s_core = 1 - self.dp, flip(self.s, 2), flip(self.s, 1)
        self.s_both = flip(self.s, 3)
        self.across = {"dp": self.dp_far}
        self.far = {"seq": self.s_far}
        self.core = {"seq": self.s_core}
        self.above, self.below = {"zero": self.z + 1}, {"zero": self.z - 1}
        self.part = self.dp * N_SEQ + self.s

    def others(self):
        for step in range(1, N_DP * N_SEQ):
            at = lax.rem(self.part + step, N_DP * N_SEQ)
            dp, s = lax.div(at, N_SEQ), lax.rem(at, N_SEQ)
            yield step, dp, s, {"dp": dp, "seq": s}

    def barrier(self):
        gate = pltpu.get_barrier_semaphore()
        signal = lambda device: pl.semaphore_signal(
            gate, inc=1, device_id=device, device_id_type=pl.DeviceIdType.MESH
        )
        for _, _, _, device in self.others():
            signal(device)
        pl.when(self.z < self.n - 1)(lambda: signal(self.above))
        pl.when(self.z > 0)(lambda: signal(self.below))
        ends = (self.z < self.n - 1).astype(jnp.int32) + (self.z > 0).astype(jnp.int32)
        pl.semaphore_wait(gate, N_DP * N_SEQ - 1 + ends)


class LineGather:
    def __init__(self, wire, place, whole, rows):
        self.wire, self.place, self.whole, self.rows = wire, place, whole, rows
        self.ups = [wire.slot() for _ in range(place.n - 1)]
        self.downs = [wire.slot() for _ in range(place.n - 1)]

    def block(self, index):
        return self.whole.at[pl.ds(pl.multiple_of(index * self.rows, self.rows), self.rows)]

    def send_up(self, step, block, when):
        self.wire.send(self.ups[step - 1], block, block, self.place.above, when)

    def send_down(self, step, block, when):
        self.wire.send(self.downs[step - 1], block, block, self.place.below, when)

    def own_from_ends(self):
        p = self.place
        self.send_up(1, self.block(p.z), p.z == 0)
        self.send_down(1, self.block(p.z), p.z == p.n - 1)

    def own_from_middle(self):
        p = self.place
        middle = (p.z > 0) & (p.z < p.n - 1)
        self.send_up(1, self.block(p.z), middle)
        self.send_down(1, self.block(p.z), middle)

    def ahead(self, step):
        p = self.place
        up, down = self.block(jnp.maximum(p.z - step, 0)), self.block(jnp.minimum(p.z + step, p.n - 1))
        self.wire.receive(self.ups[step - 1], up, p.below, p.z >= step)
        if step + 1 < p.n:
            self.send_up(step + 1, up, (p.z < p.n - 1) & (p.z >= step))
        self.wire.receive(self.downs[step - 1], down, p.above, p.z + step < p.n)
        if step + 1 < p.n:
            self.send_down(step + 1, down, (p.z > 0) & (p.z + step < p.n))


class SeqExchange:
    def __init__(self, wire, place, send, whole, rows):
        self.wire, self.place, self.out, self.whole, self.rows = wire, place, send, whole, rows
        self.slots = [wire.slot() for _ in range(1, N_SEQ)]

    def target(self, s):
        row = (self.place.z * N_SEQ + s) * self.rows
        return self.whole.at[pl.ds(pl.multiple_of(row, self.rows), self.rows)]

    def start(self, local_sem):
        p = self.place
        for step in range(1, N_SEQ):
            to = lax.rem(p.s + step, N_SEQ)
            self.wire.send(self.slots[step - 1], self.out.at[to], self.target(p.s), {"seq": to})
        own = pltpu.make_async_copy(self.out.at[p.s], self.target(p.s), local_sem)
        own.start()
        self.own = own

    def wait(self):
        p = self.place
        for step in range(1, N_SEQ):
            source = lax.rem(p.s - step + N_SEQ, N_SEQ)
            self.wire.receive(self.slots[step - 1], self.target(source), {"seq": source})
        self.own.wait()


class PlaneGather:
    def __init__(self, wire, place, block, whole):
        self.wire, self.place, self.own, self.whole = wire, place, block, whole
        self.slots = {name: wire.slot() for name in ("far", "across", "both0", "both1", "c0", "c1", "c2", "c3")}
        self.rows = block.shape[0]
        self.half = self.rows // 2

    def at(self, dp, s):
        row = (dp * N_SEQ + s) * self.rows
        return self.whole.at[pl.ds(pl.multiple_of(row, self.rows), self.rows)]

    def start(self, local_sem):
        p, w, slots = self.place, self.wire, self.slots
        mine = self.at(p.dp, p.s)
        w.send(slots["far"], self.own, mine, p.far)
        w.send(slots["across"], self.own, mine, p.across)
        w.send(slots["c0"], self.own, mine, p.core)
        self.copied = pltpu.make_async_copy(self.own, mine, local_sem)
        self.copied.start()

    def turn(self):
        p, w, slots, h = self.place, self.wire, self.slots, self.half
        far, across = self.at(p.dp, p.s_far), self.at(p.dp_far, p.s)
        w.receive(slots["far"], far, p.far)
        w.send(slots["both0"], far.at[pl.ds(0, h)], far.at[pl.ds(0, h)], p.across)
        w.send(slots["c1"], far, far, p.core)
        w.receive(slots["across"], across, p.across)
        w.send(slots["both1"], across.at[pl.ds(h, h)], across.at[pl.ds(h, h)], p.far)
        w.send(slots["c2"], across, across, p.core)

    def turn_again(self):
        p, w, slots, h = self.place, self.wire, self.slots, self.half
        both = self.at(p.dp_far, p.s_far)
        w.receive(slots["both0"], both.at[pl.ds(0, h)], p.across)
        w.receive(slots["both1"], both.at[pl.ds(h, h)], p.far)
        w.send(slots["c3"], both, both, p.core)

    def wait(self):
        p, w, slots = self.place, self.wire, self.slots
        w.receive(slots["c0"], self.at(p.dp, p.s_core), p.core)
        w.receive(slots["c1"], self.at(p.dp, p.s_both), p.core)
        w.receive(slots["c2"], self.at(p.dp_far, p.s_core), p.core)
        w.receive(slots["c3"], self.at(p.dp_far, p.s_both), p.core)
        self.copied.wait()


def add_rows(target, *sources):
    rows = target.shape[0]
    tile = 32 if rows % 32 == 0 else 16

    def one(i, carry):
        at = pl.ds(pl.multiple_of(i * tile, tile), tile)
        total = sources[0][at, :].astype(F32)
        for source in sources[1:]:
            total = total + source[at, :].astype(F32)
        target[at, :] = total.astype(target.dtype)
        return carry

    lax.fori_loop(0, rows // tile, one, 0)


class LineScatter:
    def __init__(self, wire, place, parts, held, total, own, rows, sem):
        self.wire, self.place, self.parts, self.rows = wire, place, parts, rows
        self.held, self.total, self.own, self.sem = held, total, own, sem
        self.launched, self.advanced = 0, 1
        self.up_slots = [wire.slot() for _ in range(place.n)]
        self.down_slots = [wire.slot() for _ in range(place.n)]

    def part(self, j):
        return self.parts.at[pl.ds(pl.multiple_of(j * self.rows, self.rows), self.rows)]

    def fetch(self, j, target):
        return pltpu.make_async_copy(self.part(j), target, self.sem)

    def launch(self, k):
        p = self.place
        top = p.n - 1
        up, down = top - k, k
        self.wire.send(
            self.up_slots[up], self.part(up), self.held.at[up + 1], p.above, p.z == 0
        )
        self.wire.send(
            self.down_slots[down], self.part(down), self.held.at[down], p.below, p.z == top
        )
        self.launched = k + 1

    def advance(self, k):
        p = self.place
        top = p.n - 1
        up = jnp.minimum(top - k + p.z, top)
        self.hop(up, up + 1, self.up_slots[0] + up, p.above, p.below, (p.z > 0) & (p.z <= k))
        down = jnp.maximum(k - top + p.z, 0)
        self.hop(down, down, self.down_slots[0] + down, p.below, p.above, (p.z < top) & (top - p.z <= k))
        self.advanced = k + 1

    def hop(self, j, index, slot, onto, source, active):
        held = self.held.at[index]

        def go():
            copy = self.fetch(j, self.own)
            copy.start()
            self.wire.receive(slot, held, source)
            copy.wait()
            add_rows(held, held, self.own)

        pl.when(active)(go)
        self.wire.send(slot, held, held, onto, active)

    def last(self):
        p = self.place
        for k in range(self.launched, p.n - 1):
            self.launch(k)
        for k in range(self.advanced, p.n - 1):
            self.advance(k)
        copy = self.fetch(p.z, self.own)
        copy.start()
        copy.wait()
        up, down = self.held.at[p.z + 1], self.held.at[p.z]

        @pl.when(p.z == 0)
        def _():
            self.arrive(down, self.down_slots, p.above)
            add_rows(self.total, self.own, down)

        @pl.when(p.z == p.n - 1)
        def _():
            self.arrive(up, self.up_slots, p.below)
            add_rows(self.total, self.own, up)

        @pl.when((p.z > 0) & (p.z < p.n - 1))
        def _():
            self.arrive(up, self.up_slots, p.below)
            self.arrive(down, self.down_slots, p.above)
            add_rows(self.total, self.own, up, down)

    def arrive(self, held, slots, source):
        self.wire.receive(slots[0] + self.place.z, held, source)


class Home:
    def __init__(self, wire, place, total, home, rows):
        self.wire, self.place, self.total, self.home, self.rows = wire, place, total, home, rows
        self.slots = [wire.slot() for _ in range(1, N_DP * N_SEQ)]

    def target(self, dp, s):
        return self.home.at[dp, s]

    def piece(self, s):
        return self.total.at[pl.ds(pl.multiple_of(s * self.rows, self.rows), self.rows)]

    def start(self, local_sem):
        p = self.place
        for step, dp, s, device in p.others():
            self.wire.send(self.slots[step - 1], self.piece(s), self.target(p.dp, p.s), device)
        self.copied = pltpu.make_async_copy(self.piece(p.s), self.target(p.dp, p.s), local_sem)
        self.copied.start()

    def wait(self):
        p = self.place
        parts = N_DP * N_SEQ
        for step in range(1, parts):
            at = lax.rem(p.part - step + parts, parts)
            dp, s = lax.div(at, N_SEQ), lax.rem(at, N_SEQ)
            self.wire.receive(self.slots[step - 1], self.target(dp, s), {"dp": dp, "seq": s})
        self.copied.wait()


class DenseExchange:
    def __init__(self, wire, place, source, target):
        self.wire, self.place, self.source, self.target = wire, place, source, target
        self.slots = [wire.slot() for _ in range(1, N_DP * N_SEQ)]

    def start(self, local_sem):
        p = self.place
        for step, dp, s, device in p.others():
            self.wire.send(self.slots[step - 1], self.source(dp * N_SEQ + s), self.target(p.part), device)
        self.copied = pltpu.make_async_copy(self.source(p.part), self.target(p.part), local_sem)
        self.copied.start()

    def wait(self):
        p = self.place
        parts = N_DP * N_SEQ
        for step in range(1, parts):
            at = lax.rem(p.part - step + parts, parts)
            device = {"dp": lax.div(at, N_SEQ), "seq": lax.rem(at, N_SEQ)}
            self.wire.receive(self.slots[step - 1], self.target(at), device)
        self.copied.wait()


class PlaneScatter:
    def __init__(self, wire, place, parts, mate, from_far, from_across, turned, total, own, sem):
        self.wire, self.place, self.parts, self.mate, self.sums = wire, place, parts, mate, mate
        self.from_far, self.from_across, self.turned = from_far, from_across, turned
        self.total, self.own, self.sem = total, own, sem
        self.rows = total.shape[0]
        self.half = self.rows // 2
        self.core_slots = [[wire.slot() for _ in range(2)] for _ in range(2)]
        names = ("turn_across", "turn_far", "far0", "far1", "across0", "across1")
        self.slots = {name: wire.slot() for name in names}

    def part(self, dp, s):
        row = (dp * N_SEQ + s) * self.rows
        return self.parts.at[pl.ds(pl.multiple_of(row, self.rows), self.rows)]

    def start(self):
        p = self.place
        core = lax.rem(p.s_core, 2)
        for dp in range(2):
            for y in range(2):
                self.wire.send(
                    self.core_slots[dp][y], self.part(dp, 2 * y + core), self.mate.at[dp, y], p.core
                )

    def combine(self, dp, y):
        p = self.place
        core = lax.rem(p.s, 2)
        for d in range(2):
            for v in range(2):

                @pl.when((dp == d) & (y == v))
                def _(d=d, v=v):
                    copy = pltpu.make_async_copy(self.part(d, 2 * v + core), self.own, self.sem)
                    copy.start()
                    self.wire.receive(self.core_slots[d][v], self.mate.at[d, v], p.core)
                    copy.wait()
                    add_rows(self.sums.at[d, v], self.own, self.mate.at[d, v])

    def turn(self):
        p, w, h, slots = self.place, self.wire, self.half, self.slots
        y = lax.div(p.s, 2)
        y_far = 1 - y
        low, high = pl.ds(0, h), pl.ds(h, h)
        self.combine(p.dp_far, y_far)
        both = self.sums.at[p.dp_far, y_far]
        w.send(slots["turn_across"], both.at[low], self.turned.at[low], p.across)
        w.send(slots["turn_far"], both.at[high], self.turned.at[high], p.far)
        self.combine(p.dp, y_far)
        far = self.sums.at[p.dp, y_far]
        w.send(slots["far1"], far.at[high], self.from_far.at[high], p.far)
        self.combine(p.dp_far, y)
        across = self.sums.at[p.dp_far, y]
        w.send(slots["across0"], across.at[low], self.from_across.at[low], p.across)
        self.combine(p.dp, y)

    def turn_again(self):
        p, w, h, slots = self.place, self.wire, self.half, self.slots
        y = lax.div(p.s, 2)
        low, high = pl.ds(0, h), pl.ds(h, h)
        far, across = self.sums.at[p.dp, 1 - y], self.sums.at[p.dp_far, y]
        w.receive(slots["turn_across"], self.turned.at[low], p.across)
        add_rows(far.at[low], far.at[low], self.turned.at[low])
        w.send(slots["far0"], far.at[low], self.from_far.at[low], p.far)
        w.receive(slots["turn_far"], self.turned.at[high], p.far)
        add_rows(across.at[high], across.at[high], self.turned.at[high])
        w.send(slots["across1"], across.at[high], self.from_across.at[high], p.across)

    def last(self):
        p, w, h, slots = self.place, self.wire, self.half, self.slots
        low, high = pl.ds(0, h), pl.ds(h, h)
        w.receive(slots["far1"], self.from_far.at[high], p.far)
        w.receive(slots["far0"], self.from_far.at[low], p.far)
        w.receive(slots["across0"], self.from_across.at[low], p.across)
        w.receive(slots["across1"], self.from_across.at[high], p.across)
        add_rows(self.total, self.sums.at[p.dp, lax.div(p.s, 2)], self.from_far, self.from_across)


def gelu_parts(values):
    phi_wide = 0.5 * (1.0 + lax.erf(values * (1.0 / math.sqrt(2.0))))
    density = jnp.exp(-0.5 * values * values) * (1.0 / math.sqrt(2.0 * math.pi))
    return values * phi_wide, phi_wide + values * density


TILE = 256


def pipe(body, grid, ins, outs, refs):
    pltpu.emit_pipeline(
        body, grid=(grid,), in_specs=[spec for spec in ins], out_specs=[spec for spec in outs]
    )(*refs)


def tall(width, tile=TILE):
    return pl.BlockSpec((tile, width), lambda i: (i, 0))


def slim(height, tile=TILE):
    return pl.BlockSpec((height, tile), lambda i: (0, i))


def fixed(height, width):
    return pl.BlockSpec((height, width), lambda i: (0, 0), pipeline_mode=pl.Buffered(1))


def column_sums(total, values):
    rows, width = values.shape
    total[...] += jnp.sum(values.reshape(rows // 8, 8, width), axis=0)


def rotate(block, cosine, sine):
    half = ROT // 2
    first = block[:, :128]
    rolled = jnp.concatenate([first[:, half:ROT], first[:, :half], first[:, ROT:]], axis=1)
    return jnp.concatenate([first * cosine + rolled * sine, block[:, 128:]], axis=1)


def rotate_back(block, cosine, sine):
    half = ROT // 2
    first = block[:, :128]
    scaled = first * sine
    rolled = jnp.concatenate([scaled[:, half:ROT], scaled[:, :half], scaled[:, ROT:]], axis=1)
    return jnp.concatenate([first * cosine + rolled, block[:, 128:]], axis=1)


class Layer:
    def __init__(self, refs):
        self.__dict__.update(refs)
        self.tokens = self.x.shape[0]
        self.length = self.tokens // N_DP
        self.tiles = self.tokens // TILE

    def clear(self):
        for total in (self.gain1, self.bias1, self.gain2, self.bias2, self.qkv_total, self.up_total):
            total[...] = jnp.zeros_like(total)

    def normalise(self, part, of):
        count = self.tokens // of
        rows = pl.ds(part * count, count)

        def body(x, n1, n2, xh):
            def some(i, carry):
                at = pl.ds(pl.multiple_of(i * 32, 32), 32)
                values = x[at, :].astype(F32)
                centred = values - jnp.mean(values, axis=1, keepdims=True)
                spread = jnp.mean(centred * centred, axis=1, keepdims=True)
                xhat = centred * lax.rsqrt(spread + NORM_EPSILON)
                xh[at, :] = xhat.astype(BF)
                n1[at, :] = (xhat * self.vec[0:1, :] + self.vec[1:2, :]).astype(BF)
                n2[at, :] = (xhat * self.vec[2:3, :] + self.vec[3:4, :]).astype(BF)
                return carry

            lax.fori_loop(0, TILE // 32, some, 0, unroll=4)

        pipe(
            body,
            count // TILE,
            [tall(D)],
            [tall(D)] * 3,
            [ref.at[rows] for ref in (self.x, self.n1, self.n2, self.xhat)],
        )

    def attend(self, seq):
        scale = 1.0 / math.sqrt(HEAD_DIM)
        length = self.length

        def project(q_refs, n1, qkv, g, dense):
            at = pl.ds(pl.multiple_of(pl.program_id(0) * TILE, TILE), TILE)
            cosine, sine = self.cos[at, :], self.sin[at, :]
            wide = jnp.dot(n1[...], qkv[...], preferred_element_type=F32) + self.qkv_bias[...]
            q_refs[0][at, :] = rotate(wide[:, :HEAD_W], cosine, sine).astype(BF)
            q_refs[1][at, :] = rotate(wide[:, HEAD_W : 2 * HEAD_W], cosine, sine).astype(BF)
            q_refs[2][at, :] = wide[:, 2 * HEAD_W :].astype(BF)
            q_refs[3][at, :] = lax.dot_general(g[...], dense[...], NT, preferred_element_type=F32).astype(BF)

        def one(q_ref, k_ref, v_ref, d_att_ref, k_total, v_total):
            base = seq * length
            rows = pl.ds(base, length)
            pipe(
                functools.partial(project, (q_ref, k_ref, v_ref, d_att_ref)),
                length // TILE,
                [tall(D), fixed(D, 3 * HEAD_W), tall(D), fixed(HEAD_W, D)],
                [],
                (self.n1.at[rows], self.qkv, self.g.at[rows], self.dense),
            )
            k_total[...] = jnp.zeros_like(k_total)
            v_total[...] = jnp.zeros_like(v_total)
            for i in range(length // TILE):
                seen = (i + 1) * TILE
                here = pl.ds(i * TILE, TILE)
                there = pl.ds(base + i * TILE, TILE)
                q, d_att = q_ref[here, :], d_att_ref[here, :]
                k, v = k_ref[:seen, :], v_ref[:seen, :]
                scores = lax.dot_general(q, k, NT, preferred_element_type=F32) * scale
                row = lax.broadcasted_iota(jnp.int32, scores.shape, 0) + i * TILE
                column = lax.broadcasted_iota(jnp.int32, scores.shape, 1)
                scores = jnp.where(row >= column, scores, MASKED)
                grown = jnp.exp(scores - jnp.max(scores, axis=1, keepdims=True))
                prob = grown * (1.0 / jnp.sum(grown, axis=1, keepdims=True))
                prob_low = prob.astype(BF)
                self.att[there, :] = jnp.dot(prob_low, v, preferred_element_type=F32).astype(BF)
                d_prob = lax.dot_general(d_att, v, NT, preferred_element_type=F32)
                inner = jnp.sum(d_prob * prob, axis=1, keepdims=True)
                d_scores = (prob * (d_prob - inner)).astype(BF)
                d_q = jnp.dot(d_scores, k, preferred_element_type=F32) * scale
                d_q = rotate_back(d_q, self.cos[here, :], self.sin[here, :]).astype(BF)
                self.d_proj[there, :HEAD_W] = d_q
                k_total[:seen, :] += lax.dot_general(d_scores, q, TN, preferred_element_type=F32)
                v_total[:seen, :] += lax.dot_general(prob_low, d_att, TN, preferred_element_type=F32)
            for i in range(length // TILE):
                here = pl.ds(i * TILE, TILE)
                there = pl.ds(base + i * TILE, TILE)
                d_k = rotate_back(k_total[here, :] * scale, self.cos[here, :], self.sin[here, :])
                self.d_proj[there, HEAD_W : 2 * HEAD_W] = d_k.astype(BF)
                self.d_proj[there, 2 * HEAD_W :] = v_total[here, :].astype(BF)
                column_sums(self.qkv_total, self.d_proj[there, :].astype(F32))

        low, wide = pltpu.VMEM((length, HEAD_W), BF), pltpu.VMEM((length, HEAD_W), F32)
        pl.run_scoped(one, low, low, low, low, wide, wide)

    def dense_gradient(self):
        def body(g, part):
            part[...] = lax.dot_general(self.att[...], g[...], TN, preferred_element_type=F32).astype(BF)

        pipe(body, D // 512, [slim(self.tokens, 512)], [slim(HEAD_W, 512)], (self.g, self.dn_part))

    def qkv_gradient(self):
        def body(n1, part):
            part[...] = lax.dot_general(n1[...], self.d_proj[...], TN, preferred_element_type=F32).astype(BF)

        pipe(body, D // TILE, [slim(self.tokens)], [tall(3 * HEAD_W)], (self.n1, self.qk_part))

    def back_one(self):
        def body(qkv, xh, part):
            at = pl.ds(pl.multiple_of(pl.program_id(0) * TILE, TILE), TILE)
            d_n = lax.dot_general(self.d_proj[at, :], qkv[...], NT, preferred_element_type=F32)
            part[...] = (d_n * self.vec[0:1, :]).astype(BF)
            column_sums(self.bias1, d_n)
            column_sums(self.gain1, d_n * xh[...].astype(F32))

        pipe(body, self.tiles, [fixed(D, 3 * HEAD_W), tall(D)], [tall(D)], (self.qkv, self.xhat, self.s1))

    def expand(self):
        def body(n2, up, hidden, slope):
            pre = jnp.dot(n2[...], up[...], preferred_element_type=F32) + self.up_bias[...]
            value, rise = gelu_parts(pre)
            hidden[...] = value.astype(BF)
            slope[...] = rise.astype(BF)

        pipe(
            body,
            self.tiles,
            [tall(D), fixed(D, HID_W)],
            [tall(HID_W)] * 2,
            (self.n2, self.up, self.hidden, self.slope),
        )

    def down_gradient(self):
        def body(g, hidden, part):
            part[...] = lax.dot_general(g[...], hidden[...], TN, preferred_element_type=F32).astype(BF)

        pipe(
            body,
            D // TILE,
            [slim(self.tokens), fixed(self.tokens, HID_W)],
            [tall(HID_W)],
            (self.g, self.hidden, self.wt_part),
        )

    def contract_back(self):
        def body(g, wt, slope, d_pre):
            d_hidden = jnp.dot(g[...], wt[...], preferred_element_type=F32)
            low = (d_hidden * slope[...].astype(F32)).astype(BF)
            d_pre[...] = low
            column_sums(self.up_total, low.astype(F32))

        pipe(
            body,
            self.tiles,
            [tall(D), fixed(D, HID_W), tall(HID_W)],
            [tall(HID_W)],
            (self.g, self.wt, self.slope, self.d_pre),
        )

    def up_gradient(self):
        def body(n2, d_pre, part):
            part[...] = lax.dot_general(n2[...], d_pre[...], TN, preferred_element_type=F32).astype(BF)

        pipe(
            body,
            D // TILE,
            [slim(self.tokens), fixed(self.tokens, HID_W)],
            [tall(HID_W)],
            (self.n2, self.d_pre, self.up_part),
        )

    def back_two(self):
        def body(d_pre, up, xh, s1, part):
            d_n = lax.dot_general(d_pre[...], up[...], NT, preferred_element_type=F32)
            part[...] = (s1[...].astype(F32) + d_n * self.vec[2:3, :]).astype(BF)
            column_sums(self.bias2, d_n)
            column_sums(self.gain2, d_n * xh[...].astype(F32))

        pipe(
            body,
            self.tiles,
            [tall(HID_W), fixed(D, HID_W), tall(D), tall(D)],
            [tall(D)],
            (self.d_pre, self.up, self.xhat, self.s1, self.tok_parts),
        )

    def output(self):
        def body(hidden, dense, wt, part):
            at = pl.ds(pl.multiple_of(pl.program_id(0) * TILE, TILE), TILE)
            total = jnp.dot(self.att[at, :], dense[...], preferred_element_type=F32)
            total = total + lax.dot_general(hidden[...], wt[...], NT, preferred_element_type=F32)
            part[...] = total.astype(BF)

        pipe(
            body,
            self.tiles,
            [tall(HID_W), fixed(HEAD_W, D), fixed(D, HID_W)],
            [tall(D)],
            (self.hidden, self.dense, self.wt, self.out_parts),
        )


def any_spec(count):
    return [pl.BlockSpec(memory_space=pl.ANY)] * count


def slots_needed(n_zero):
    return 20 * n_zero + 120


INPUTS = ("x_own", "g_own", "dn_low", "qk_low", "up_low", "wt_low", "vec_own", "out_bias", "cos", "sin")
RESULTS = ("out_sum", "tok_sum", "dn_home", "qk_home", "up_home", "wt_home", "vec_all", "vec_sums")
TOTALS = (("gain1", D), ("bias1", D), ("gain2", D), ("bias2", D), ("qkv_total", 3 * HEAD_W), ("up_total", HID_W))
WIDTHS = (HEAD_W, 3 * HEAD_W, HID_W, HID_W)


def buffers(tokens):
    square = ("x", "g", "n1", "n2", "xhat", "s1", "tok_parts", "out_parts")
    shapes = {name: (tokens, D) for name in square}
    shapes.update({name: (tokens, HID_W) for name in ("hidden", "slope", "d_pre")})
    shapes.update(dense=(HEAD_W, D), dn_part=(HEAD_W, D), dn_all=(D, HEAD_W), dn_cols=(D, HEAD_W))
    shapes.update(qkv=(D, 3 * HEAD_W), qk_part=(D, 3 * HEAD_W))
    shapes.update({name: (D, HID_W) for name in ("up", "wt", "up_part", "wt_part")})
    return shapes


VEC_ROWS = 16
CHUNK = 128


class VectorGather:
    def __init__(self, wire, place, own, whole):
        self.wire, self.place, self.own, self.whole = wire, place, own, whole
        self.slots = [wire.slot() for _ in range(1, N_SEQ)]
        self.line = LineGather(wire, place, whole, N_SEQ)

    def target(self, s):
        return self.whole.at[pl.ds(self.place.z * N_SEQ + s, 1)]

    def start(self, local_sem):
        p = self.place
        for step in range(1, N_SEQ):
            self.wire.send(self.slots[step - 1], self.own, self.target(p.s), {"seq": lax.rem(p.s + step, N_SEQ)})
        self.copied = pltpu.make_async_copy(self.own, self.target(p.s), local_sem)
        self.copied.start()

    def wait(self):
        p = self.place
        for step in range(1, N_SEQ):
            source = lax.rem(p.s - step + N_SEQ, N_SEQ)
            self.wire.receive(self.slots[step - 1], self.target(source), {"seq": source})
        self.copied.wait()


def lay_out_vectors(layer, place):
    rows = layer.vec_all.shape[1]


    def piece(q):
        shard, row = (q // rows, q % rows) if isinstance(q, int) else (lax.div(q, rows), lax.rem(q, rows))
        return layer.vec_all[shard, pl.ds(row, 1), :]

    count = D // CHUNK
    for row, first in enumerate((0, count, 6 * count, 7 * count)):
        for i in range(count):
            layer.vec[row : row + 1, i * CHUNK : (i + 1) * CHUNK] = piece(first + i)
    each = HEAD_W // CHUNK
    for t in range(3):
        for i in range(each):
            at = t * HEAD_W + i * CHUNK
            layer.qkv_bias[:, at : at + CHUNK] = piece((2 + t) * count + place.part * each + i)
    each = HID_W // CHUNK
    for i in range(each):
        layer.up_bias[:, i * CHUNK : (i + 1) * CHUNK] = piece(8 * count + place.part * each + i)


def partial_vectors(layer):
    fold = lambda total: jnp.sum(total[...], axis=0, keepdims=True)
    rows = [fold(total) for total in (layer.gain1, layer.bias1, layer.gain2, layer.bias2)]
    rows.append(layer.out_bias[...])
    wide = jnp.concatenate(rows + [jnp.zeros((3, D), F32)], axis=0)
    for c in range(PARTS):
        layer.pieces_out[c] = wide[:, c * HEAD_W : (c + 1) * HEAD_W]


def own_vectors(layer, own):
    total = layer.pieces_in[0]
    for c in range(1, PARTS):
        total = total + layer.pieces_in[c]
    own[pl.ds(0, 8), :] = total
    qkv = jnp.sum(layer.qkv_total[...], axis=0, keepdims=True)
    up = jnp.sum(layer.up_total[...], axis=0, keepdims=True)
    cut = lambda row, count: [row[:, i * HEAD_W : (i + 1) * HEAD_W] for i in range(count)]
    rows = cut(qkv, 3) + cut(up, 4) + [jnp.zeros((1, HEAD_W), F32)]
    own[pl.ds(8, 8), :] = jnp.concatenate(rows, axis=0)


def layer_body(n_zero, rows, tokens, *refs):
    names = INPUTS + RESULTS + tuple(buffers(tokens))
    names += ("att", "d_proj", "send_sems", "recv_sems", "local_sems", "own", "total")
    names += ("vec", "qkv_bias", "up_bias", "pieces_out", "pieces_in", "vec_line", "vec_total")
    names += tuple(name for name, _ in TOTALS)
    held = dict(zip(names, refs))
    scratch = list(refs[len(names) :])
    take = lambda count: [scratch.pop(0) for _ in range(count)]
    layer = Layer(held)
    place = Place(n_zero)
    wire = Wire(layer.send_sems, layer.recv_sems)
    local = lambda index: layer.local_sems.at[index]
    block = rows * N_SEQ
    chunk = lambda c: pl.ds(pl.multiple_of(c * HEAD_W, HEAD_W), HEAD_W)

    sources = (layer.dn_low, layer.qk_low, layer.up_low, layer.wt_low)
    wholes = (layer.dn_all, layer.qkv, layer.up, layer.wt)
    exchanges = [SeqExchange(wire, place, low, whole, rows) for low, whole in zip(sources, wholes)]
    dn, qk, up, wt = [LineGather(wire, place, whole, block) for whole in wholes]
    x = PlaneGather(wire, place, layer.x_own, layer.x)
    g = PlaneGather(wire, place, layer.g_own, layer.g)
    dense_in = DenseExchange(
        wire, place, lambda c: layer.dn_all.at[chunk(c)], lambda c: layer.dense.at[:, chunk(c)]
    )
    dense_out = DenseExchange(
        wire, place, lambda c: layer.dn_part.at[:, chunk(c)], lambda c: layer.dn_cols.at[chunk(c)]
    )
    planes = []
    for k, parts in enumerate((layer.out_parts, layer.tok_parts)):
        mate, far, across, turned = take(4)
        planes.append(
            PlaneScatter(wire, place, parts, mate, far, across, turned, layer.total, layer.own, local(k))
        )
    out, tok = planes
    sums, homes = [], []
    parts = (layer.dn_cols, layer.qk_part, layer.up_part, layer.wt_part)
    results = (layer.dn_home, layer.qk_home, layer.up_home, layer.wt_home)
    for k, width in enumerate(WIDTHS):
        ring, total = take(2)
        own = take(1)[0]
        sums.append(LineScatter(wire, place, parts[k], ring, total, own, block, local(2 + k)))
        homes.append(Home(wire, place, total, results[k], rows))
    dn_sum, qk_sum, up_sum, wt_sum = sums

    def finish(k):
        sums[k].last()
        homes[k].start(local(6 + k))

    def store(scatter, result):
        scatter.last()
        copy = pltpu.make_async_copy(scatter.total, result, scatter.sem)
        copy.start()
        copy.wait()

    alone = layer.vec_all.shape[0] == 1
    gather = None if alone else VectorGather(wire, place, layer.vec_own, layer.vec_all)

    def vector_in_start():
        if not alone:
            gather.start(local(18))

    def vector_in_pass():
        if not alone:
            gather.wait()
            gather.line.own_from_ends()
            gather.line.own_from_middle()

    def vector_in_rest():
        if alone:
            copy = pltpu.make_async_copy(layer.vec_own, layer.vec_all, local(18))
            copy.start()
            copy.wait()
        else:
            for step in range(1, n_zero):
                gather.line.ahead(step)
        lay_out_vectors(layer, place)

    pieces = DenseExchange(
        wire, place, lambda c: layer.pieces_out.at[c], lambda c: layer.pieces_in.at[c]
    )
    vector_line = LineGather(wire, place, layer.vec_line, VEC_ROWS)
    vector_spread = DenseExchange(
        wire, place, lambda c: layer.vec_total, lambda c: layer.vec_sums.at[c]
    )

    def vector_out_start():
        partial_vectors(layer)
        pieces.start(local(18))

    def vector_out_pass():
        pieces.wait()
        own = vector_line.block(place.z)
        own_vectors(layer, own)
        vector_line.own_from_ends()
        vector_line.own_from_middle()

    def vector_out_spread():
        total = layer.vec_line[pl.ds(0, VEC_ROWS), :]
        for j in range(1, n_zero):
            total = total + layer.vec_line[pl.ds(j * VEC_ROWS, VEC_ROWS), :]
        layer.vec_total[...] = total
        vector_spread.start(local(19))

    place.barrier()
    layer.clear()
    exchanges[0].start(local(12))
    vector_in_start()
    exchanges[2].start(local(14))
    x.start(local(10))
    exchanges[0].wait()
    dn.own_from_ends()
    dn.own_from_middle()
    vector_in_pass()
    dn.ahead(1)
    exchanges[2].wait()
    up.own_from_ends()
    exchanges[1].start(local(13))
    up.own_from_middle()
    dn.ahead(2)
    x.turn()
    g.start(local(11))
    up.ahead(1)
    exchanges[3].start(local(15))
    vector_in_rest()
    x.turn_again()
    up.ahead(2)
    x.wait()
    layer.normalise(0, 2)
    exchanges[1].wait()
    qk.own_from_ends()
    qk.own_from_middle()
    for step in range(3, n_zero):
        dn.ahead(step)
    layer.normalise(1, 2)
    g.turn()
    for step in range(3, n_zero):
        up.ahead(step)
    layer.expand()
    exchanges[3].wait()
    wt.own_from_ends()
    qk.ahead(1)
    g.turn_again()
    g.wait()
    layer.down_gradient()
    dense_in.start(local(16))
    qk.ahead(2)
    wt_sum.launch(0)
    for step in range(3, n_zero):
        qk.ahead(step)
    wt.own_from_middle()
    dense_in.wait()
    layer.attend(0)
    wt_sum.launch(1)
    wt.ahead(1)
    wt_sum.launch(2)
    layer.attend(1)
    wt_sum.advance(1)
    layer.qkv_gradient()
    layer.dense_gradient()
    qk_sum.launch(0)
    qk_sum.launch(1)
    wt.ahead(2)
    qk_sum.launch(2)
    dense_out.start(local(17))
    layer.back_one()
    for step in range(3, n_zero):
        wt.ahead(step)
    dense_out.wait()
    wt_sum.advance(2)
    layer.contract_back()
    layer.output()
    dn_sum.launch(0)
    out.start()
    finish(3)
    layer.up_gradient()
    up_sum.launch(0)
    out.turn()
    qk_sum.advance(1)
    dn_sum.launch(1)
    layer.back_two()
    up_sum.launch(1)
    out.turn_again()
    homes[3].wait()
    dn_sum.advance(1)
    tok.start()
    qk_sum.advance(2)
    tok.turn()
    vector_out_start()
    dn_sum.launch(2)
    up_sum.advance(1)
    dn_sum.advance(2)
    tok.turn_again()
    up_sum.launch(2)
    up_sum.advance(2)
    store(out, layer.out_sum)
    vector_out_pass()
    finish(1)
    finish(0)
    store(tok, layer.tok_sum)
    finish(2)
    vector_line.ahead(1)
    for step in range(2, n_zero):
        vector_line.ahead(step)
    vector_out_spread()
    homes[2].wait()
    homes[0].wait()
    homes[1].wait()
    vector_spread.wait()
    wire.finish()


def layer_call(n_zero, rows, tokens, *operands):
    local = tokens // PARTS
    block = rows * N_SEQ
    slots = slots_needed(n_zero)
    shards = (9 * D + FF) // (operands[6].shape[1] * CHUNK)
    vmem = lambda *dims: pltpu.VMEM(dims, BF)
    scratch = [
        vmem(tokens, HEAD_W),
        vmem(tokens, 3 * HEAD_W),
        pltpu.SemaphoreType.DMA((slots,)),
        pltpu.SemaphoreType.DMA((slots,)),
        pltpu.SemaphoreType.DMA((20,)),
        vmem(local, D),
        pltpu.VMEM((local, D), F32),
    ]
    wide = lambda *dims: pltpu.VMEM(dims, F32)
    scratch += [wide(4, D), wide(1, 3 * HEAD_W), wide(1, HID_W), wide(PARTS, 8, HEAD_W)]
    scratch += [wide(PARTS, 8, HEAD_W), wide(n_zero * VEC_ROWS, HEAD_W), wide(VEC_ROWS, HEAD_W)]
    scratch += [wide(8, width) for _, width in TOTALS]
    for _ in range(2):
        scratch += [vmem(2, 2, local, D), vmem(local, D), vmem(local, D), vmem(local, D)]
    for width in WIDTHS:
        scratch += [vmem(n_zero + 1, block, width), vmem(block, width), vmem(block, width)]
    homes = [jax.ShapeDtypeStruct((N_DP, N_SEQ, rows, width), BF) for width in WIDTHS]
    anywhere = pl.BlockSpec(memory_space=pl.ANY)
    vector = pl.BlockSpec(memory_space=pltpu.VMEM)
    held = buffers(tokens)
    return pl.pallas_call(
        functools.partial(layer_body, n_zero, rows, tokens),
        in_specs=[anywhere] * 7 + [vector] * 3,
        out_specs=[anywhere] * (len(RESULTS) - 2) + [vector] * 2 + [anywhere] * len(held),
        out_shape=[jax.ShapeDtypeStruct((local, D), F32)] * 2
        + homes
        + [
            jax.ShapeDtypeStruct((shards,) + operands[6].shape[1:], F32),
            jax.ShapeDtypeStruct((PARTS, VEC_ROWS, HEAD_W), F32),
        ]
        + [jax.ShapeDtypeStruct(shape, BF) for shape in held.values()],
        scratch_shapes=scratch,
        compiler_params=pltpu.CompilerParams(
            collective_id=0, has_side_effects=True, vmem_limit_bytes=62 * 1024 * 1024
        ),
        name="layer",
    )(*operands)


def adam_body(decay, flipped, home, param, first, second, new, first_new, second_new, grad_out):
    if flipped:
        gradient = home[0, 0].astype(F32).T
    else:
        gradient = jnp.concatenate([home[0, k] for k in range(home.shape[1])], axis=1).astype(F32)
    updated = adam_step(param[...], gradient, first[...], second[...], decay)
    new[...], first_new[...], second_new[...] = updated
    grad_out[...] = gradient


def adam(home, pieces, param, first, second):
    rows, width = home.shape[2], home.shape[3] // pieces
    together = max(1, min(N_SEQ, HID_W // width))
    groups = PARTS // together
    block = pl.BlockSpec((rows, width * together), lambda c, t: (0, t * groups + c))
    each = N_SEQ // together
    return pl.pallas_call(
        functools.partial(adam_body, WEIGHT_DECAY, False),
        grid=(groups, pieces),
        in_specs=[
            pl.BlockSpec((1, together, rows, width), lambda c, t: (c // each, c % each, 0, t)),
            block,
            block,
            block,
        ],
        out_specs=[block] * 4,
        out_shape=[jax.ShapeDtypeStruct(param.shape, F32)] * 4,
        compiler_params=pltpu.CompilerParams(vmem_limit_bytes=48 * 1024 * 1024),
        name="adam",
    )(home, param, first, second)


def adam_pair_body(decay, *refs):
    adam_body(decay, False, *refs[0:4], *refs[8:12])
    adam_body(decay, True, *refs[4:8], *refs[12:16])


def adam_pair(up_home, up, wt_home, down):
    rows, width = up_home.shape[2:]
    home = pl.BlockSpec((1, 1, rows, width), lambda c: (c // N_SEQ, c % N_SEQ, 0, 0))
    columns = pl.BlockSpec((rows, width), lambda c: (0, c))
    tall_rows = pl.BlockSpec((width, rows), lambda c: (c, 0))
    results = pl.pallas_call(
        functools.partial(adam_pair_body, WEIGHT_DECAY),
        grid=(PARTS,),
        in_specs=[home] + [columns] * 3 + [home] + [tall_rows] * 3,
        out_specs=[columns] * 4 + [tall_rows] * 4,
        out_shape=[jax.ShapeDtypeStruct(up[0].shape, F32)] * 4 + [jax.ShapeDtypeStruct(down[0].shape, F32)] * 4,
        compiler_params=pltpu.CompilerParams(vmem_limit_bytes=56 * 1024 * 1024),
        name="adam_pair",
    )(up_home, *up, wt_home, *down)
    return results[:4], results[4:]


def pack_body(half, *refs):
    dense, query, key, value, up, down, dn_low, qk_low, up_low, wt_low = refs
    dn_low[0] = dense[...].astype(BF)
    qk_low[0] = jnp.concatenate([query[...], key[...], value[...]], axis=1).astype(BF)
    up_low[0] = up[...].astype(BF)
    wt_low[0] = down[...].T.astype(BF)


def pack(half, qkv_weight, dense_weight, up_weight, down_weight):
    rows = qkv_weight.shape[0]
    columns = lambda width, t: pl.BlockSpec((rows, width), lambda s, h: (0, t * PARTS + h[0] * N_SEQ + s))
    widths = (HEAD_W, 3 * HEAD_W, HID_W, HID_W)
    return pl.pallas_call(
        pack_body,
        grid_spec=pltpu.PrefetchScalarGridSpec(
            num_scalar_prefetch=1,
            grid=(N_SEQ,),
            in_specs=[columns(HEAD_W, 0)]
            + [columns(HEAD_W, t) for t in range(3)]
            + [columns(HID_W, 0), pl.BlockSpec((HID_W, rows), lambda s, h: (h[0] * N_SEQ + s, 0))],
            out_specs=[pl.BlockSpec((1, rows, width), lambda s, h: (s, 0, 0)) for width in widths],
        ),
        out_shape=[jax.ShapeDtypeStruct((N_SEQ, rows, width), BF) for width in widths],
        compiler_params=pltpu.CompilerParams(vmem_limit_bytes=48 * 1024 * 1024),
        name="pack",
    )(half, dense_weight, qkv_weight, qkv_weight, qkv_weight, up_weight, down_weight)


def rotary_rows(length):
    exponent = np.arange(ROT // 2, dtype=np.float32) * np.float32(2.0 / ROT)
    inverse = np.power(np.float32(10000.0), -exponent)
    angles = np.arange(length, dtype=np.float32)[:, None] * inverse[None, :]
    cosine, sine = np.cos(angles), np.sin(angles)
    ones = np.ones((length, 128 - ROT), np.float32)
    cosine = np.concatenate([cosine, cosine, ones], axis=1)
    sine = np.concatenate([-sine, sine, 0.0 * ones], axis=1)
    return jnp.asarray(cosine), jnp.asarray(sine)


def make_body(sizes):
    n_zero = sizes["zero"]
    everywhere = ("dp", "zero", "seq")

    def body(
        inputs,
        out_grad,
        vectors,
        qkv_weight,
        dense_weight,
        up_weight,
        down_weight,
        vectors_first,
        qkv_first,
        dense_first,
        up_first,
        down_first,
        vectors_second,
        qkv_second,
        dense_second,
        up_second,
        down_second,
    ):
        dp_i, zero_i, seq_i = (lax.axis_index(axis) for axis in everywhere)
        seqs_here, local_len = inputs.shape[0], inputs.shape[1]
        token_rows = seqs_here * local_len
        rows = qkv_weight.shape[0]

        dn_low, qk_low, up_low, wt_low = pack(
            dp_i.astype(jnp.int32).reshape(1), qkv_weight, dense_weight, up_weight, down_weight
        )
        tokens_low = inputs.reshape(token_rows, D)
        grad_low = out_grad.reshape(token_rows, D)
        tokens = N_DP * N_SEQ * token_rows
        grad_wide = grad_low.astype(F32)
        d_out_bias = jnp.sum(grad_wide, axis=0, keepdims=True)
        vec_low = lax.reduce_precision(vectors, exponent_bits=8, mantissa_bits=7)
        if vectors.shape[0] % CHUNK == 0:
            vec_low = vec_low.reshape(1, -1, CHUNK)
        else:
            vec_low = lax.all_gather(vec_low, ("zero", "seq"), axis=0, tiled=True).reshape(1, -1, CHUNK)
        results = layer_call(
            n_zero,
            rows,
            tokens,
            tokens_low,
            grad_low,
            dn_low,
            qk_low,
            up_low,
            wt_low,
            vec_low,
            d_out_bias,
            *rotary_rows(tokens // N_DP),
        )
        out_sum, d_xhat, dn_home, qk_home, up_home, wt_home, vec_all, vec_sums = results[: len(RESULTS)]
        vec_flat = vec_all.reshape(-1)
        dense_bias, down_bias = vec_flat[5 * D : 6 * D], vec_flat[8 * D + FF : 9 * D + FF]

        def statistics(values):
            average = jnp.mean(values, axis=-1, keepdims=True)
            centred = values - average
            spread = jnp.mean(centred * centred, axis=-1, keepdims=True)
            return centred, lax.rsqrt(spread + NORM_EPSILON)

        tokens_wide = tokens_low.astype(F32)
        outputs = (tokens_wide + out_sum + dense_bias + down_bias).astype(BF).reshape(inputs.shape)
        centred_own, rate_own = statistics(tokens_wide)
        xhat_own = centred_own * rate_own
        d_tokens = rate_own * (
            d_xhat
            - jnp.mean(d_xhat, axis=-1, keepdims=True)
            - xhat_own * jnp.mean(d_xhat * xhat_own, axis=-1, keepdims=True)
        )
        input_grad = (grad_wide + d_tokens).astype(BF).reshape(inputs.shape)

        row = lambda k: vec_sums[:, k].reshape(-1)
        vector_sum = jnp.concatenate(
            [
                row(0),
                row(1),
                vec_sums[:, 8:11].transpose(1, 0, 2).reshape(-1),
                row(4),
                row(2),
                row(3),
                vec_sums[:, 11:15].reshape(-1),
                row(4),
            ]
        )
        vectors_grad = lax.dynamic_slice_in_dim(
            vector_sum, (zero_i * N_SEQ + seq_i) * vectors.shape[0], vectors.shape[0], 0
        )

        vec_upd = adam_step(vectors, vectors_grad, vectors_first, vectors_second, 0.0) + (vectors_grad,)
        qkv_upd = adam(qk_home, 3, qkv_weight, qkv_first, qkv_second)
        dense_upd = adam(dn_home, 1, dense_weight, dense_first, dense_second)
        up_upd, down_upd = adam_pair(
            up_home,
            (up_weight, up_first, up_second),
            wt_home,
            (down_weight, down_first, down_second),
        )
        updates = (vec_upd, qkv_upd, dense_upd, up_upd, down_upd)
        picked = lambda k: tuple(update[k] for update in updates)
        return (outputs, input_grad) + picked(3) + picked(0) + picked(1) + picked(2)

    return body


def solution(mesh):
    wide = P(("dp", "zero"), "seq", None)
    vector = P(("zero", "seq"))
    rows = P(("zero", "seq"), None)
    columns = P(None, ("zero", "seq"))
    state = (vector, rows, rows, rows, columns)
    return jax.shard_map(
        make_body(dict(mesh.shape)),
        mesh=mesh,
        in_specs=(wide, wide) + state * 3,
        out_specs=(wide, wide) + state * 4,
        check_vma=False,
    )
```

```python
import functools
import math

import jax
import jax.numpy as jnp
import numpy as np
from jax import lax
from jax.experimental import pallas as pl
from jax.experimental.pallas import tpu as pltpu
from jax.sharding import PartitionSpec as P

D = 2048
HEADS = 8
HEAD_DIM = 256
FF = 8192
ROT = 64
ADAM_STEP = 4

BETA_ONE = 0.9
BETA_TWO = 0.95
LEARN_RATE = 0.5
EPSILON = 1e-08
WEIGHT_DECAY = 0.1
NORM_EPSILON = 1e-05
MASKED = -1e30
N_DP = 2
N_SEQ = 4
PARTS = N_DP * N_SEQ
HEAD_W = D // PARTS
HID_W = FF // PARTS
BF = jnp.bfloat16
F32 = jnp.float32
NT = (((1,), (1,)), ((), ()))
TN = (((0,), (0,)), ((), ()))


def adam_step(parameter, gradient, first_moment, second, decay_rate):
    first_new = BETA_ONE * first_moment + (1.0 - BETA_ONE) * gradient
    second_new = BETA_TWO * second + (1.0 - BETA_TWO) * gradient * gradient
    first_hat = first_new / (1.0 - BETA_ONE**ADAM_STEP)
    second_hat = second_new / (1.0 - BETA_TWO**ADAM_STEP)
    param_new = parameter - LEARN_RATE * (
        first_hat / (jnp.sqrt(second_hat) + EPSILON) + decay_rate * parameter
    )
    return (param_new, first_new, second_new)


class Wire:
    def __init__(self, send_sems, recv_sems):
        self.send_sems, self.recv_sems, self.used = send_sems, recv_sems, 0
        self.sent = []

    def slot(self):
        self.used += 1
        return self.used - 1

    def copy(self, slot, source, target, device):
        return pltpu.make_async_remote_copy(
            src_ref=source,
            dst_ref=target,
            send_sem=self.send_sems.at[slot],
            recv_sem=self.recv_sems.at[slot],
            device_id=device,
            device_id_type=pl.DeviceIdType.MESH,
        )

    def send(self, slot, source, target, device, when=None):
        copy = self.copy(slot, source, target, device)
        guarded(when, copy.start)
        self.sent.append((copy, when))

    def receive(self, slot, target, device, when=None):
        copy = self.copy(slot, target, target, device)
        guarded(when, copy.wait_recv)

    def finish(self):
        for copy, when in self.sent:
            guarded(when, copy.wait_send)
        self.sent = []


def guarded(when, action):
    if when is None:
        action()
    else:
        pl.when(when)(action)


class Place:
    def __init__(self, n_zero):
        self.n = n_zero
        self.dp, self.z, self.s = (lax.axis_index(a) for a in ("dp", "zero", "seq"))
        flip = lambda value, bit: jnp.bitwise_xor(value, bit)
        self.dp_far, self.s_far, self.s_core = 1 - self.dp, flip(self.s, 2), flip(self.s, 1)
        self.s_both = flip(self.s, 3)
        self.across = {"dp": self.dp_far}
        self.far = {"seq": self.s_far}
        self.core = {"seq": self.s_core}
        self.above, self.below = {"zero": self.z + 1}, {"zero": self.z - 1}
        self.part = self.dp * N_SEQ + self.s

    def others(self):
        for step in range(1, N_DP * N_SEQ):
            at = lax.rem(self.part + step, N_DP * N_SEQ)
            dp, s = lax.div(at, N_SEQ), lax.rem(at, N_SEQ)
            yield step, dp, s, {"dp": dp, "seq": s}

    def barrier(self):
        gate = pltpu.get_barrier_semaphore()
        signal = lambda device: pl.semaphore_signal(
            gate, inc=1, device_id=device, device_id_type=pl.DeviceIdType.MESH
        )
        for _, _, _, device in self.others():
            signal(device)
        pl.when(self.z < self.n - 1)(lambda: signal(self.above))
        pl.when(self.z > 0)(lambda: signal(self.below))
        ends = (self.z < self.n - 1).astype(jnp.int32) + (self.z > 0).astype(jnp.int32)
        pl.semaphore_wait(gate, N_DP * N_SEQ - 1 + ends)


class LineGather:
    def __init__(self, wire, place, whole, rows):
        self.wire, self.place, self.whole, self.rows = wire, place, whole, rows
        self.ups = [wire.slot() for _ in range(place.n - 1)]
        self.downs = [wire.slot() for _ in range(place.n - 1)]

    def block(self, index):
        return self.whole.at[pl.ds(pl.multiple_of(index * self.rows, self.rows), self.rows)]

    def send_up(self, step, block, when):
        self.wire.send(self.ups[step - 1], block, block, self.place.above, when)

    def send_down(self, step, block, when):
        self.wire.send(self.downs[step - 1], block, block, self.place.below, when)

    def own_from_ends(self):
        p = self.place
        self.send_up(1, self.block(p.z), p.z == 0)
        self.send_down(1, self.block(p.z), p.z == p.n - 1)

    def own_from_middle(self):
        p = self.place
        middle = (p.z > 0) & (p.z < p.n - 1)
        self.send_up(1, self.block(p.z), middle)
        self.send_down(1, self.block(p.z), middle)

    def ahead(self, step):
        p = self.place
        up, down = self.block(jnp.maximum(p.z - step, 0)), self.block(jnp.minimum(p.z + step, p.n - 1))
        self.wire.receive(self.ups[step - 1], up, p.below, p.z >= step)
        if step + 1 < p.n:
            self.send_up(step + 1, up, (p.z < p.n - 1) & (p.z >= step))
        self.wire.receive(self.downs[step - 1], down, p.above, p.z + step < p.n)
        if step + 1 < p.n:
            self.send_down(step + 1, down, (p.z > 0) & (p.z + step < p.n))


class SeqExchange:
    def __init__(self, wire, place, send, whole, rows):
        self.wire, self.place, self.out, self.whole, self.rows = wire, place, send, whole, rows
        self.slots = [wire.slot() for _ in range(1, N_SEQ)]

    def target(self, s):
        row = (self.place.z * N_SEQ + s) * self.rows
        return self.whole.at[pl.ds(pl.multiple_of(row, self.rows), self.rows)]

    def start(self, local_sem):
        p = self.place
        for step in range(1, N_SEQ):
            to = lax.rem(p.s + step, N_SEQ)
            self.wire.send(self.slots[step - 1], self.out.at[to], self.target(p.s), {"seq": to})
        own = pltpu.make_async_copy(self.out.at[p.s], self.target(p.s), local_sem)
        own.start()
        self.own = own

    def wait(self):
        p = self.place
        for step in range(1, N_SEQ):
            source = lax.rem(p.s - step + N_SEQ, N_SEQ)
            self.wire.receive(self.slots[step - 1], self.target(source), {"seq": source})
        self.own.wait()


class PlaneGather:
    def __init__(self, wire, place, block, whole):
        self.wire, self.place, self.own, self.whole = wire, place, block, whole
        self.slots = {name: wire.slot() for name in ("far", "across", "both0", "both1", "c0", "c1", "c2", "c3")}
        self.rows = block.shape[0]
        self.half = self.rows // 2

    def at(self, dp, s):
        row = (dp * N_SEQ + s) * self.rows
        return self.whole.at[pl.ds(pl.multiple_of(row, self.rows), self.rows)]

    def start(self, local_sem):
        p, w, slots = self.place, self.wire, self.slots
        mine = self.at(p.dp, p.s)
        w.send(slots["far"], self.own, mine, p.far)
        w.send(slots["across"], self.own, mine, p.across)
        w.send(slots["c0"], self.own, mine, p.core)
        self.copied = pltpu.make_async_copy(self.own, mine, local_sem)
        self.copied.start()

    def turn(self):
        p, w, slots, h = self.place, self.wire, self.slots, self.half
        far, across = self.at(p.dp, p.s_far), self.at(p.dp_far, p.s)
        w.receive(slots["far"], far, p.far)
        w.send(slots["both0"], far.at[pl.ds(0, h)], far.at[pl.ds(0, h)], p.across)
        w.send(slots["c1"], far, far, p.core)
        w.receive(slots["across"], across, p.across)
        w.send(slots["both1"], across.at[pl.ds(h, h)], across.at[pl.ds(h, h)], p.far)
        w.send(slots["c2"], across, across, p.core)

    def turn_again(self):
        p, w, slots, h = self.place, self.wire, self.slots, self.half
        both = self.at(p.dp_far, p.s_far)
        w.receive(slots["both0"], both.at[pl.ds(0, h)], p.across)
        w.receive(slots["both1"], both.at[pl.ds(h, h)], p.far)
        w.send(slots["c3"], both, both, p.core)

    def wait(self):
        p, w, slots = self.place, self.wire, self.slots
        w.receive(slots["c0"], self.at(p.dp, p.s_core), p.core)
        w.receive(slots["c1"], self.at(p.dp, p.s_both), p.core)
        w.receive(slots["c2"], self.at(p.dp_far, p.s_core), p.core)
        w.receive(slots["c3"], self.at(p.dp_far, p.s_both), p.core)
        self.copied.wait()


def add_rows(target, *sources):
    rows = target.shape[0]
    tile = 32 if rows % 32 == 0 else 16

    def one(i, carry):
        at = pl.ds(pl.multiple_of(i * tile, tile), tile)
        total = sources[0][at, :].astype(F32)
        for source in sources[1:]:
            total = total + source[at, :].astype(F32)
        target[at, :] = total.astype(target.dtype)
        return carry

    lax.fori_loop(0, rows // tile, one, 0)


class LineScatter:
    def __init__(self, wire, place, parts, held, total, own, rows, sem):
        self.wire, self.place, self.parts, self.rows = wire, place, parts, rows
        self.held, self.total, self.own, self.sem = held, total, own, sem
        self.launched, self.advanced = 0, 1
        self.up_slots = [wire.slot() for _ in range(place.n)]
        self.down_slots = [wire.slot() for _ in range(place.n)]

    def part(self, j):
        return self.parts.at[pl.ds(pl.multiple_of(j * self.rows, self.rows), self.rows)]

    def fetch(self, j, target):
        return pltpu.make_async_copy(self.part(j), target, self.sem)

    def launch(self, k):
        p = self.place
        top = p.n - 1
        up, down = top - k, k
        self.wire.send(
            self.up_slots[up], self.part(up), self.held.at[up + 1], p.above, p.z == 0
        )
        self.wire.send(
            self.down_slots[down], self.part(down), self.held.at[down], p.below, p.z == top
        )
        self.launched = k + 1

    def advance(self, k):
        p = self.place
        top = p.n - 1
        up = jnp.minimum(top - k + p.z, top)
        self.hop(up, up + 1, self.up_slots[0] + up, p.above, p.below, (p.z > 0) & (p.z <= k))
        down = jnp.maximum(k - top + p.z, 0)
        self.hop(down, down, self.down_slots[0] + down, p.below, p.above, (p.z < top) & (top - p.z <= k))
        self.advanced = k + 1

    def hop(self, j, index, slot, onto, source, active):
        held = self.held.at[index]

        def go():
            copy = self.fetch(j, self.own)
            copy.start()
            self.wire.receive(slot, held, source)
            copy.wait()
            add_rows(held, held, self.own)

        pl.when(active)(go)
        self.wire.send(slot, held, held, onto, active)

    def last(self):
        p = self.place
        for k in range(self.launched, p.n - 1):
            self.launch(k)
        for k in range(self.advanced, p.n - 1):
            self.advance(k)
        copy = self.fetch(p.z, self.own)
        copy.start()
        copy.wait()
        up, down = self.held.at[p.z + 1], self.held.at[p.z]

        @pl.when(p.z == 0)
        def _():
            self.arrive(down, self.down_slots, p.above)
            add_rows(self.total, self.own, down)

        @pl.when(p.z == p.n - 1)
        def _():
            self.arrive(up, self.up_slots, p.below)
            add_rows(self.total, self.own, up)

        @pl.when((p.z > 0) & (p.z < p.n - 1))
        def _():
            self.arrive(up, self.up_slots, p.below)
            self.arrive(down, self.down_slots, p.above)
            add_rows(self.total, self.own, up, down)

    def arrive(self, held, slots, source):
        self.wire.receive(slots[0] + self.place.z, held, source)


class Home:
    def __init__(self, wire, place, total, home, first, width, rows):
        self.wire, self.place, self.total, self.home, self.rows = wire, place, total, home, rows
        self.columns = pl.ds(first, width)
        self.slots = [wire.slot() for _ in range(1, N_DP * N_SEQ)]

    def target(self, dp, s):
        return self.home.at[dp, s, :, self.columns]

    def piece(self, s):
        return self.total.at[pl.ds(pl.multiple_of(s * self.rows, self.rows), self.rows)]

    def start(self, local_sem):
        p = self.place
        for step, dp, s, device in p.others():
            self.wire.send(self.slots[step - 1], self.piece(s), self.target(p.dp, p.s), device)
        self.copied = pltpu.make_async_copy(self.piece(p.s), self.target(p.dp, p.s), local_sem)
        self.copied.start()

    def wait(self):
        p = self.place
        parts = N_DP * N_SEQ
        for step in range(1, parts):
            at = lax.rem(p.part - step + parts, parts)
            dp, s = lax.div(at, N_SEQ), lax.rem(at, N_SEQ)
            self.wire.receive(self.slots[step - 1], self.target(dp, s), {"dp": dp, "seq": s})
        self.copied.wait()


class DenseExchange:
    def __init__(self, wire, place, source, target):
        self.wire, self.place, self.source, self.target = wire, place, source, target
        self.slots = [wire.slot() for _ in range(1, N_DP * N_SEQ)]

    def start(self, local_sem):
        p = self.place
        for step, dp, s, device in p.others():
            self.wire.send(self.slots[step - 1], self.source(dp * N_SEQ + s), self.target(p.part), device)
        self.copied = pltpu.make_async_copy(self.source(p.part), self.target(p.part), local_sem)
        self.copied.start()

    def wait(self):
        p = self.place
        parts = N_DP * N_SEQ
        for step in range(1, parts):
            at = lax.rem(p.part - step + parts, parts)
            device = {"dp": lax.div(at, N_SEQ), "seq": lax.rem(at, N_SEQ)}
            self.wire.receive(self.slots[step - 1], self.target(at), device)
        self.copied.wait()


class PlaneScatter:
    def __init__(self, wire, place, parts, mate, from_far, from_across, turned, total, own, sem):
        self.wire, self.place, self.parts, self.mate, self.sums = wire, place, parts, mate, mate
        self.from_far, self.from_across, self.turned = from_far, from_across, turned
        self.total, self.own, self.sem = total, own, sem
        self.rows = total.shape[0]
        self.half = self.rows // 2
        self.core_slots = [[wire.slot() for _ in range(2)] for _ in range(2)]
        names = ("turn_across", "turn_far", "far0", "far1", "across0", "across1")
        self.slots = {name: wire.slot() for name in names}

    def part(self, dp, s):
        row = (dp * N_SEQ + s) * self.rows
        return self.parts.at[pl.ds(pl.multiple_of(row, self.rows), self.rows)]

    def start(self):
        p = self.place
        core = lax.rem(p.s_core, 2)
        for dp in range(2):
            for y in range(2):
                self.wire.send(
                    self.core_slots[dp][y], self.part(dp, 2 * y + core), self.mate.at[dp, y], p.core
                )

    def combine(self, dp, y):
        p = self.place
        core = lax.rem(p.s, 2)
        for d in range(2):
            for v in range(2):

                @pl.when((dp == d) & (y == v))
                def _(d=d, v=v):
                    copy = pltpu.make_async_copy(self.part(d, 2 * v + core), self.own, self.sem)
                    copy.start()
                    self.wire.receive(self.core_slots[d][v], self.mate.at[d, v], p.core)
                    copy.wait()
                    add_rows(self.sums.at[d, v], self.own, self.mate.at[d, v])

    def turn(self):
        p, w, h, slots = self.place, self.wire, self.half, self.slots
        y = lax.div(p.s, 2)
        y_far = 1 - y
        low, high = pl.ds(0, h), pl.ds(h, h)
        self.combine(p.dp_far, y_far)
        both = self.sums.at[p.dp_far, y_far]
        w.send(slots["turn_across"], both.at[low], self.turned.at[low], p.across)
        w.send(slots["turn_far"], both.at[high], self.turned.at[high], p.far)
        self.combine(p.dp, y_far)
        far = self.sums.at[p.dp, y_far]
        w.send(slots["far1"], far.at[high], self.from_far.at[high], p.far)
        self.combine(p.dp_far, y)
        across = self.sums.at[p.dp_far, y]
        w.send(slots["across0"], across.at[low], self.from_across.at[low], p.across)
        self.combine(p.dp, y)

    def turn_again(self):
        p, w, h, slots = self.place, self.wire, self.half, self.slots
        y = lax.div(p.s, 2)
        low, high = pl.ds(0, h), pl.ds(h, h)
        far, across = self.sums.at[p.dp, 1 - y], self.sums.at[p.dp_far, y]
        w.receive(slots["turn_across"], self.turned.at[low], p.across)
        add_rows(far.at[low], far.at[low], self.turned.at[low])
        w.send(slots["far0"], far.at[low], self.from_far.at[low], p.far)
        w.receive(slots["turn_far"], self.turned.at[high], p.far)
        add_rows(across.at[high], across.at[high], self.turned.at[high])
        w.send(slots["across1"], across.at[high], self.from_across.at[high], p.across)

    def last(self):
        p, w, h, slots = self.place, self.wire, self.half, self.slots
        low, high = pl.ds(0, h), pl.ds(h, h)
        w.receive(slots["far1"], self.from_far.at[high], p.far)
        w.receive(slots["far0"], self.from_far.at[low], p.far)
        w.receive(slots["across0"], self.from_across.at[low], p.across)
        w.receive(slots["across1"], self.from_across.at[high], p.across)
        add_rows(self.total, self.sums.at[p.dp, lax.div(p.s, 2)], self.from_far, self.from_across)


def gelu_parts(values):
    phi_wide = 0.5 * (1.0 + lax.erf(values * (1.0 / math.sqrt(2.0))))
    density = jnp.exp(-0.5 * values * values) * (1.0 / math.sqrt(2.0 * math.pi))
    return values * phi_wide, phi_wide + values * density


TILE = 256


def pipe(body, grid, ins, outs, refs):
    pltpu.emit_pipeline(
        body, grid=(grid,), in_specs=[spec for spec in ins], out_specs=[spec for spec in outs]
    )(*refs)


def tall(width, tile=TILE):
    return pl.BlockSpec((tile, width), lambda i: (i, 0))


def slim(height, tile=TILE):
    return pl.BlockSpec((height, tile), lambda i: (0, i))


def fixed(height, width):
    return pl.BlockSpec((height, width), lambda i: (0, 0), pipeline_mode=pl.Buffered(1))


def column_sums(total, values):
    rows, width = values.shape
    total[...] += jnp.sum(values.reshape(rows // 8, 8, width), axis=0)


def rotate(block, cosine, sine):
    half = ROT // 2
    first = block[:, :128]
    rolled = jnp.concatenate([first[:, half:ROT], first[:, :half], first[:, ROT:]], axis=1)
    return jnp.concatenate([first * cosine + rolled * sine, block[:, 128:]], axis=1)


def rotate_back(block, cosine, sine):
    half = ROT // 2
    first = block[:, :128]
    scaled = first * sine
    rolled = jnp.concatenate([scaled[:, half:ROT], scaled[:, :half], scaled[:, ROT:]], axis=1)
    return jnp.concatenate([first * cosine + rolled, block[:, 128:]], axis=1)


class Layer:
    def __init__(self, refs):
        self.__dict__.update(refs)
        self.tokens = self.x.shape[0]
        self.length = self.tokens // N_DP
        self.tiles = self.tokens // TILE

    def clear(self):
        for total in (self.gain1, self.bias1, self.gain2, self.bias2, self.qkv_total, self.up_total):
            total[...] = jnp.zeros_like(total)

    def normalise(self, part, of):
        count = self.tokens // of
        rows = pl.ds(part * count, count)

        def body(x, n1, n2, xh):
            def some(i, carry):
                at = pl.ds(pl.multiple_of(i * 32, 32), 32)
                values = x[at, :].astype(F32)
                centred = values - jnp.mean(values, axis=1, keepdims=True)
                spread = jnp.mean(centred * centred, axis=1, keepdims=True)
                xhat = centred * lax.rsqrt(spread + NORM_EPSILON)
                xh[at, :] = xhat.astype(BF)
                n1[at, :] = (xhat * self.vec[0:1, :] + self.vec[1:2, :]).astype(BF)
                n2[at, :] = (xhat * self.vec[2:3, :] + self.vec[3:4, :]).astype(BF)
                return carry

            lax.fori_loop(0, TILE // 32, some, 0, unroll=4)

        pipe(
            body,
            count // TILE,
            [tall(D)],
            [tall(D)] * 3,
            [ref.at[rows] for ref in (self.x, self.n1, self.n2, self.xhat)],
        )

    def attend(self, seq):
        scale = 1.0 / math.sqrt(HEAD_DIM)
        length = self.length

        def project(q_refs, n1, qkv, g, dense):
            at = pl.ds(pl.multiple_of(pl.program_id(0) * TILE, TILE), TILE)
            cosine, sine = self.cos[at, :], self.sin[at, :]
            wide = jnp.dot(n1[...], qkv[...], preferred_element_type=F32) + self.qkv_bias[...]
            q_refs[0][at, :] = rotate(wide[:, :HEAD_W], cosine, sine).astype(BF)
            q_refs[1][at, :] = rotate(wide[:, HEAD_W : 2 * HEAD_W], cosine, sine).astype(BF)
            q_refs[2][at, :] = wide[:, 2 * HEAD_W :].astype(BF)
            q_refs[3][at, :] = lax.dot_general(g[...], dense[...], NT, preferred_element_type=F32).astype(BF)

        def one(q_ref, k_ref, v_ref, d_att_ref, k_total, v_total):
            base = seq * length
            rows = pl.ds(base, length)
            pipe(
                functools.partial(project, (q_ref, k_ref, v_ref, d_att_ref)),
                length // TILE,
                [tall(D), fixed(D, 3 * HEAD_W), tall(D), fixed(HEAD_W, D)],
                [],
                (self.n1.at[rows], self.qkv, self.g.at[rows], self.dense),
            )
            k_total[...] = jnp.zeros_like(k_total)
            v_total[...] = jnp.zeros_like(v_total)
            for i in range(length // TILE):
                seen = (i + 1) * TILE
                here = pl.ds(i * TILE, TILE)
                there = pl.ds(base + i * TILE, TILE)
                q, d_att = q_ref[here, :], d_att_ref[here, :]
                k, v = k_ref[:seen, :], v_ref[:seen, :]
                scores = lax.dot_general(q, k, NT, preferred_element_type=F32) * scale
                row = lax.broadcasted_iota(jnp.int32, scores.shape, 0) + i * TILE
                column = lax.broadcasted_iota(jnp.int32, scores.shape, 1)
                scores = jnp.where(row >= column, scores, MASKED)
                grown = jnp.exp(scores - jnp.max(scores, axis=1, keepdims=True))
                prob = grown * (1.0 / jnp.sum(grown, axis=1, keepdims=True))
                prob_low = prob.astype(BF)
                self.att[there, :] = jnp.dot(prob_low, v, preferred_element_type=F32).astype(BF)
                d_prob = lax.dot_general(d_att, v, NT, preferred_element_type=F32)
                inner = jnp.sum(d_prob * prob, axis=1, keepdims=True)
                d_scores = (prob * (d_prob - inner)).astype(BF)
                d_q = jnp.dot(d_scores, k, preferred_element_type=F32) * scale
                d_q = rotate_back(d_q, self.cos[here, :], self.sin[here, :]).astype(BF)
                self.d_proj[there, :HEAD_W] = d_q
                k_total[:seen, :] += lax.dot_general(d_scores, q, TN, preferred_element_type=F32)
                v_total[:seen, :] += lax.dot_general(prob_low, d_att, TN, preferred_element_type=F32)
            for i in range(length // TILE):
                here = pl.ds(i * TILE, TILE)
                there = pl.ds(base + i * TILE, TILE)
                d_k = rotate_back(k_total[here, :] * scale, self.cos[here, :], self.sin[here, :])
                self.d_proj[there, HEAD_W : 2 * HEAD_W] = d_k.astype(BF)
                self.d_proj[there, 2 * HEAD_W :] = v_total[here, :].astype(BF)
                column_sums(self.qkv_total, self.d_proj[there, :].astype(F32))

        low, wide = pltpu.VMEM((length, HEAD_W), BF), pltpu.VMEM((length, HEAD_W), F32)
        pl.run_scoped(one, low, low, low, low, wide, wide)

    def dense_gradient(self):
        def body(g, part):
            part[...] = lax.dot_general(self.att[...], g[...], TN, preferred_element_type=F32).astype(BF)

        pipe(body, D // 512, [slim(self.tokens, 512)], [slim(HEAD_W, 512)], (self.g, self.dn_part))

    def qkv_gradient(self):
        def body(n1, part):
            part[...] = lax.dot_general(n1[...], self.d_proj[...], TN, preferred_element_type=F32).astype(BF)

        pipe(body, D // TILE, [slim(self.tokens)], [tall(3 * HEAD_W)], (self.n1, self.qk_part))

    def back_one(self):
        def body(qkv, xh, part):
            at = pl.ds(pl.multiple_of(pl.program_id(0) * TILE, TILE), TILE)
            d_n = lax.dot_general(self.d_proj[at, :], qkv[...], NT, preferred_element_type=F32)
            part[...] = (d_n * self.vec[0:1, :]).astype(BF)
            column_sums(self.bias1, d_n)
            column_sums(self.gain1, d_n * xh[...].astype(F32))

        pipe(body, self.tiles, [fixed(D, 3 * HEAD_W), tall(D)], [tall(D)], (self.qkv, self.xhat, self.s1))

    def expand(self):
        def body(n2, up, hidden, slope):
            pre = jnp.dot(n2[...], up[...], preferred_element_type=F32) + self.up_bias[...]
            value, rise = gelu_parts(pre)
            hidden[...] = value.astype(BF)
            slope[...] = rise.astype(BF)

        pipe(
            body,
            self.tiles,
            [tall(D), fixed(D, HID_W)],
            [tall(HID_W)] * 2,
            (self.n2, self.up, self.hidden, self.slope),
        )

    def down_gradient(self):
        def body(g, hidden, part):
            part[...] = lax.dot_general(g[...], hidden[...], TN, preferred_element_type=F32).astype(BF)

        pipe(
            body,
            D // TILE,
            [slim(self.tokens), fixed(self.tokens, HID_W)],
            [tall(HID_W)],
            (self.g, self.hidden, self.wt_part),
        )

    def contract_back(self):
        def body(g, wt, slope, d_pre):
            d_hidden = jnp.dot(g[...], wt[...], preferred_element_type=F32)
            low = (d_hidden * slope[...].astype(F32)).astype(BF)
            d_pre[...] = low
            column_sums(self.up_total, low.astype(F32))

        pipe(
            body,
            self.tiles,
            [tall(D), fixed(D, HID_W), tall(HID_W)],
            [tall(HID_W)],
            (self.g, self.wt, self.slope, self.d_pre),
        )

    def up_gradient(self):
        def body(n2, d_pre, part):
            part[...] = lax.dot_general(n2[...], d_pre[...], TN, preferred_element_type=F32).astype(BF)

        pipe(
            body,
            D // TILE,
            [slim(self.tokens), fixed(self.tokens, HID_W)],
            [tall(HID_W)],
            (self.n2, self.d_pre, self.up_part),
        )

    def back_two(self):
        def body(d_pre, up, xh, s1, part):
            d_n = lax.dot_general(d_pre[...], up[...], NT, preferred_element_type=F32)
            part[...] = (s1[...].astype(F32) + d_n * self.vec[2:3, :]).astype(BF)
            column_sums(self.bias2, d_n)
            column_sums(self.gain2, d_n * xh[...].astype(F32))

        pipe(
            body,
            self.tiles,
            [tall(HID_W), fixed(D, HID_W), tall(D), tall(D)],
            [tall(D)],
            (self.d_pre, self.up, self.xhat, self.s1, self.tok_parts),
        )

    def output(self):
        def body(hidden, dense, wt, part):
            at = pl.ds(pl.multiple_of(pl.program_id(0) * TILE, TILE), TILE)
            total = jnp.dot(self.att[at, :], dense[...], preferred_element_type=F32)
            total = total + lax.dot_general(hidden[...], wt[...], NT, preferred_element_type=F32)
            part[...] = total.astype(BF)

        pipe(
            body,
            self.tiles,
            [tall(HID_W), fixed(HEAD_W, D), fixed(D, HID_W)],
            [tall(D)],
            (self.hidden, self.dense, self.wt, self.out_parts),
        )


def any_spec(count):
    return [pl.BlockSpec(memory_space=pl.ANY)] * count


def slots_needed(n_zero):
    return 28 * n_zero + 160


INPUTS = ("x_own", "g_own", "dn_low", "qk_low", "up_low", "wt_low", "vec_own", "out_bias", "cos", "sin")
RESULTS = ("out_sum", "tok_sum", "dn_home", "qk_home", "up_home", "wt_home", "vec_all", "vec_sums")
TOTALS = (("gain1", D), ("bias1", D), ("gain2", D), ("bias2", D), ("qkv_total", 3 * HEAD_W), ("up_total", HID_W))
HALF_W = HID_W // 2
WIDTHS = (HEAD_W, 3 * HEAD_W, HALF_W, HALF_W, HALF_W, HALF_W)


def buffers(tokens):
    square = ("x", "g", "n1", "n2", "xhat", "s1", "tok_parts", "out_parts")
    shapes = {name: (tokens, D) for name in square}
    shapes.update({name: (tokens, HID_W) for name in ("hidden", "slope", "d_pre")})
    shapes.update(dense=(HEAD_W, D), dn_part=(HEAD_W, D), dn_all=(D, HEAD_W), dn_cols=(D, HEAD_W))
    shapes.update(qkv=(D, 3 * HEAD_W), qk_part=(D, 3 * HEAD_W))
    shapes.update({name: (D, HID_W) for name in ("up", "wt", "up_part", "wt_part")})
    return shapes


VEC_ROWS = 16
CHUNK = 128


class VectorGather:
    def __init__(self, wire, place, own, whole):
        self.wire, self.place, self.own, self.whole = wire, place, own, whole
        self.slots = [wire.slot() for _ in range(1, N_SEQ)]
        self.line = LineGather(wire, place, whole, N_SEQ)

    def target(self, s):
        return self.whole.at[pl.ds(self.place.z * N_SEQ + s, 1)]

    def start(self, local_sem):
        p = self.place
        for step in range(1, N_SEQ):
            self.wire.send(self.slots[step - 1], self.own, self.target(p.s), {"seq": lax.rem(p.s + step, N_SEQ)})
        self.copied = pltpu.make_async_copy(self.own, self.target(p.s), local_sem)
        self.copied.start()

    def wait(self):
        p = self.place
        for step in range(1, N_SEQ):
            source = lax.rem(p.s - step + N_SEQ, N_SEQ)
            self.wire.receive(self.slots[step - 1], self.target(source), {"seq": source})
        self.copied.wait()


def lay_out_vectors(layer, place):
    rows = layer.vec_all.shape[1]


    def piece(q):
        shard, row = (q // rows, q % rows) if isinstance(q, int) else (lax.div(q, rows), lax.rem(q, rows))
        return layer.vec_all[shard, pl.ds(row, 1), :]

    count = D // CHUNK
    for row, first in enumerate((0, count, 6 * count, 7 * count)):
        for i in range(count):
            layer.vec[row : row + 1, i * CHUNK : (i + 1) * CHUNK] = piece(first + i)
    each = HEAD_W // CHUNK
    for t in range(3):
        for i in range(each):
            at = t * HEAD_W + i * CHUNK
            layer.qkv_bias[:, at : at + CHUNK] = piece((2 + t) * count + place.part * each + i)
    each = HID_W // CHUNK
    for i in range(each):
        layer.up_bias[:, i * CHUNK : (i + 1) * CHUNK] = piece(8 * count + place.part * each + i)


def partial_vectors(layer):
    fold = lambda total: jnp.sum(total[...], axis=0, keepdims=True)
    rows = [fold(total) for total in (layer.gain1, layer.bias1, layer.gain2, layer.bias2, layer.out_bias)]
    wide = jnp.concatenate(rows + [jnp.zeros((3, D), F32)], axis=0)
    for c in range(PARTS):
        layer.pieces_out[c] = wide[:, c * HEAD_W : (c + 1) * HEAD_W]


def own_vectors(layer, own):
    total = layer.pieces_in[0]
    for c in range(1, PARTS):
        total = total + layer.pieces_in[c]
    own[pl.ds(0, 8), :] = total
    qkv = jnp.sum(layer.qkv_total[...], axis=0, keepdims=True)
    up = jnp.sum(layer.up_total[...], axis=0, keepdims=True)
    cut = lambda row, count: [row[:, i * HEAD_W : (i + 1) * HEAD_W] for i in range(count)]
    rows = cut(qkv, 3) + cut(up, 4) + [jnp.zeros((1, HEAD_W), F32)]
    own[pl.ds(8, 8), :] = jnp.concatenate(rows, axis=0)


def layer_body(n_zero, rows, tokens, *refs):
    names = INPUTS + RESULTS + tuple(buffers(tokens))
    names += ("att", "d_proj", "send_sems", "recv_sems", "local_sems", "own", "total")
    names += ("vec", "qkv_bias", "up_bias", "pieces_out", "pieces_in", "vec_line", "vec_total")
    names += tuple(name for name, _ in TOTALS)
    held = dict(zip(names, refs))
    scratch = list(refs[len(names) :])
    take = lambda count: [scratch.pop(0) for _ in range(count)]
    layer = Layer(held)
    place = Place(n_zero)
    wire = Wire(layer.send_sems, layer.recv_sems)
    local = lambda index: layer.local_sems.at[index]
    block = rows * N_SEQ
    chunk = lambda c: pl.ds(pl.multiple_of(c * HEAD_W, HEAD_W), HEAD_W)

    sources = (layer.dn_low, layer.qk_low, layer.up_low, layer.wt_low)
    wholes = (layer.dn_all, layer.qkv, layer.up, layer.wt)
    exchanges = [SeqExchange(wire, place, low, whole, rows) for low, whole in zip(sources, wholes)]
    dn, qk, up, wt = [LineGather(wire, place, whole, block) for whole in wholes]
    x = PlaneGather(wire, place, layer.x_own, layer.x)
    g = PlaneGather(wire, place, layer.g_own, layer.g)
    dense_in = DenseExchange(
        wire, place, lambda c: layer.dn_all.at[chunk(c)], lambda c: layer.dense.at[:, chunk(c)]
    )
    dense_out = DenseExchange(
        wire, place, lambda c: layer.dn_part.at[:, chunk(c)], lambda c: layer.dn_cols.at[chunk(c)]
    )
    planes = []
    for k, parts in enumerate((layer.out_parts, layer.tok_parts)):
        mate, far, across, turned = take(4)
        planes.append(
            PlaneScatter(wire, place, parts, mate, far, across, turned, layer.total, layer.own, local(k))
        )
    out, tok = planes
    sums, homes = [], []
    part_half = lambda ref, k: ref.at[:, pl.ds(k * HALF_W, HALF_W)]
    parts = [layer.dn_cols, layer.qk_part]
    parts += [part_half(ref, k) for ref in (layer.up_part, layer.wt_part) for k in (0, 1)]
    results = [(layer.dn_home, 0), (layer.qk_home, 0)]
    results += [(home, k * HALF_W) for home in (layer.up_home, layer.wt_home) for k in (0, 1)]
    for k, width in enumerate(WIDTHS):
        ring, total, own = take(3)
        sums.append(LineScatter(wire, place, parts[k], ring, total, own, block, local(20 + k)))
        homes.append(Home(wire, place, total, *results[k], width, rows))

    def finish(k):
        sums[k].last()
        homes[k].start(local(26 + k))

    def store(scatter, result):
        scatter.last()
        copy = pltpu.make_async_copy(scatter.total, result, scatter.sem)
        copy.start()
        copy.wait()

    alone = layer.vec_all.shape[0] == 1
    gather = None if alone else VectorGather(wire, place, layer.vec_own, layer.vec_all)

    def vector_in_start():
        if not alone:
            gather.start(local(18))

    def vector_in_pass():
        if not alone:
            gather.wait()
            gather.line.own_from_ends()
            gather.line.own_from_middle()

    def vector_in_rest():
        if alone:
            copy = pltpu.make_async_copy(layer.vec_own, layer.vec_all, local(18))
            copy.start()
            copy.wait()
        else:
            for step in range(1, n_zero):
                gather.line.ahead(step)
        lay_out_vectors(layer, place)

    pieces = DenseExchange(
        wire, place, lambda c: layer.pieces_out.at[c], lambda c: layer.pieces_in.at[c]
    )
    vector_line = LineGather(wire, place, layer.vec_line, VEC_ROWS)
    vector_spread = DenseExchange(
        wire, place, lambda c: layer.vec_total, lambda c: layer.vec_sums.at[c]
    )

    def vector_out_start():
        partial_vectors(layer)
        pieces.start(local(18))

    def vector_out_pass():
        pieces.wait()
        own = vector_line.block(place.z)
        own_vectors(layer, own)
        vector_line.own_from_ends()
        vector_line.own_from_middle()

    def vector_out_spread():
        total = layer.vec_line[pl.ds(0, VEC_ROWS), :]
        for j in range(1, n_zero):
            total = total + layer.vec_line[pl.ds(j * VEC_ROWS, VEC_ROWS), :]
        layer.vec_total[...] = total
        vector_spread.start(local(19))

    place.barrier()
    layer.clear()
    exchanges[0].start(local(12))
    vector_in_start()
    exchanges[2].start(local(14))
    exchanges[0].wait()
    dn.own_from_ends()
    dn.own_from_middle()
    exchanges[1].start(local(13))
    vector_in_pass()
    dn.ahead(1)
    exchanges[2].wait()
    up.own_from_ends()
    x.start(local(10))
    g.start(local(11))
    up.own_from_middle()
    dn.ahead(2)
    vector_in_rest()
    exchanges[1].wait()
    qk.own_from_ends()
    up.ahead(1)
    x.turn()
    qk.own_from_middle()
    for step in range(3, n_zero):
        dn.ahead(step)
    g.turn()
    x.turn_again()
    x.wait()
    exchanges[3].start(local(15))
    up.ahead(2)
    layer.normalise(0, 2)
    g.turn_again()
    layer.normalise(1, 2)
    qk.ahead(1)
    for step in range(3, n_zero):
        up.ahead(step)
    dense_in.start(local(16))
    exchanges[3].wait()
    wt.own_from_ends()
    layer.expand()
    qk.ahead(2)
    wt.own_from_middle()
    g.wait()
    layer.down_gradient()
    sums[4].launch(0)
    sums[5].launch(0)
    for step in range(3, n_zero):
        qk.ahead(step)
    dense_in.wait()
    layer.attend(0)
    sums[4].launch(1)
    sums[5].launch(1)
    wt.ahead(1)
    layer.attend(1)
    sums[4].launch(2)
    layer.qkv_gradient()
    sums[5].launch(2)
    sums[5].advance(1)
    sums[1].launch(0)
    sums[4].advance(1)
    wt.ahead(2)
    layer.dense_gradient()
    dense_out.start(local(17))
    layer.back_one()
    for step in range(3, n_zero):
        wt.ahead(step)
    sums[5].advance(2)
    sums[1].launch(1)
    layer.contract_back()
    sums[4].advance(2)
    finish(5)
    layer.output()
    sums[1].launch(2)
    out.start()
    finish(4)
    layer.up_gradient()
    dense_out.wait()
    sums[2].launch(0)
    out.turn()
    sums[0].launch(0)
    sums[2].launch(1)
    homes[5].wait()
    sums[0].launch(1)
    sums[1].advance(1)
    layer.back_two()
    tok.start()
    out.turn_again()
    sums[1].advance(2)
    sums[3].launch(0)
    vector_out_start()
    sums[2].launch(2)
    sums[2].advance(1)
    tok.turn()
    sums[0].advance(1)
    tok.turn_again()
    sums[3].launch(1)
    sums[0].launch(2)
    finish(1)
    sums[2].advance(2)
    sums[3].advance(1)
    sums[0].advance(2)
    sums[3].launch(2)
    finish(2)
    store(out, layer.out_sum)
    homes[4].wait()
    sums[3].advance(2)
    vector_out_pass()
    finish(0)
    homes[1].wait()
    finish(3)
    homes[2].wait()
    vector_line.ahead(1)
    store(tok, layer.tok_sum)
    for step in range(2, n_zero):
        vector_line.ahead(step)
    vector_out_spread()
    homes[3].wait()
    homes[0].wait()
    vector_spread.wait()
    wire.finish()


def layer_call(n_zero, rows, tokens, *operands):
    local = tokens // PARTS
    block = rows * N_SEQ
    slots = slots_needed(n_zero)
    shards = (9 * D + FF) // (operands[6].shape[1] * CHUNK)
    vmem = lambda *dims: pltpu.VMEM(dims, BF)
    scratch = [
        vmem(tokens, HEAD_W),
        vmem(tokens, 3 * HEAD_W),
        pltpu.SemaphoreType.DMA((slots,)),
        pltpu.SemaphoreType.DMA((slots,)),
        pltpu.SemaphoreType.DMA((32,)),
        vmem(local, D),
        pltpu.VMEM((local, D), F32),
    ]
    wide = lambda *dims: pltpu.VMEM(dims, F32)
    scratch += [wide(4, D), wide(1, 3 * HEAD_W), wide(1, HID_W), wide(PARTS, 8, HEAD_W)]
    scratch += [wide(PARTS, 8, HEAD_W), wide(n_zero * VEC_ROWS, HEAD_W), wide(VEC_ROWS, HEAD_W)]
    scratch += [wide(8, width) for _, width in TOTALS]
    for _ in range(2):
        scratch += [vmem(2, 2, local, D), vmem(local, D), vmem(local, D), vmem(local, D)]
    for width in WIDTHS:
        scratch += [vmem(n_zero + 1, block, width), vmem(block, width), vmem(block, width)]
    homes = [
        jax.ShapeDtypeStruct((N_DP, N_SEQ, rows, width), BF)
        for width in (HEAD_W, 3 * HEAD_W, HID_W, HID_W)
    ]
    anywhere = pl.BlockSpec(memory_space=pl.ANY)
    vector = pl.BlockSpec(memory_space=pltpu.VMEM)
    held = buffers(tokens)
    return pl.pallas_call(
        functools.partial(layer_body, n_zero, rows, tokens),
        in_specs=[anywhere] * 7 + [vector] * 3,
        out_specs=[anywhere] * (len(RESULTS) - 2) + [vector] * 2 + [anywhere] * len(held),
        out_shape=[jax.ShapeDtypeStruct((local, D), F32)] * 2
        + homes
        + [
            jax.ShapeDtypeStruct((shards,) + operands[6].shape[1:], F32),
            jax.ShapeDtypeStruct((PARTS, VEC_ROWS, HEAD_W), F32),
        ]
        + [jax.ShapeDtypeStruct(shape, BF) for shape in held.values()],
        scratch_shapes=scratch,
        compiler_params=pltpu.CompilerParams(
            collective_id=0, has_side_effects=True, vmem_limit_bytes=62 * 1024 * 1024
        ),
        name="layer",
    )(*operands)


def update(gradient, held, results):
    param, first, second = (ref[...] for ref in held)
    for ref, value in zip(results, adam_step(param, gradient, first, second, WEIGHT_DECAY)):
        ref[...] = value
    results[3][...] = gradient


def finish_body(*refs):
    refs = list(refs)
    take = lambda count: [refs.pop(0) for _ in range(count)]
    up_home, wt_home, dn_home, *qk_homes = take(6)
    up, down, dense, qkv = (take(3) for _ in range(4))
    x, g, out_sum, tok_sum, bias = take(5)
    results = [take(4) for _ in range(4)]
    outputs, input_grad = take(2)
    update(up_home[0, 0].astype(F32), up, results[0])
    update(wt_home[0, 0].astype(F32).T, down, results[1])
    update(dn_home[0, 0].astype(F32), dense, results[2])
    columns = jnp.concatenate([home[0, 0] for home in qk_homes], axis=1)
    update(columns.astype(F32), qkv, results[3])
    tokens = x[...].astype(F32)
    outputs[...] = (tokens + out_sum[...] + bias[...]).astype(BF)
    centred = tokens - jnp.mean(tokens, axis=1, keepdims=True)
    spread = jnp.mean(centred * centred, axis=1, keepdims=True)
    rate = lax.rsqrt(spread + NORM_EPSILON)
    xhat = centred * rate
    d_xhat = tok_sum[...]
    d_tokens = rate * (
        d_xhat
        - jnp.mean(d_xhat, axis=1, keepdims=True)
        - xhat * jnp.mean(d_xhat * xhat, axis=1, keepdims=True)
    )
    input_grad[...] = (g[...].astype(F32) + d_tokens).astype(BF)


def finish_call(homes, states, x, g, out_sum, tok_sum, bias):
    up_home, wt_home, dn_home, qk_home = homes
    rows = up_home.shape[2]
    home = lambda width: pl.BlockSpec((1, 1, rows, width), lambda c: (c // N_SEQ, c % N_SEQ, 0, 0))

    def third(k):
        def at(c):
            unit = 3 * c + k
            part = unit % PARTS
            return (part // N_SEQ, part % N_SEQ, 0, unit // PARTS)

        return pl.BlockSpec((1, 1, rows, HEAD_W), at)

    columns = lambda width: pl.BlockSpec((rows, width), lambda c: (0, c))
    blocks = (columns(HID_W), pl.BlockSpec((HID_W, rows), lambda c: (c, 0)), columns(HEAD_W), columns(3 * HEAD_W))
    some = pl.BlockSpec((x.shape[0] // PARTS, D), lambda c: (c, 0))
    whole = pl.BlockSpec((1, D), lambda c: (0, 0))
    return pl.pallas_call(
        finish_body,
        grid=(PARTS,),
        in_specs=[home(HID_W), home(HID_W), home(HEAD_W)]
        + [third(k) for k in range(3)]
        + [block for block in blocks for _ in range(3)]
        + [some] * 4
        + [whole],
        out_specs=[block for block in blocks for _ in range(4)] + [some] * 2,
        out_shape=[jax.ShapeDtypeStruct(state[0].shape, F32) for state in states for _ in range(4)]
        + [jax.ShapeDtypeStruct(x.shape, BF)] * 2,
        compiler_params=pltpu.CompilerParams(vmem_limit_bytes=60 * 1024 * 1024),
        name="finish",
    )(
        up_home,
        wt_home,
        dn_home,
        qk_home,
        qk_home,
        qk_home,
        *(array for state in states for array in state),
        x,
        g,
        out_sum,
        tok_sum,
        bias,
    )


def pack_body(half, *refs):
    dense, query, key, value, up, down, g, dn_low, qk_low, up_low, wt_low, g_total = refs

    @pl.when(pl.program_id(0) == 0)
    def _():
        g_total[...] = jnp.zeros_like(g_total)

    column_sums(g_total, g[...].astype(F32))
    dn_low[0] = dense[...].astype(BF)
    qk_low[0] = jnp.concatenate([query[...], key[...], value[...]], axis=1).astype(BF)
    up_low[0] = up[...].astype(BF)
    wt_low[0] = down[...].T.astype(BF)


def pack(half, qkv_weight, dense_weight, up_weight, down_weight, g):
    rows = qkv_weight.shape[0]
    columns = lambda width, t: pl.BlockSpec((rows, width), lambda s, h: (0, t * PARTS + h[0] * N_SEQ + s))
    widths = (HEAD_W, 3 * HEAD_W, HID_W, HID_W)
    return pl.pallas_call(
        pack_body,
        grid_spec=pltpu.PrefetchScalarGridSpec(
            num_scalar_prefetch=1,
            grid=(N_SEQ,),
            in_specs=[columns(HEAD_W, 0)]
            + [columns(HEAD_W, t) for t in range(3)]
            + [columns(HID_W, 0), pl.BlockSpec((HID_W, rows), lambda s, h: (h[0] * N_SEQ + s, 0))]
            + [pl.BlockSpec((g.shape[0] // N_SEQ, D), lambda s, h: (s, 0))],
            out_specs=[pl.BlockSpec((1, rows, width), lambda s, h: (s, 0, 0)) for width in widths]
            + [pl.BlockSpec((8, D), lambda s, h: (0, 0))],
        ),
        out_shape=[jax.ShapeDtypeStruct((N_SEQ, rows, width), BF) for width in widths]
        + [jax.ShapeDtypeStruct((8, D), F32)],
        compiler_params=pltpu.CompilerParams(vmem_limit_bytes=62 * 1024 * 1024),
        name="pack",
    )(half, dense_weight, qkv_weight, qkv_weight, qkv_weight, up_weight, down_weight, g)


def rotary_rows(length):
    exponent = np.arange(ROT // 2, dtype=np.float32) * np.float32(2.0 / ROT)
    inverse = np.power(np.float32(10000.0), -exponent)
    angles = np.arange(length, dtype=np.float32)[:, None] * inverse[None, :]
    cosine, sine = np.cos(angles), np.sin(angles)
    ones = np.ones((length, 128 - ROT), np.float32)
    cosine = np.concatenate([cosine, cosine, ones], axis=1)
    sine = np.concatenate([-sine, sine, 0.0 * ones], axis=1)
    return jnp.asarray(cosine), jnp.asarray(sine)


def make_body(sizes):
    n_zero = sizes["zero"]
    everywhere = ("dp", "zero", "seq")

    def body(
        inputs,
        out_grad,
        vectors,
        qkv_weight,
        dense_weight,
        up_weight,
        down_weight,
        vectors_first,
        qkv_first,
        dense_first,
        up_first,
        down_first,
        vectors_second,
        qkv_second,
        dense_second,
        up_second,
        down_second,
    ):
        dp_i, zero_i, seq_i = (lax.axis_index(axis) for axis in everywhere)
        seqs_here, local_len = inputs.shape[0], inputs.shape[1]
        token_rows = seqs_here * local_len
        rows = qkv_weight.shape[0]

        tokens_low = inputs.reshape(token_rows, D)
        grad_low = out_grad.reshape(token_rows, D)
        dn_low, qk_low, up_low, wt_low, d_out_bias = pack(
            dp_i.astype(jnp.int32).reshape(1), qkv_weight, dense_weight, up_weight, down_weight, grad_low
        )
        tokens = N_DP * N_SEQ * token_rows
        vec_low = lax.reduce_precision(vectors, exponent_bits=8, mantissa_bits=7)
        if vectors.shape[0] % CHUNK == 0:
            vec_low = vec_low.reshape(1, -1, CHUNK)
        else:
            vec_low = lax.all_gather(vec_low, ("zero", "seq"), axis=0, tiled=True).reshape(1, -1, CHUNK)
        results = layer_call(
            n_zero,
            rows,
            tokens,
            tokens_low,
            grad_low,
            dn_low,
            qk_low,
            up_low,
            wt_low,
            vec_low,
            d_out_bias,
            *rotary_rows(tokens // N_DP),
        )
        out_sum, d_xhat, dn_home, qk_home, up_home, wt_home, vec_all, vec_sums = results[: len(RESULTS)]
        vec_flat = vec_all.reshape(-1)
        dense_bias, down_bias = vec_flat[5 * D : 6 * D], vec_flat[8 * D + FF : 9 * D + FF]

        row = lambda k: vec_sums[:, k].reshape(-1)
        vector_sum = jnp.concatenate(
            [
                row(0),
                row(1),
                vec_sums[:, 8:11].transpose(1, 0, 2).reshape(-1),
                row(4),
                row(2),
                row(3),
                vec_sums[:, 11:15].reshape(-1),
                row(4),
            ]
        )
        vectors_grad = lax.dynamic_slice_in_dim(
            vector_sum, (zero_i * N_SEQ + seq_i) * vectors.shape[0], vectors.shape[0], 0
        )

        vec_upd = adam_step(vectors, vectors_grad, vectors_first, vectors_second, 0.0) + (vectors_grad,)
        *changed, outputs, input_grad = finish_call(
            (up_home, wt_home, dn_home, qk_home),
            (
                (up_weight, up_first, up_second),
                (down_weight, down_first, down_second),
                (dense_weight, dense_first, dense_second),
                (qkv_weight, qkv_first, qkv_second),
            ),
            tokens_low,
            grad_low,
            out_sum,
            d_xhat,
            (dense_bias + down_bias).reshape(1, D),
        )
        outputs, input_grad = outputs.reshape(inputs.shape), input_grad.reshape(inputs.shape)
        up_upd, down_upd, dense_upd, qkv_upd = (tuple(changed[4 * k : 4 * k + 4]) for k in range(4))
        updates = (vec_upd, qkv_upd, dense_upd, up_upd, down_upd)
        picked = lambda k: tuple(update[k] for update in updates)
        return (outputs, input_grad) + picked(3) + picked(0) + picked(1) + picked(2)

    return body


def solution(mesh):
    wide = P(("dp", "zero"), "seq", None)
    vector = P(("zero", "seq"))
    rows = P(("zero", "seq"), None)
    columns = P(None, ("zero", "seq"))
    state = (vector, rows, rows, rows, columns)
    return jax.shard_map(
        make_body(dict(mesh.shape)),
        mesh=mesh,
        in_specs=(wide, wide) + state * 3,
        out_specs=(wide, wide) + state * 4,
        check_vma=False,
    )
```

```python
import functools
import math

import jax
import jax.numpy as jnp
import numpy as np
from jax import lax
from jax.experimental import pallas as pl
from jax.experimental.pallas import tpu as pltpu
from jax.sharding import PartitionSpec as P

D = 2048
HEADS = 8
HEAD_DIM = 256
FF = 8192
ROT = 64
ADAM_STEP = 4

BETA_ONE = 0.9
BETA_TWO = 0.95
LEARN_RATE = 0.5
EPSILON = 1e-08
WEIGHT_DECAY = 0.1
NORM_EPSILON = 1e-05
MASKED = -1e30
N_DP = 2
N_SEQ = 4
PARTS = N_DP * N_SEQ
HEAD_W = D // PARTS
HID_W = FF // PARTS
BF = jnp.bfloat16
F32 = jnp.float32
NT = (((1,), (1,)), ((), ()))
TN = (((0,), (0,)), ((), ()))


def adam_step(parameter, gradient, first_moment, second, decay_rate):
    first_new = BETA_ONE * first_moment + (1.0 - BETA_ONE) * gradient
    second_new = BETA_TWO * second + (1.0 - BETA_TWO) * gradient * gradient
    first_hat = first_new / (1.0 - BETA_ONE**ADAM_STEP)
    second_hat = second_new / (1.0 - BETA_TWO**ADAM_STEP)
    param_new = parameter - LEARN_RATE * (
        first_hat / (jnp.sqrt(second_hat) + EPSILON) + decay_rate * parameter
    )
    return (param_new, first_new, second_new)


class Wire:
    def __init__(self, send_sems, recv_sems):
        self.send_sems, self.recv_sems, self.used = send_sems, recv_sems, 0
        self.sent = []

    def slot(self):
        self.used += 1
        return self.used - 1

    def copy(self, slot, source, target, device):
        return pltpu.make_async_remote_copy(
            src_ref=source,
            dst_ref=target,
            send_sem=self.send_sems.at[slot],
            recv_sem=self.recv_sems.at[slot],
            device_id=device,
            device_id_type=pl.DeviceIdType.MESH,
        )

    def send(self, slot, source, target, device, when=None):
        copy = self.copy(slot, source, target, device)
        guarded(when, copy.start)
        self.sent.append((copy, when))

    def receive(self, slot, target, device, when=None):
        copy = self.copy(slot, target, target, device)
        guarded(when, copy.wait_recv)

    def finish(self):
        for copy, when in self.sent:
            guarded(when, copy.wait_send)
        self.sent = []


def guarded(when, action):
    if when is None:
        action()
    else:
        pl.when(when)(action)


class Place:
    def __init__(self, n_zero):
        self.n = n_zero
        self.dp, self.z, self.s = (lax.axis_index(a) for a in ("dp", "zero", "seq"))
        flip = lambda value, bit: jnp.bitwise_xor(value, bit)
        self.dp_far, self.s_far, self.s_core = 1 - self.dp, flip(self.s, 2), flip(self.s, 1)
        self.s_both = flip(self.s, 3)
        self.across = {"dp": self.dp_far}
        self.far = {"seq": self.s_far}
        self.core = {"seq": self.s_core}
        self.above, self.below = {"zero": self.z + 1}, {"zero": self.z - 1}
        self.part = self.dp * N_SEQ + self.s

    def others(self):
        for step in range(1, N_DP * N_SEQ):
            at = lax.rem(self.part + step, N_DP * N_SEQ)
            dp, s = lax.div(at, N_SEQ), lax.rem(at, N_SEQ)
            yield step, dp, s, {"dp": dp, "seq": s}

    def barrier(self):
        gate = pltpu.get_barrier_semaphore()
        signal = lambda device: pl.semaphore_signal(
            gate, inc=1, device_id=device, device_id_type=pl.DeviceIdType.MESH
        )
        for _, _, _, device in self.others():
            signal(device)
        pl.when(self.z < self.n - 1)(lambda: signal(self.above))
        pl.when(self.z > 0)(lambda: signal(self.below))
        ends = (self.z < self.n - 1).astype(jnp.int32) + (self.z > 0).astype(jnp.int32)
        pl.semaphore_wait(gate, N_DP * N_SEQ - 1 + ends)


class LineGather:
    def __init__(self, wire, place, whole, rows):
        self.wire, self.place, self.whole, self.rows = wire, place, whole, rows
        self.ups = [wire.slot() for _ in range(place.n - 1)]
        self.downs = [wire.slot() for _ in range(place.n - 1)]

    def block(self, index):
        return self.whole.at[pl.ds(pl.multiple_of(index * self.rows, self.rows), self.rows)]

    def send_up(self, step, block, when):
        self.wire.send(self.ups[step - 1], block, block, self.place.above, when)

    def send_down(self, step, block, when):
        self.wire.send(self.downs[step - 1], block, block, self.place.below, when)

    def own_from_ends(self):
        p = self.place
        self.send_up(1, self.block(p.z), p.z == 0)
        self.send_down(1, self.block(p.z), p.z == p.n - 1)

    def own_from_middle(self):
        p = self.place
        middle = (p.z > 0) & (p.z < p.n - 1)
        self.send_up(1, self.block(p.z), middle)
        self.send_down(1, self.block(p.z), middle)

    def ahead(self, step):
        p = self.place
        up, down = self.block(jnp.maximum(p.z - step, 0)), self.block(jnp.minimum(p.z + step, p.n - 1))
        self.wire.receive(self.ups[step - 1], up, p.below, p.z >= step)
        if step + 1 < p.n:
            self.send_up(step + 1, up, (p.z < p.n - 1) & (p.z >= step))
        self.wire.receive(self.downs[step - 1], down, p.above, p.z + step < p.n)
        if step + 1 < p.n:
            self.send_down(step + 1, down, (p.z > 0) & (p.z + step < p.n))


class SeqExchange:
    def __init__(self, wire, place, send, whole, rows):
        self.wire, self.place, self.out, self.whole, self.rows = wire, place, send, whole, rows
        self.slots = [wire.slot() for _ in range(1, N_SEQ)]

    def target(self, s):
        row = (self.place.z * N_SEQ + s) * self.rows
        return self.whole.at[pl.ds(pl.multiple_of(row, self.rows), self.rows)]

    def start(self, local_sem):
        p = self.place
        for step in range(1, N_SEQ):
            to = lax.rem(p.s + step, N_SEQ)
            self.wire.send(self.slots[step - 1], self.out.at[to], self.target(p.s), {"seq": to})
        own = pltpu.make_async_copy(self.out.at[p.s], self.target(p.s), local_sem)
        own.start()
        self.own = own

    def wait(self):
        p = self.place
        for step in range(1, N_SEQ):
            source = lax.rem(p.s - step + N_SEQ, N_SEQ)
            self.wire.receive(self.slots[step - 1], self.target(source), {"seq": source})
        self.own.wait()


class PlaneGather:
    def __init__(self, wire, place, block, whole):
        self.wire, self.place, self.own, self.whole = wire, place, block, whole
        self.slots = {name: wire.slot() for name in ("far", "across", "both0", "both1", "c0", "c1", "c2", "c3")}
        self.rows = block.shape[0]
        self.half = self.rows // 2

    def at(self, dp, s):
        row = (dp * N_SEQ + s) * self.rows
        return self.whole.at[pl.ds(pl.multiple_of(row, self.rows), self.rows)]

    def start(self, local_sem):
        p, w, slots = self.place, self.wire, self.slots
        mine = self.at(p.dp, p.s)
        w.send(slots["far"], self.own, mine, p.far)
        w.send(slots["across"], self.own, mine, p.across)
        w.send(slots["c0"], self.own, mine, p.core)
        self.copied = pltpu.make_async_copy(self.own, mine, local_sem)
        self.copied.start()

    def turn(self):
        p, w, slots, h = self.place, self.wire, self.slots, self.half
        far, across = self.at(p.dp, p.s_far), self.at(p.dp_far, p.s)
        w.receive(slots["far"], far, p.far)
        w.send(slots["both0"], far.at[pl.ds(0, h)], far.at[pl.ds(0, h)], p.across)
        w.send(slots["c1"], far, far, p.core)
        w.receive(slots["across"], across, p.across)
        w.send(slots["both1"], across.at[pl.ds(h, h)], across.at[pl.ds(h, h)], p.far)
        w.send(slots["c2"], across, across, p.core)

    def turn_again(self):
        p, w, slots, h = self.place, self.wire, self.slots, self.half
        both = self.at(p.dp_far, p.s_far)
        w.receive(slots["both0"], both.at[pl.ds(0, h)], p.across)
        w.receive(slots["both1"], both.at[pl.ds(h, h)], p.far)
        w.send(slots["c3"], both, both, p.core)

    def wait(self):
        p, w, slots = self.place, self.wire, self.slots
        w.receive(slots["c0"], self.at(p.dp, p.s_core), p.core)
        w.receive(slots["c1"], self.at(p.dp, p.s_both), p.core)
        w.receive(slots["c2"], self.at(p.dp_far, p.s_core), p.core)
        w.receive(slots["c3"], self.at(p.dp_far, p.s_both), p.core)
        self.copied.wait()


def add_rows(target, *sources):
    rows = target.shape[0]
    tile = 32 if rows % 32 == 0 else 16

    def one(i, carry):
        at = pl.ds(pl.multiple_of(i * tile, tile), tile)
        total = sources[0][at, :].astype(F32)
        for source in sources[1:]:
            total = total + source[at, :].astype(F32)
        target[at, :] = total.astype(target.dtype)
        return carry

    lax.fori_loop(0, rows // tile, one, 0)


class LineScatter:
    def __init__(self, wire, place, parts, held, total, own, rows, sem):
        self.wire, self.place, self.parts, self.rows = wire, place, parts, rows
        self.held, self.total, self.own, self.sem = held, total, own, sem
        self.launched, self.advanced = 0, 1
        self.up_slots = [wire.slot() for _ in range(place.n)]
        self.down_slots = [wire.slot() for _ in range(place.n)]

    def part(self, j):
        return self.parts.at[pl.ds(pl.multiple_of(j * self.rows, self.rows), self.rows)]

    def fetch(self, j, target):
        return pltpu.make_async_copy(self.part(j), target, self.sem)

    def launch(self, k):
        p = self.place
        top = p.n - 1
        up, down = top - k, k
        self.wire.send(
            self.up_slots[up], self.part(up), self.held.at[up + 1], p.above, p.z == 0
        )
        self.wire.send(
            self.down_slots[down], self.part(down), self.held.at[down], p.below, p.z == top
        )
        self.launched = k + 1

    def advance(self, k):
        p = self.place
        top = p.n - 1
        up = jnp.minimum(top - k + p.z, top)
        self.hop(up, up + 1, self.up_slots[0] + up, p.above, p.below, (p.z > 0) & (p.z <= k))
        down = jnp.maximum(k - top + p.z, 0)
        self.hop(down, down, self.down_slots[0] + down, p.below, p.above, (p.z < top) & (top - p.z <= k))
        self.advanced = k + 1

    def hop(self, j, index, slot, onto, source, active):
        held = self.held.at[index]

        def go():
            copy = self.fetch(j, self.own)
            copy.start()
            self.wire.receive(slot, held, source)
            copy.wait()
            add_rows(held, held, self.own)

        pl.when(active)(go)
        self.wire.send(slot, held, held, onto, active)

    def last(self):
        p = self.place
        for k in range(self.launched, p.n - 1):
            self.launch(k)
        for k in range(self.advanced, p.n - 1):
            self.advance(k)
        copy = self.fetch(p.z, self.own)
        copy.start()
        copy.wait()
        up, down = self.held.at[p.z + 1], self.held.at[p.z]

        @pl.when(p.z == 0)
        def _():
            self.arrive(down, self.down_slots, p.above)
            add_rows(self.total, self.own, down)

        @pl.when(p.z == p.n - 1)
        def _():
            self.arrive(up, self.up_slots, p.below)
            add_rows(self.total, self.own, up)

        @pl.when((p.z > 0) & (p.z < p.n - 1))
        def _():
            self.arrive(up, self.up_slots, p.below)
            self.arrive(down, self.down_slots, p.above)
            add_rows(self.total, self.own, up, down)

    def arrive(self, held, slots, source):
        self.wire.receive(slots[0] + self.place.z, held, source)


class Home:
    def __init__(self, wire, place, total, home, first, width, rows):
        self.wire, self.place, self.total, self.home, self.rows = wire, place, total, home, rows
        self.columns = pl.ds(first, width)
        self.slots = [wire.slot() for _ in range(1, N_DP * N_SEQ)]

    def target(self, dp, s):
        return self.home.at[dp, s, :, self.columns]

    def piece(self, s):
        return self.total.at[pl.ds(pl.multiple_of(s * self.rows, self.rows), self.rows)]

    def start(self, local_sem):
        p = self.place
        for step, dp, s, device in p.others():
            self.wire.send(self.slots[step - 1], self.piece(s), self.target(p.dp, p.s), device)
        self.copied = pltpu.make_async_copy(self.piece(p.s), self.target(p.dp, p.s), local_sem)
        self.copied.start()

    def wait(self):
        p = self.place
        parts = N_DP * N_SEQ
        for step in range(1, parts):
            at = lax.rem(p.part - step + parts, parts)
            dp, s = lax.div(at, N_SEQ), lax.rem(at, N_SEQ)
            self.wire.receive(self.slots[step - 1], self.target(dp, s), {"dp": dp, "seq": s})
        self.copied.wait()


class DenseExchange:
    def __init__(self, wire, place, source, target):
        self.wire, self.place, self.source, self.target = wire, place, source, target
        self.slots = [wire.slot() for _ in range(1, N_DP * N_SEQ)]

    def start(self, local_sem):
        p = self.place
        for step, dp, s, device in p.others():
            self.wire.send(self.slots[step - 1], self.source(dp * N_SEQ + s), self.target(p.part), device)
        self.copied = pltpu.make_async_copy(self.source(p.part), self.target(p.part), local_sem)
        self.copied.start()

    def wait(self):
        p = self.place
        parts = N_DP * N_SEQ
        for step in range(1, parts):
            at = lax.rem(p.part - step + parts, parts)
            device = {"dp": lax.div(at, N_SEQ), "seq": lax.rem(at, N_SEQ)}
            self.wire.receive(self.slots[step - 1], self.target(at), device)
        self.copied.wait()


class PlaneScatter:
    def __init__(self, wire, place, parts, mate, from_far, from_across, turned, total, own, sem):
        self.wire, self.place, self.parts, self.mate, self.sums = wire, place, parts, mate, mate
        self.from_far, self.from_across, self.turned = from_far, from_across, turned
        self.total, self.own, self.sem = total, own, sem
        self.rows = total.shape[0]
        self.half = self.rows // 2
        self.core_slots = [[wire.slot() for _ in range(2)] for _ in range(2)]
        names = ("turn_across", "turn_far", "far0", "far1", "across0", "across1")
        self.slots = {name: wire.slot() for name in names}

    def part(self, dp, s):
        row = (dp * N_SEQ + s) * self.rows
        return self.parts.at[pl.ds(pl.multiple_of(row, self.rows), self.rows)]

    def start(self):
        p = self.place
        core = lax.rem(p.s_core, 2)
        for dp in range(2):
            for y in range(2):
                self.wire.send(
                    self.core_slots[dp][y], self.part(dp, 2 * y + core), self.mate.at[dp, y], p.core
                )

    def combine(self, dp, y):
        p = self.place
        core = lax.rem(p.s, 2)
        for d in range(2):
            for v in range(2):

                @pl.when((dp == d) & (y == v))
                def _(d=d, v=v):
                    copy = pltpu.make_async_copy(self.part(d, 2 * v + core), self.own, self.sem)
                    copy.start()
                    self.wire.receive(self.core_slots[d][v], self.mate.at[d, v], p.core)
                    copy.wait()
                    add_rows(self.sums.at[d, v], self.own, self.mate.at[d, v])

    def turn(self):
        p, w, h, slots = self.place, self.wire, self.half, self.slots
        y = lax.div(p.s, 2)
        y_far = 1 - y
        low, high = pl.ds(0, h), pl.ds(h, h)
        self.combine(p.dp_far, y_far)
        both = self.sums.at[p.dp_far, y_far]
        w.send(slots["turn_across"], both.at[low], self.turned.at[low], p.across)
        w.send(slots["turn_far"], both.at[high], self.turned.at[high], p.far)
        self.combine(p.dp, y_far)
        far = self.sums.at[p.dp, y_far]
        w.send(slots["far1"], far.at[high], self.from_far.at[high], p.far)
        self.combine(p.dp_far, y)
        across = self.sums.at[p.dp_far, y]
        w.send(slots["across0"], across.at[low], self.from_across.at[low], p.across)
        self.combine(p.dp, y)

    def turn_again(self):
        p, w, h, slots = self.place, self.wire, self.half, self.slots
        y = lax.div(p.s, 2)
        low, high = pl.ds(0, h), pl.ds(h, h)
        far, across = self.sums.at[p.dp, 1 - y], self.sums.at[p.dp_far, y]
        w.receive(slots["turn_across"], self.turned.at[low], p.across)
        add_rows(far.at[low], far.at[low], self.turned.at[low])
        w.send(slots["far0"], far.at[low], self.from_far.at[low], p.far)
        w.receive(slots["turn_far"], self.turned.at[high], p.far)
        add_rows(across.at[high], across.at[high], self.turned.at[high])
        w.send(slots["across1"], across.at[high], self.from_across.at[high], p.across)

    def last(self):
        p, w, h, slots = self.place, self.wire, self.half, self.slots
        low, high = pl.ds(0, h), pl.ds(h, h)
        w.receive(slots["far1"], self.from_far.at[high], p.far)
        w.receive(slots["far0"], self.from_far.at[low], p.far)
        w.receive(slots["across0"], self.from_across.at[low], p.across)
        w.receive(slots["across1"], self.from_across.at[high], p.across)
        add_rows(self.total, self.sums.at[p.dp, lax.div(p.s, 2)], self.from_far, self.from_across)


def gelu_parts(values):
    phi_wide = 0.5 * (1.0 + lax.erf(values * (1.0 / math.sqrt(2.0))))
    density = jnp.exp(-0.5 * values * values) * (1.0 / math.sqrt(2.0 * math.pi))
    return values * phi_wide, phi_wide + values * density


TILE = 256
WIDE = 512


def pipe(body, grid, ins, outs, refs):
    pltpu.emit_pipeline(
        body, grid=(grid,), in_specs=[spec for spec in ins], out_specs=[spec for spec in outs]
    )(*refs)


def tall(width, tile=TILE):
    return pl.BlockSpec((tile, width), lambda i: (i, 0))


def slim(height, tile=TILE):
    return pl.BlockSpec((height, tile), lambda i: (0, i))


def fixed(height, width):
    return pl.BlockSpec((height, width), lambda i: (0, 0), pipeline_mode=pl.Buffered(1))


def column_sums(total, values):
    rows, width = values.shape
    total[...] += jnp.sum(values.reshape(rows // 8, 8, width), axis=0)


def rotate(block, cosine, sine):
    half = ROT // 2
    first = block[:, :128]
    rolled = jnp.concatenate([first[:, half:ROT], first[:, :half], first[:, ROT:]], axis=1)
    return jnp.concatenate([first * cosine + rolled * sine, block[:, 128:]], axis=1)


def rotate_back(block, cosine, sine):
    half = ROT // 2
    first = block[:, :128]
    scaled = first * sine
    rolled = jnp.concatenate([scaled[:, half:ROT], scaled[:, :half], scaled[:, ROT:]], axis=1)
    return jnp.concatenate([first * cosine + rolled, block[:, 128:]], axis=1)


class Layer:
    def __init__(self, refs):
        self.__dict__.update(refs)
        self.tokens = self.x.shape[0]
        self.length = self.tokens // N_DP
        self.tiles = self.tokens // TILE

    def clear(self):
        for total in (self.gain1, self.bias1, self.gain2, self.bias2, self.qkv_total, self.up_total):
            total[...] = jnp.zeros_like(total)

    def normalise(self, part, of):
        count = self.tokens // of
        rows = pl.ds(part * count, count)

        def body(x, n1, n2, xh):
            def some(i, carry):
                at = pl.ds(pl.multiple_of(i * 32, 32), 32)
                values = x[at, :].astype(F32)
                centred = values - jnp.mean(values, axis=1, keepdims=True)
                spread = jnp.mean(centred * centred, axis=1, keepdims=True)
                xhat = centred * lax.rsqrt(spread + NORM_EPSILON)
                xh[at, :] = xhat.astype(BF)
                n1[at, :] = (xhat * self.vec[0:1, :] + self.vec[1:2, :]).astype(BF)
                n2[at, :] = (xhat * self.vec[2:3, :] + self.vec[3:4, :]).astype(BF)
                return carry

            lax.fori_loop(0, TILE // 32, some, 0, unroll=4)

        pipe(
            body,
            count // TILE,
            [tall(D)],
            [tall(D)] * 3,
            [ref.at[rows] for ref in (self.x, self.n1, self.n2, self.xhat)],
        )

    def attend(self, seq):
        scale = 1.0 / math.sqrt(HEAD_DIM)
        length = self.length

        def project(q_refs, n1, qkv, g, dense):
            at = pl.ds(pl.multiple_of(pl.program_id(0) * TILE, TILE), TILE)
            cosine, sine = self.cos[at, :], self.sin[at, :]
            wide = jnp.dot(n1[...], qkv[...], preferred_element_type=F32) + self.qkv_bias[...]
            q_refs[0][at, :] = rotate(wide[:, :HEAD_W], cosine, sine).astype(BF)
            q_refs[1][at, :] = rotate(wide[:, HEAD_W : 2 * HEAD_W], cosine, sine).astype(BF)
            q_refs[2][at, :] = wide[:, 2 * HEAD_W :].astype(BF)
            q_refs[3][at, :] = lax.dot_general(g[...], dense[...], NT, preferred_element_type=F32).astype(BF)

        def one(q_ref, k_ref, v_ref, d_att_ref, k_total, v_total):
            base = seq * length
            rows = pl.ds(base, length)
            pipe(
                functools.partial(project, (q_ref, k_ref, v_ref, d_att_ref)),
                length // TILE,
                [tall(D), fixed(D, 3 * HEAD_W), tall(D), fixed(HEAD_W, D)],
                [],
                (self.n1.at[rows], self.qkv, self.g.at[rows], self.dense),
            )
            k_total[...] = jnp.zeros_like(k_total)
            v_total[...] = jnp.zeros_like(v_total)
            for i in range(length // TILE):
                seen = (i + 1) * TILE
                here = pl.ds(i * TILE, TILE)
                there = pl.ds(base + i * TILE, TILE)
                q, d_att = q_ref[here, :], d_att_ref[here, :]
                k, v = k_ref[:seen, :], v_ref[:seen, :]
                scores = lax.dot_general(q, k, NT, preferred_element_type=F32) * scale
                row = lax.broadcasted_iota(jnp.int32, scores.shape, 0) + i * TILE
                column = lax.broadcasted_iota(jnp.int32, scores.shape, 1)
                scores = jnp.where(row >= column, scores, MASKED)
                grown = jnp.exp(scores - jnp.max(scores, axis=1, keepdims=True))
                prob = grown * (1.0 / jnp.sum(grown, axis=1, keepdims=True))
                prob_low = prob.astype(BF)
                self.att[there, :] = jnp.dot(prob_low, v, preferred_element_type=F32).astype(BF)
                d_prob = lax.dot_general(d_att, v, NT, preferred_element_type=F32)
                inner = jnp.sum(d_prob * prob, axis=1, keepdims=True)
                d_scores = (prob * (d_prob - inner)).astype(BF)
                d_q = jnp.dot(d_scores, k, preferred_element_type=F32) * scale
                d_q = rotate_back(d_q, self.cos[here, :], self.sin[here, :]).astype(BF)
                self.d_proj[there, :HEAD_W] = d_q
                k_total[:seen, :] += lax.dot_general(d_scores, q, TN, preferred_element_type=F32)
                v_total[:seen, :] += lax.dot_general(prob_low, d_att, TN, preferred_element_type=F32)
            for i in range(length // TILE):
                here = pl.ds(i * TILE, TILE)
                there = pl.ds(base + i * TILE, TILE)
                d_k = rotate_back(k_total[here, :] * scale, self.cos[here, :], self.sin[here, :])
                self.d_proj[there, HEAD_W : 2 * HEAD_W] = d_k.astype(BF)
                self.d_proj[there, 2 * HEAD_W :] = v_total[here, :].astype(BF)
                column_sums(self.qkv_total, self.d_proj[there, :].astype(F32))

        low, wide = pltpu.VMEM((length, HEAD_W), BF), pltpu.VMEM((length, HEAD_W), F32)
        pl.run_scoped(one, low, low, low, low, wide, wide)

    def dense_gradient(self):
        def body(g, part):
            part[...] = lax.dot_general(self.att[...], g[...], TN, preferred_element_type=F32).astype(BF)

        pipe(body, D // 512, [slim(self.tokens, 512)], [slim(HEAD_W, 512)], (self.g, self.dn_part))

    def qkv_gradient(self):
        def body(n1, part):
            part[...] = lax.dot_general(n1[...], self.d_proj[...], TN, preferred_element_type=F32).astype(BF)

        pipe(body, D // WIDE, [slim(self.tokens, WIDE)], [tall(3 * HEAD_W, WIDE)], (self.n1, self.qk_part))

    def back_one(self):
        def body(qkv, xh, part):
            at = pl.ds(pl.multiple_of(pl.program_id(0) * TILE, TILE), TILE)
            d_n = lax.dot_general(self.d_proj[at, :], qkv[...], NT, preferred_element_type=F32)
            part[...] = (d_n * self.vec[0:1, :]).astype(BF)
            column_sums(self.bias1, d_n)
            column_sums(self.gain1, d_n * xh[...].astype(F32))

        pipe(body, self.tiles, [fixed(D, 3 * HEAD_W), tall(D)], [tall(D)], (self.qkv, self.xhat, self.s1))

    def expand(self):
        def body(n2, up, hidden, slope):
            pre = jnp.dot(n2[...], up[...], preferred_element_type=F32) + self.up_bias[...]
            value, rise = gelu_parts(pre)
            hidden[...] = value.astype(BF)
            slope[...] = rise.astype(BF)

        pipe(
            body,
            self.tiles,
            [tall(D), fixed(D, HID_W)],
            [tall(HID_W)] * 2,
            (self.n2, self.up, self.hidden, self.slope),
        )

    def down_gradient(self):
        def body(g, hidden, part):
            part[...] = lax.dot_general(g[...], hidden[...], TN, preferred_element_type=F32).astype(BF)

        pipe(
            body,
            D // WIDE,
            [slim(self.tokens, WIDE), fixed(self.tokens, HID_W)],
            [tall(HID_W, WIDE)],
            (self.g, self.hidden, self.wt_part),
        )

    def contract_back(self):
        def body(g, wt, slope, d_pre):
            d_hidden = jnp.dot(g[...], wt[...], preferred_element_type=F32)
            low = (d_hidden * slope[...].astype(F32)).astype(BF)
            d_pre[...] = low
            column_sums(self.up_total, low.astype(F32))

        pipe(
            body,
            self.tokens // WIDE,
            [tall(D, WIDE), fixed(D, HID_W), tall(HID_W, WIDE)],
            [tall(HID_W, WIDE)],
            (self.g, self.wt, self.slope, self.d_pre),
        )

    def up_gradient(self):
        def body(n2, d_pre, part):
            part[...] = lax.dot_general(n2[...], d_pre[...], TN, preferred_element_type=F32).astype(BF)

        pipe(
            body,
            D // WIDE,
            [slim(self.tokens, WIDE), fixed(self.tokens, HID_W)],
            [tall(HID_W, WIDE)],
            (self.n2, self.d_pre, self.up_part),
        )

    def back_two(self):
        def body(d_pre, up, xh, s1, part):
            d_n = lax.dot_general(d_pre[...], up[...], NT, preferred_element_type=F32)
            part[...] = (s1[...].astype(F32) + d_n * self.vec[2:3, :]).astype(BF)
            column_sums(self.bias2, d_n)
            column_sums(self.gain2, d_n * xh[...].astype(F32))

        pipe(
            body,
            self.tiles,
            [tall(HID_W), fixed(D, HID_W), tall(D), tall(D)],
            [tall(D)],
            (self.d_pre, self.up, self.xhat, self.s1, self.tok_parts),
        )

    def output(self):
        def body(hidden, dense, wt, part):
            at = pl.ds(pl.multiple_of(pl.program_id(0) * TILE, TILE), TILE)
            total = jnp.dot(self.att[at, :], dense[...], preferred_element_type=F32)
            total = total + lax.dot_general(hidden[...], wt[...], NT, preferred_element_type=F32)
            part[...] = total.astype(BF)

        pipe(
            body,
            self.tiles,
            [tall(HID_W), fixed(HEAD_W, D), fixed(D, HID_W)],
            [tall(D)],
            (self.hidden, self.dense, self.wt, self.out_parts),
        )


def any_spec(count):
    return [pl.BlockSpec(memory_space=pl.ANY)] * count


def slots_needed(n_zero):
    return 28 * n_zero + 160


INPUTS = ("x_own", "g_own", "dn_low", "qk_low", "up_low", "wt_low", "vec_own", "out_bias", "cos", "sin")
RESULTS = ("out_sum", "tok_sum", "dn_home", "qk_home", "up_home", "wt_home", "vec_all", "vec_sums")
TOTALS = (("gain1", D), ("bias1", D), ("gain2", D), ("bias2", D), ("qkv_total", 3 * HEAD_W), ("up_total", HID_W))
HALF_W = HID_W // 2
WIDTHS = (HEAD_W, 3 * HEAD_W, HALF_W, HALF_W, HALF_W, HALF_W)


def buffers(tokens):
    square = ("x", "g", "n1", "n2", "xhat", "s1", "tok_parts", "out_parts")
    shapes = {name: (tokens, D) for name in square}
    shapes.update({name: (tokens, HID_W) for name in ("hidden", "slope", "d_pre")})
    shapes.update(dense=(HEAD_W, D), dn_part=(HEAD_W, D), dn_all=(D, HEAD_W), dn_cols=(D, HEAD_W))
    shapes.update(qkv=(D, 3 * HEAD_W), qk_part=(D, 3 * HEAD_W))
    shapes.update({name: (D, HID_W) for name in ("up", "wt", "up_part", "wt_part")})
    return shapes


VEC_ROWS = 16
CHUNK = 128


class VectorGather:
    def __init__(self, wire, place, own, whole):
        self.wire, self.place, self.own, self.whole = wire, place, own, whole
        self.slots = [wire.slot() for _ in range(1, N_SEQ)]
        self.line = LineGather(wire, place, whole, N_SEQ)

    def target(self, s):
        return self.whole.at[pl.ds(self.place.z * N_SEQ + s, 1)]

    def start(self, local_sem):
        p = self.place
        for step in range(1, N_SEQ):
            self.wire.send(self.slots[step - 1], self.own, self.target(p.s), {"seq": lax.rem(p.s + step, N_SEQ)})
        self.copied = pltpu.make_async_copy(self.own, self.target(p.s), local_sem)
        self.copied.start()

    def wait(self):
        p = self.place
        for step in range(1, N_SEQ):
            source = lax.rem(p.s - step + N_SEQ, N_SEQ)
            self.wire.receive(self.slots[step - 1], self.target(source), {"seq": source})
        self.copied.wait()


def lay_out_vectors(layer, place):
    rows = layer.vec_all.shape[1]


    def piece(q):
        shard, row = (q // rows, q % rows) if isinstance(q, int) else (lax.div(q, rows), lax.rem(q, rows))
        return layer.vec_all[shard, pl.ds(row, 1), :]

    count = D // CHUNK
    for row, first in enumerate((0, count, 6 * count, 7 * count)):
        for i in range(count):
            layer.vec[row : row + 1, i * CHUNK : (i + 1) * CHUNK] = piece(first + i)
    each = HEAD_W // CHUNK
    for t in range(3):
        for i in range(each):
            at = t * HEAD_W + i * CHUNK
            layer.qkv_bias[:, at : at + CHUNK] = piece((2 + t) * count + place.part * each + i)
    each = HID_W // CHUNK
    for i in range(each):
        layer.up_bias[:, i * CHUNK : (i + 1) * CHUNK] = piece(8 * count + place.part * each + i)


def partial_vectors(layer):
    fold = lambda total: jnp.sum(total[...], axis=0, keepdims=True)
    rows = [fold(total) for total in (layer.gain1, layer.bias1, layer.gain2, layer.bias2, layer.out_bias)]
    wide = jnp.concatenate(rows + [jnp.zeros((3, D), F32)], axis=0)
    for c in range(PARTS):
        layer.pieces_out[c] = wide[:, c * HEAD_W : (c + 1) * HEAD_W]


def own_vectors(layer, own):
    total = layer.pieces_in[0]
    for c in range(1, PARTS):
        total = total + layer.pieces_in[c]
    own[pl.ds(0, 8), :] = total
    qkv = jnp.sum(layer.qkv_total[...], axis=0, keepdims=True)
    up = jnp.sum(layer.up_total[...], axis=0, keepdims=True)
    cut = lambda row, count: [row[:, i * HEAD_W : (i + 1) * HEAD_W] for i in range(count)]
    rows = cut(qkv, 3) + cut(up, 4) + [jnp.zeros((1, HEAD_W), F32)]
    own[pl.ds(8, 8), :] = jnp.concatenate(rows, axis=0)


def layer_body(n_zero, rows, tokens, *refs):
    names = INPUTS + RESULTS + tuple(buffers(tokens))
    names += ("att", "d_proj", "send_sems", "recv_sems", "local_sems", "own", "total")
    names += ("vec", "qkv_bias", "up_bias", "pieces_out", "pieces_in", "vec_line", "vec_total")
    names += tuple(name for name, _ in TOTALS)
    held = dict(zip(names, refs))
    scratch = list(refs[len(names) :])
    take = lambda count: [scratch.pop(0) for _ in range(count)]
    layer = Layer(held)
    place = Place(n_zero)
    wire = Wire(layer.send_sems, layer.recv_sems)
    local = lambda index: layer.local_sems.at[index]
    block = rows * N_SEQ
    chunk = lambda c: pl.ds(pl.multiple_of(c * HEAD_W, HEAD_W), HEAD_W)

    sources = (layer.dn_low, layer.qk_low, layer.up_low, layer.wt_low)
    wholes = (layer.dn_all, layer.qkv, layer.up, layer.wt)
    exchanges = [SeqExchange(wire, place, low, whole, rows) for low, whole in zip(sources, wholes)]
    dn, qk, up, wt = [LineGather(wire, place, whole, block) for whole in wholes]
    x = PlaneGather(wire, place, layer.x_own, layer.x)
    g = PlaneGather(wire, place, layer.g_own, layer.g)
    dense_in = DenseExchange(
        wire, place, lambda c: layer.dn_all.at[chunk(c)], lambda c: layer.dense.at[:, chunk(c)]
    )
    dense_out = DenseExchange(
        wire, place, lambda c: layer.dn_part.at[:, chunk(c)], lambda c: layer.dn_cols.at[chunk(c)]
    )
    planes = []
    for k, parts in enumerate((layer.out_parts, layer.tok_parts)):
        mate, far, across, turned = take(4)
        planes.append(
            PlaneScatter(wire, place, parts, mate, far, across, turned, layer.total, layer.own, local(k))
        )
    out, tok = planes
    sums, homes = [], []
    part_half = lambda ref, k: ref.at[:, pl.ds(k * HALF_W, HALF_W)]
    parts = [layer.dn_cols, layer.qk_part]
    parts += [part_half(ref, k) for ref in (layer.up_part, layer.wt_part) for k in (0, 1)]
    results = [(layer.dn_home, 0), (layer.qk_home, 0)]
    results += [(home, k * HALF_W) for home in (layer.up_home, layer.wt_home) for k in (0, 1)]
    for k, width in enumerate(WIDTHS):
        ring, total, own = take(3)
        sums.append(LineScatter(wire, place, parts[k], ring, total, own, block, local(20 + k)))
        homes.append(Home(wire, place, total, *results[k], width, rows))

    def finish(k):
        sums[k].last()
        homes[k].start(local(26 + k))

    def store(scatter, result):
        scatter.last()
        copy = pltpu.make_async_copy(scatter.total, result, scatter.sem)
        copy.start()
        copy.wait()

    alone = layer.vec_all.shape[0] == 1
    gather = None if alone else VectorGather(wire, place, layer.vec_own, layer.vec_all)

    def vector_in_start():
        if not alone:
            gather.start(local(18))

    def vector_in_pass():
        if not alone:
            gather.wait()
            gather.line.own_from_ends()
            gather.line.own_from_middle()

    def vector_in_rest():
        if alone:
            copy = pltpu.make_async_copy(layer.vec_own, layer.vec_all, local(18))
            copy.start()
            copy.wait()
        else:
            for step in range(1, n_zero):
                gather.line.ahead(step)
        lay_out_vectors(layer, place)

    pieces = DenseExchange(
        wire, place, lambda c: layer.pieces_out.at[c], lambda c: layer.pieces_in.at[c]
    )
    vector_line = LineGather(wire, place, layer.vec_line, VEC_ROWS)
    vector_spread = DenseExchange(
        wire, place, lambda c: layer.vec_total, lambda c: layer.vec_sums.at[c]
    )

    def vector_out_start():
        partial_vectors(layer)
        pieces.start(local(18))

    def vector_out_pass():
        pieces.wait()
        own = vector_line.block(place.z)
        own_vectors(layer, own)
        vector_line.own_from_ends()
        vector_line.own_from_middle()

    def vector_out_spread():
        total = layer.vec_line[pl.ds(0, VEC_ROWS), :]
        for j in range(1, n_zero):
            total = total + layer.vec_line[pl.ds(j * VEC_ROWS, VEC_ROWS), :]
        layer.vec_total[...] = total
        vector_spread.start(local(19))

    place.barrier()
    layer.clear()
    exchanges[0].start(local(12))
    vector_in_start()
    exchanges[2].start(local(14))
    exchanges[0].wait()
    dn.own_from_ends()
    dn.own_from_middle()
    exchanges[1].start(local(13))
    vector_in_pass()
    dn.ahead(1)
    exchanges[2].wait()
    up.own_from_ends()
    x.start(local(10))
    g.start(local(11))
    up.own_from_middle()
    dn.ahead(2)
    vector_in_rest()
    exchanges[1].wait()
    qk.own_from_ends()
    up.ahead(1)
    x.turn()
    qk.own_from_middle()
    for step in range(3, n_zero):
        dn.ahead(step)
    g.turn()
    x.turn_again()
    x.wait()
    exchanges[3].start(local(15))
    up.ahead(2)
    layer.normalise(0, 2)
    g.turn_again()
    layer.normalise(1, 2)
    qk.ahead(1)
    for step in range(3, n_zero):
        up.ahead(step)
    dense_in.start(local(16))
    exchanges[3].wait()
    wt.own_from_ends()
    layer.expand()
    qk.ahead(2)
    wt.own_from_middle()
    g.wait()
    layer.down_gradient()
    sums[4].launch(0)
    sums[5].launch(0)
    for step in range(3, n_zero):
        qk.ahead(step)
    dense_in.wait()
    layer.attend(0)
    sums[4].launch(1)
    sums[5].launch(1)
    wt.ahead(1)
    layer.attend(1)
    sums[4].launch(2)
    layer.qkv_gradient()
    sums[5].launch(2)
    sums[5].advance(1)
    sums[1].launch(0)
    sums[4].advance(1)
    wt.ahead(2)
    layer.dense_gradient()
    dense_out.start(local(17))
    layer.back_one()
    for step in range(3, n_zero):
        wt.ahead(step)
    sums[5].advance(2)
    sums[1].launch(1)
    layer.contract_back()
    sums[4].advance(2)
    finish(5)
    layer.output()
    sums[1].launch(2)
    out.start()
    finish(4)
    layer.up_gradient()
    dense_out.wait()
    sums[2].launch(0)
    out.turn()
    sums[0].launch(0)
    sums[2].launch(1)
    homes[5].wait()
    sums[0].launch(1)
    sums[1].advance(1)
    layer.back_two()
    tok.start()
    out.turn_again()
    sums[1].advance(2)
    sums[3].launch(0)
    vector_out_start()
    sums[2].launch(2)
    sums[2].advance(1)
    tok.turn()
    sums[0].advance(1)
    tok.turn_again()
    sums[3].launch(1)
    sums[0].launch(2)
    finish(1)
    sums[2].advance(2)
    sums[3].advance(1)
    sums[0].advance(2)
    sums[3].launch(2)
    finish(2)
    store(out, layer.out_sum)
    homes[4].wait()
    sums[3].advance(2)
    vector_out_pass()
    finish(0)
    homes[1].wait()
    finish(3)
    homes[2].wait()
    vector_line.ahead(1)
    store(tok, layer.tok_sum)
    for step in range(2, n_zero):
        vector_line.ahead(step)
    vector_out_spread()
    homes[3].wait()
    homes[0].wait()
    vector_spread.wait()
    wire.finish()


def layer_call(n_zero, rows, tokens, *operands):
    local = tokens // PARTS
    block = rows * N_SEQ
    slots = slots_needed(n_zero)
    shards = (9 * D + FF) // (operands[6].shape[1] * CHUNK)
    vmem = lambda *dims: pltpu.VMEM(dims, BF)
    scratch = [
        vmem(tokens, HEAD_W),
        vmem(tokens, 3 * HEAD_W),
        pltpu.SemaphoreType.DMA((slots,)),
        pltpu.SemaphoreType.DMA((slots,)),
        pltpu.SemaphoreType.DMA((32,)),
        vmem(local, D),
        pltpu.VMEM((local, D), F32),
    ]
    wide = lambda *dims: pltpu.VMEM(dims, F32)
    scratch += [wide(4, D), wide(1, 3 * HEAD_W), wide(1, HID_W), wide(PARTS, 8, HEAD_W)]
    scratch += [wide(PARTS, 8, HEAD_W), wide(n_zero * VEC_ROWS, HEAD_W), wide(VEC_ROWS, HEAD_W)]
    scratch += [wide(8, width) for _, width in TOTALS]
    for _ in range(2):
        scratch += [vmem(2, 2, local, D), vmem(local, D), vmem(local, D), vmem(local, D)]
    for width in WIDTHS:
        scratch += [vmem(n_zero + 1, block, width), vmem(block, width), vmem(block, width)]
    homes = [
        jax.ShapeDtypeStruct((N_DP, N_SEQ, rows, width), BF)
        for width in (HEAD_W, 3 * HEAD_W, HID_W, HID_W)
    ]
    anywhere = pl.BlockSpec(memory_space=pl.ANY)
    vector = pl.BlockSpec(memory_space=pltpu.VMEM)
    held = buffers(tokens)
    return pl.pallas_call(
        functools.partial(layer_body, n_zero, rows, tokens),
        in_specs=[anywhere] * 7 + [vector] * 3,
        out_specs=[anywhere] * (len(RESULTS) - 2) + [vector] * 2 + [anywhere] * len(held),
        out_shape=[jax.ShapeDtypeStruct((local, D), F32)] * 2
        + homes
        + [
            jax.ShapeDtypeStruct((shards,) + operands[6].shape[1:], F32),
            jax.ShapeDtypeStruct((PARTS, VEC_ROWS, HEAD_W), F32),
        ]
        + [jax.ShapeDtypeStruct(shape, BF) for shape in held.values()],
        scratch_shapes=scratch,
        compiler_params=pltpu.CompilerParams(
            collective_id=0, has_side_effects=True, vmem_limit_bytes=62 * 1024 * 1024
        ),
        name="layer",
    )(*operands)


def update(gradient, held, results):
    param, first, second = (ref[...] for ref in held)
    for ref, value in zip(results, adam_step(param, gradient, first, second, WEIGHT_DECAY)):
        ref[...] = value
    results[3][...] = gradient


def finish_body(*refs):
    refs = list(refs)
    take = lambda count: [refs.pop(0) for _ in range(count)]
    up_home, wt_home, dn_home, *qk_homes = take(6)
    up, down, dense, qkv = (take(3) for _ in range(4))
    x, g, out_sum, tok_sum, bias = take(5)
    results = [take(4) for _ in range(4)]
    outputs, input_grad = take(2)
    update(up_home[0, 0].astype(F32), up, results[0])
    update(wt_home[0, 0].astype(F32).T, down, results[1])
    update(dn_home[0, 0].astype(F32), dense, results[2])
    columns = jnp.concatenate([home[0, 0] for home in qk_homes], axis=1)
    update(columns.astype(F32), qkv, results[3])
    tokens = x[...].astype(F32)
    outputs[...] = (tokens + out_sum[...] + bias[...]).astype(BF)
    centred = tokens - jnp.mean(tokens, axis=1, keepdims=True)
    spread = jnp.mean(centred * centred, axis=1, keepdims=True)
    rate = lax.rsqrt(spread + NORM_EPSILON)
    xhat = centred * rate
    d_xhat = tok_sum[...]
    d_tokens = rate * (
        d_xhat
        - jnp.mean(d_xhat, axis=1, keepdims=True)
        - xhat * jnp.mean(d_xhat * xhat, axis=1, keepdims=True)
    )
    input_grad[...] = (g[...].astype(F32) + d_tokens).astype(BF)


def finish_call(homes, states, x, g, out_sum, tok_sum, bias):
    up_home, wt_home, dn_home, qk_home = homes
    rows = up_home.shape[2]
    home = lambda width: pl.BlockSpec((1, 1, rows, width), lambda c: (c // N_SEQ, c % N_SEQ, 0, 0))

    def third(k):
        def at(c):
            unit = 3 * c + k
            part = unit % PARTS
            return (part // N_SEQ, part % N_SEQ, 0, unit // PARTS)

        return pl.BlockSpec((1, 1, rows, HEAD_W), at)

    columns = lambda width: pl.BlockSpec((rows, width), lambda c: (0, c))
    blocks = (columns(HID_W), pl.BlockSpec((HID_W, rows), lambda c: (c, 0)), columns(HEAD_W), columns(3 * HEAD_W))
    some = pl.BlockSpec((x.shape[0] // PARTS, D), lambda c: (c, 0))
    whole = pl.BlockSpec((1, D), lambda c: (0, 0))
    return pl.pallas_call(
        finish_body,
        grid=(PARTS,),
        in_specs=[home(HID_W), home(HID_W), home(HEAD_W)]
        + [third(k) for k in range(3)]
        + [block for block in blocks for _ in range(3)]
        + [some] * 4
        + [whole],
        out_specs=[block for block in blocks for _ in range(4)] + [some] * 2,
        out_shape=[jax.ShapeDtypeStruct(state[0].shape, F32) for state in states for _ in range(4)]
        + [jax.ShapeDtypeStruct(x.shape, BF)] * 2,
        compiler_params=pltpu.CompilerParams(vmem_limit_bytes=60 * 1024 * 1024),
        name="finish",
    )(
        up_home,
        wt_home,
        dn_home,
        qk_home,
        qk_home,
        qk_home,
        *(array for state in states for array in state),
        x,
        g,
        out_sum,
        tok_sum,
        bias,
    )


def pack_body(half, *refs):
    dense, query, key, value, up, down, g, dn_low, qk_low, up_low, wt_low, g_total = refs

    @pl.when(pl.program_id(0) == 0)
    def _():
        g_total[...] = jnp.zeros_like(g_total)

    column_sums(g_total, g[...].astype(F32))
    dn_low[0] = dense[...].astype(BF)
    qk_low[0] = jnp.concatenate([query[...], key[...], value[...]], axis=1).astype(BF)
    up_low[0] = up[...].astype(BF)
    wt_low[0] = down[...].T.astype(BF)


def pack(half, qkv_weight, dense_weight, up_weight, down_weight, g):
    rows = qkv_weight.shape[0]
    columns = lambda width, t: pl.BlockSpec((rows, width), lambda s, h: (0, t * PARTS + h[0] * N_SEQ + s))
    widths = (HEAD_W, 3 * HEAD_W, HID_W, HID_W)
    return pl.pallas_call(
        pack_body,
        grid_spec=pltpu.PrefetchScalarGridSpec(
            num_scalar_prefetch=1,
            grid=(N_SEQ,),
            in_specs=[columns(HEAD_W, 0)]
            + [columns(HEAD_W, t) for t in range(3)]
            + [columns(HID_W, 0), pl.BlockSpec((HID_W, rows), lambda s, h: (h[0] * N_SEQ + s, 0))]
            + [pl.BlockSpec((g.shape[0] // N_SEQ, D), lambda s, h: (s, 0))],
            out_specs=[pl.BlockSpec((1, rows, width), lambda s, h: (s, 0, 0)) for width in widths]
            + [pl.BlockSpec((8, D), lambda s, h: (0, 0))],
        ),
        out_shape=[jax.ShapeDtypeStruct((N_SEQ, rows, width), BF) for width in widths]
        + [jax.ShapeDtypeStruct((8, D), F32)],
        compiler_params=pltpu.CompilerParams(vmem_limit_bytes=62 * 1024 * 1024),
        name="pack",
    )(half, dense_weight, qkv_weight, qkv_weight, qkv_weight, up_weight, down_weight, g)


def rotary_rows(length):
    exponent = np.arange(ROT // 2, dtype=np.float32) * np.float32(2.0 / ROT)
    inverse = np.power(np.float32(10000.0), -exponent)
    angles = np.arange(length, dtype=np.float32)[:, None] * inverse[None, :]
    cosine, sine = np.cos(angles), np.sin(angles)
    ones = np.ones((length, 128 - ROT), np.float32)
    cosine = np.concatenate([cosine, cosine, ones], axis=1)
    sine = np.concatenate([-sine, sine, 0.0 * ones], axis=1)
    return jnp.asarray(cosine), jnp.asarray(sine)


def make_body(sizes):
    n_zero = sizes["zero"]
    everywhere = ("dp", "zero", "seq")

    def body(
        inputs,
        out_grad,
        vectors,
        qkv_weight,
        dense_weight,
        up_weight,
        down_weight,
        vectors_first,
        qkv_first,
        dense_first,
        up_first,
        down_first,
        vectors_second,
        qkv_second,
        dense_second,
        up_second,
        down_second,
    ):
        dp_i, zero_i, seq_i = (lax.axis_index(axis) for axis in everywhere)
        seqs_here, local_len = inputs.shape[0], inputs.shape[1]
        token_rows = seqs_here * local_len
        rows = qkv_weight.shape[0]

        tokens_low = inputs.reshape(token_rows, D)
        grad_low = out_grad.reshape(token_rows, D)
        dn_low, qk_low, up_low, wt_low, d_out_bias = pack(
            dp_i.astype(jnp.int32).reshape(1), qkv_weight, dense_weight, up_weight, down_weight, grad_low
        )
        tokens = N_DP * N_SEQ * token_rows
        vec_low = lax.reduce_precision(vectors, exponent_bits=8, mantissa_bits=7)
        if vectors.shape[0] % CHUNK == 0:
            vec_low = vec_low.reshape(1, -1, CHUNK)
        else:
            vec_low = lax.all_gather(vec_low, ("zero", "seq"), axis=0, tiled=True).reshape(1, -1, CHUNK)
        results = layer_call(
            n_zero,
            rows,
            tokens,
            tokens_low,
            grad_low,
            dn_low,
            qk_low,
            up_low,
            wt_low,
            vec_low,
            d_out_bias,
            *rotary_rows(tokens // N_DP),
        )
        out_sum, d_xhat, dn_home, qk_home, up_home, wt_home, vec_all, vec_sums = results[: len(RESULTS)]
        vec_flat = vec_all.reshape(-1)
        dense_bias, down_bias = vec_flat[5 * D : 6 * D], vec_flat[8 * D + FF : 9 * D + FF]

        row = lambda k: vec_sums[:, k].reshape(-1)
        vector_sum = jnp.concatenate(
            [
                row(0),
                row(1),
                vec_sums[:, 8:11].transpose(1, 0, 2).reshape(-1),
                row(4),
                row(2),
                row(3),
                vec_sums[:, 11:15].reshape(-1),
                row(4),
            ]
        )
        vectors_grad = lax.dynamic_slice_in_dim(
            vector_sum, (zero_i * N_SEQ + seq_i) * vectors.shape[0], vectors.shape[0], 0
        )

        vec_upd = adam_step(vectors, vectors_grad, vectors_first, vectors_second, 0.0) + (vectors_grad,)
        *changed, outputs, input_grad = finish_call(
            (up_home, wt_home, dn_home, qk_home),
            (
                (up_weight, up_first, up_second),
                (down_weight, down_first, down_second),
                (dense_weight, dense_first, dense_second),
                (qkv_weight, qkv_first, qkv_second),
            ),
            tokens_low,
            grad_low,
            out_sum,
            d_xhat,
            (dense_bias + down_bias).reshape(1, D),
        )
        outputs, input_grad = outputs.reshape(inputs.shape), input_grad.reshape(inputs.shape)
        up_upd, down_upd, dense_upd, qkv_upd = (tuple(changed[4 * k : 4 * k + 4]) for k in range(4))
        updates = (vec_upd, qkv_upd, dense_upd, up_upd, down_upd)
        picked = lambda k: tuple(update[k] for update in updates)
        return (outputs, input_grad) + picked(3) + picked(0) + picked(1) + picked(2)

    return body


def solution(mesh):
    wide = P(("dp", "zero"), "seq", None)
    vector = P(("zero", "seq"))
    rows = P(("zero", "seq"), None)
    columns = P(None, ("zero", "seq"))
    state = (vector, rows, rows, rows, columns)
    return jax.shard_map(
        make_body(dict(mesh.shape)),
        mesh=mesh,
        in_specs=(wide, wide) + state * 3,
        out_specs=(wide, wide) + state * 4,
        check_vma=False,
    )
```

```python
import functools
import math

import jax
import jax.numpy as jnp
import numpy as np
from jax import lax
from jax.experimental import pallas as pl
from jax.experimental.pallas import tpu as pltpu
from jax.sharding import PartitionSpec as P

D = 2048
HEADS = 8
HEAD_DIM = 256
FF = 8192
ROT = 64
ADAM_STEP = 4

BETA_ONE = 0.9
BETA_TWO = 0.95
LEARN_RATE = 0.5
EPSILON = 1e-08
WEIGHT_DECAY = 0.1
NORM_EPSILON = 1e-05
MASKED = -1e30
N_DP = 2
N_SEQ = 4
PARTS = N_DP * N_SEQ
HEAD_W = D // PARTS
HID_W = FF // PARTS
BF = jnp.bfloat16
F32 = jnp.float32
NT = (((1,), (1,)), ((), ()))
TN = (((0,), (0,)), ((), ()))


def adam_step(parameter, gradient, first_moment, second, decay_rate):
    first_new = BETA_ONE * first_moment + (1.0 - BETA_ONE) * gradient
    second_new = BETA_TWO * second + (1.0 - BETA_TWO) * gradient * gradient
    first_hat = first_new / (1.0 - BETA_ONE**ADAM_STEP)
    second_hat = second_new / (1.0 - BETA_TWO**ADAM_STEP)
    param_new = parameter - LEARN_RATE * (
        first_hat / (jnp.sqrt(second_hat) + EPSILON) + decay_rate * parameter
    )
    return (param_new, first_new, second_new)


class Wire:
    def __init__(self, send_sems, recv_sems):
        self.send_sems, self.recv_sems, self.used = send_sems, recv_sems, 0
        self.sent = []

    def slot(self):
        self.used += 1
        return self.used - 1

    def copy(self, slot, source, target, device):
        return pltpu.make_async_remote_copy(
            src_ref=source,
            dst_ref=target,
            send_sem=self.send_sems.at[slot],
            recv_sem=self.recv_sems.at[slot],
            device_id=device,
            device_id_type=pl.DeviceIdType.MESH,
        )

    def send(self, slot, source, target, device, when=None):
        copy = self.copy(slot, source, target, device)
        guarded(when, copy.start)
        self.sent.append((copy, when))

    def receive(self, slot, target, device, when=None):
        copy = self.copy(slot, target, target, device)
        guarded(when, copy.wait_recv)

    def finish(self):
        for copy, when in self.sent:
            guarded(when, copy.wait_send)
        self.sent = []


def guarded(when, action):
    if when is None:
        action()
    else:
        pl.when(when)(action)


class Place:
    def __init__(self, n_zero):
        self.n = n_zero
        self.dp, self.z, self.s = (lax.axis_index(a) for a in ("dp", "zero", "seq"))
        flip = lambda value, bit: jnp.bitwise_xor(value, bit)
        self.dp_far, self.s_far, self.s_core = 1 - self.dp, flip(self.s, 2), flip(self.s, 1)
        self.s_both = flip(self.s, 3)
        self.across = {"dp": self.dp_far}
        self.far = {"seq": self.s_far}
        self.core = {"seq": self.s_core}
        self.above, self.below = {"zero": self.z + 1}, {"zero": self.z - 1}
        self.part = self.dp * N_SEQ + self.s

    def others(self):
        for step in range(1, N_DP * N_SEQ):
            at = lax.rem(self.part + step, N_DP * N_SEQ)
            dp, s = lax.div(at, N_SEQ), lax.rem(at, N_SEQ)
            yield step, dp, s, {"dp": dp, "seq": s}

    def barrier(self):
        gate = pltpu.get_barrier_semaphore()
        signal = lambda device: pl.semaphore_signal(
            gate, inc=1, device_id=device, device_id_type=pl.DeviceIdType.MESH
        )
        for _, _, _, device in self.others():
            signal(device)
        pl.when(self.z < self.n - 1)(lambda: signal(self.above))
        pl.when(self.z > 0)(lambda: signal(self.below))
        ends = (self.z < self.n - 1).astype(jnp.int32) + (self.z > 0).astype(jnp.int32)
        pl.semaphore_wait(gate, N_DP * N_SEQ - 1 + ends)


class LineGather:
    def __init__(self, wire, place, whole, rows):
        self.wire, self.place, self.whole, self.rows = wire, place, whole, rows
        self.ups = [wire.slot() for _ in range(place.n - 1)]
        self.downs = [wire.slot() for _ in range(place.n - 1)]

    def block(self, index):
        return self.whole.at[pl.ds(pl.multiple_of(index * self.rows, self.rows), self.rows)]

    def send_up(self, step, block, when):
        self.wire.send(self.ups[step - 1], block, block, self.place.above, when)

    def send_down(self, step, block, when):
        self.wire.send(self.downs[step - 1], block, block, self.place.below, when)

    def own_from_ends(self):
        p = self.place
        self.send_up(1, self.block(p.z), p.z == 0)
        self.send_down(1, self.block(p.z), p.z == p.n - 1)

    def own_from_middle(self):
        p = self.place
        middle = (p.z > 0) & (p.z < p.n - 1)
        self.send_up(1, self.block(p.z), middle)
        self.send_down(1, self.block(p.z), middle)

    def ahead(self, step):
        p = self.place
        up, down = self.block(jnp.maximum(p.z - step, 0)), self.block(jnp.minimum(p.z + step, p.n - 1))
        self.wire.receive(self.ups[step - 1], up, p.below, p.z >= step)
        if step + 1 < p.n:
            self.send_up(step + 1, up, (p.z < p.n - 1) & (p.z >= step))
        self.wire.receive(self.downs[step - 1], down, p.above, p.z + step < p.n)
        if step + 1 < p.n:
            self.send_down(step + 1, down, (p.z > 0) & (p.z + step < p.n))


class SeqExchange:
    def __init__(self, wire, place, send, whole, rows):
        self.wire, self.place, self.out, self.whole, self.rows = wire, place, send, whole, rows
        self.slots = [wire.slot() for _ in range(1, N_SEQ)]

    def target(self, s):
        row = (self.place.z * N_SEQ + s) * self.rows
        return self.whole.at[pl.ds(pl.multiple_of(row, self.rows), self.rows)]

    def start(self, local_sem):
        p = self.place
        for step in range(1, N_SEQ):
            to = lax.rem(p.s + step, N_SEQ)
            self.wire.send(self.slots[step - 1], self.out.at[to], self.target(p.s), {"seq": to})
        own = pltpu.make_async_copy(self.out.at[p.s], self.target(p.s), local_sem)
        own.start()
        self.own = own

    def wait(self):
        p = self.place
        for step in range(1, N_SEQ):
            source = lax.rem(p.s - step + N_SEQ, N_SEQ)
            self.wire.receive(self.slots[step - 1], self.target(source), {"seq": source})
        self.own.wait()


class PlaneGather:
    def __init__(self, wire, place, block, whole):
        self.wire, self.place, self.own, self.whole = wire, place, block, whole
        self.slots = {name: wire.slot() for name in ("far", "across", "both0", "both1", "c0", "c1", "c2", "c3")}
        self.rows = block.shape[0]
        self.half = self.rows // 2

    def at(self, dp, s):
        row = (dp * N_SEQ + s) * self.rows
        return self.whole.at[pl.ds(pl.multiple_of(row, self.rows), self.rows)]

    def start(self, local_sem):
        p, w, slots = self.place, self.wire, self.slots
        mine = self.at(p.dp, p.s)
        w.send(slots["far"], self.own, mine, p.far)
        w.send(slots["across"], self.own, mine, p.across)
        w.send(slots["c0"], self.own, mine, p.core)
        self.copied = pltpu.make_async_copy(self.own, mine, local_sem)
        self.copied.start()

    def turn(self):
        p, w, slots, h = self.place, self.wire, self.slots, self.half
        far, across = self.at(p.dp, p.s_far), self.at(p.dp_far, p.s)
        w.receive(slots["far"], far, p.far)
        w.send(slots["both0"], far.at[pl.ds(0, h)], far.at[pl.ds(0, h)], p.across)
        w.send(slots["c1"], far, far, p.core)
        w.receive(slots["across"], across, p.across)
        w.send(slots["both1"], across.at[pl.ds(h, h)], across.at[pl.ds(h, h)], p.far)
        w.send(slots["c2"], across, across, p.core)

    def turn_again(self):
        p, w, slots, h = self.place, self.wire, self.slots, self.half
        both = self.at(p.dp_far, p.s_far)
        w.receive(slots["both0"], both.at[pl.ds(0, h)], p.across)
        w.receive(slots["both1"], both.at[pl.ds(h, h)], p.far)
        w.send(slots["c3"], both, both, p.core)

    def wait(self):
        p, w, slots = self.place, self.wire, self.slots
        w.receive(slots["c0"], self.at(p.dp, p.s_core), p.core)
        w.receive(slots["c1"], self.at(p.dp, p.s_both), p.core)
        w.receive(slots["c2"], self.at(p.dp_far, p.s_core), p.core)
        w.receive(slots["c3"], self.at(p.dp_far, p.s_both), p.core)
        self.copied.wait()


def add_rows(target, *sources):
    rows = target.shape[0]
    tile = 32 if rows % 32 == 0 else 16

    def one(i, carry):
        at = pl.ds(pl.multiple_of(i * tile, tile), tile)
        total = sources[0][at, :].astype(F32)
        for source in sources[1:]:
            total = total + source[at, :].astype(F32)
        target[at, :] = total.astype(target.dtype)
        return carry

    lax.fori_loop(0, rows // tile, one, 0)


class LineScatter:
    def __init__(self, wire, place, parts, held, total, own, rows, sem):
        self.wire, self.place, self.parts, self.rows = wire, place, parts, rows
        self.held, self.total, self.own, self.sem = held, total, own, sem
        self.launched, self.advanced = 0, 1
        self.up_slots = [wire.slot() for _ in range(place.n)]
        self.down_slots = [wire.slot() for _ in range(place.n)]

    def part(self, j):
        return self.parts.at[pl.ds(pl.multiple_of(j * self.rows, self.rows), self.rows)]

    def fetch(self, j, target):
        return pltpu.make_async_copy(self.part(j), target, self.sem)

    def launch(self, k):
        p = self.place
        top = p.n - 1
        up, down = top - k, k
        self.wire.send(
            self.up_slots[up], self.part(up), self.held.at[up + 1], p.above, p.z == 0
        )
        self.wire.send(
            self.down_slots[down], self.part(down), self.held.at[down], p.below, p.z == top
        )
        self.launched = k + 1

    def advance(self, k):
        p = self.place
        top = p.n - 1
        up = jnp.minimum(top - k + p.z, top)
        self.hop(up, up + 1, self.up_slots[0] + up, p.above, p.below, (p.z > 0) & (p.z <= k))
        down = jnp.maximum(k - top + p.z, 0)
        self.hop(down, down, self.down_slots[0] + down, p.below, p.above, (p.z < top) & (top - p.z <= k))
        self.advanced = k + 1

    def hop(self, j, index, slot, onto, source, active):
        held = self.held.at[index]

        def go():
            copy = self.fetch(j, self.own)
            copy.start()
            self.wire.receive(slot, held, source)
            copy.wait()
            add_rows(held, held, self.own)

        pl.when(active)(go)
        self.wire.send(slot, held, held, onto, active)

    def last(self):
        p = self.place
        for k in range(self.launched, p.n - 1):
            self.launch(k)
        for k in range(self.advanced, p.n - 1):
            self.advance(k)
        copy = self.fetch(p.z, self.own)
        copy.start()
        copy.wait()
        up, down = self.held.at[p.z + 1], self.held.at[p.z]

        @pl.when(p.z == 0)
        def _():
            self.arrive(down, self.down_slots, p.above)
            add_rows(self.total, self.own, down)

        @pl.when(p.z == p.n - 1)
        def _():
            self.arrive(up, self.up_slots, p.below)
            add_rows(self.total, self.own, up)

        @pl.when((p.z > 0) & (p.z < p.n - 1))
        def _():
            self.arrive(up, self.up_slots, p.below)
            self.arrive(down, self.down_slots, p.above)
            add_rows(self.total, self.own, up, down)

    def arrive(self, held, slots, source):
        self.wire.receive(slots[0] + self.place.z, held, source)


class Home:
    def __init__(self, wire, place, total, home, first, width, rows):
        self.wire, self.place, self.total, self.home, self.rows = wire, place, total, home, rows
        self.columns = pl.ds(first, width)
        self.slots = [wire.slot() for _ in range(1, N_DP * N_SEQ)]

    def target(self, dp, s):
        return self.home.at[dp, s, :, self.columns]

    def piece(self, s):
        return self.total.at[pl.ds(pl.multiple_of(s * self.rows, self.rows), self.rows)]

    def start(self, local_sem):
        p = self.place
        for step, dp, s, device in p.others():
            self.wire.send(self.slots[step - 1], self.piece(s), self.target(p.dp, p.s), device)
        self.copied = pltpu.make_async_copy(self.piece(p.s), self.target(p.dp, p.s), local_sem)
        self.copied.start()

    def wait(self):
        p = self.place
        parts = N_DP * N_SEQ
        for step in range(1, parts):
            at = lax.rem(p.part - step + parts, parts)
            dp, s = lax.div(at, N_SEQ), lax.rem(at, N_SEQ)
            self.wire.receive(self.slots[step - 1], self.target(dp, s), {"dp": dp, "seq": s})
        self.copied.wait()


class DenseExchange:
    def __init__(self, wire, place, source, target):
        self.wire, self.place, self.source, self.target = wire, place, source, target
        self.slots = [wire.slot() for _ in range(1, N_DP * N_SEQ)]

    def start(self, local_sem):
        p = self.place
        for step, dp, s, device in p.others():
            self.wire.send(self.slots[step - 1], self.source(dp * N_SEQ + s), self.target(p.part), device)
        self.copied = pltpu.make_async_copy(self.source(p.part), self.target(p.part), local_sem)
        self.copied.start()

    def wait(self):
        p = self.place
        parts = N_DP * N_SEQ
        for step in range(1, parts):
            at = lax.rem(p.part - step + parts, parts)
            device = {"dp": lax.div(at, N_SEQ), "seq": lax.rem(at, N_SEQ)}
            self.wire.receive(self.slots[step - 1], self.target(at), device)
        self.copied.wait()


class PlaneScatter:
    def __init__(self, wire, place, parts, mate, from_far, from_across, turned, total, own, sem):
        self.wire, self.place, self.parts, self.mate, self.sums = wire, place, parts, mate, mate
        self.from_far, self.from_across, self.turned = from_far, from_across, turned
        self.total, self.own, self.sem = total, own, sem
        self.rows = total.shape[0]
        self.half = self.rows // 2
        self.core_slots = [[wire.slot() for _ in range(2)] for _ in range(2)]
        names = ("turn_across", "turn_far", "far0", "far1", "across0", "across1")
        self.slots = {name: wire.slot() for name in names}

    def part(self, dp, s):
        row = (dp * N_SEQ + s) * self.rows
        return self.parts.at[pl.ds(pl.multiple_of(row, self.rows), self.rows)]

    def start(self):
        p = self.place
        core = lax.rem(p.s_core, 2)
        for dp in range(2):
            for y in range(2):
                self.wire.send(
                    self.core_slots[dp][y], self.part(dp, 2 * y + core), self.mate.at[dp, y], p.core
                )

    def combine(self, dp, y):
        p = self.place
        core = lax.rem(p.s, 2)
        for d in range(2):
            for v in range(2):

                @pl.when((dp == d) & (y == v))
                def _(d=d, v=v):
                    copy = pltpu.make_async_copy(self.part(d, 2 * v + core), self.own, self.sem)
                    copy.start()
                    self.wire.receive(self.core_slots[d][v], self.mate.at[d, v], p.core)
                    copy.wait()
                    add_rows(self.sums.at[d, v], self.own, self.mate.at[d, v])

    def turn(self):
        p, w, h, slots = self.place, self.wire, self.half, self.slots
        y = lax.div(p.s, 2)
        y_far = 1 - y
        low, high = pl.ds(0, h), pl.ds(h, h)
        self.combine(p.dp_far, y_far)
        both = self.sums.at[p.dp_far, y_far]
        w.send(slots["turn_across"], both.at[low], self.turned.at[low], p.across)
        w.send(slots["turn_far"], both.at[high], self.turned.at[high], p.far)
        self.combine(p.dp, y_far)
        far = self.sums.at[p.dp, y_far]
        w.send(slots["far1"], far.at[high], self.from_far.at[high], p.far)
        self.combine(p.dp_far, y)
        across = self.sums.at[p.dp_far, y]
        w.send(slots["across0"], across.at[low], self.from_across.at[low], p.across)
        self.combine(p.dp, y)

    def turn_again(self):
        p, w, h, slots = self.place, self.wire, self.half, self.slots
        y = lax.div(p.s, 2)
        low, high = pl.ds(0, h), pl.ds(h, h)
        far, across = self.sums.at[p.dp, 1 - y], self.sums.at[p.dp_far, y]
        w.receive(slots["turn_across"], self.turned.at[low], p.across)
        add_rows(far.at[low], far.at[low], self.turned.at[low])
        w.send(slots["far0"], far.at[low], self.from_far.at[low], p.far)
        w.receive(slots["turn_far"], self.turned.at[high], p.far)
        add_rows(across.at[high], across.at[high], self.turned.at[high])
        w.send(slots["across1"], across.at[high], self.from_across.at[high], p.across)

    def last(self):
        p, w, h, slots = self.place, self.wire, self.half, self.slots
        low, high = pl.ds(0, h), pl.ds(h, h)
        w.receive(slots["far1"], self.from_far.at[high], p.far)
        w.receive(slots["far0"], self.from_far.at[low], p.far)
        w.receive(slots["across0"], self.from_across.at[low], p.across)
        w.receive(slots["across1"], self.from_across.at[high], p.across)
        add_rows(self.total, self.sums.at[p.dp, lax.div(p.s, 2)], self.from_far, self.from_across)


def gelu_parts(values):
    phi_wide = 0.5 * (1.0 + lax.erf(values * (1.0 / math.sqrt(2.0))))
    density = jnp.exp(-0.5 * values * values) * (1.0 / math.sqrt(2.0 * math.pi))
    return values * phi_wide, phi_wide + values * density


TILE = 256
WIDE = 512


def pipe(body, grid, ins, outs, refs):
    pltpu.emit_pipeline(
        body, grid=(grid,), in_specs=[spec for spec in ins], out_specs=[spec for spec in outs]
    )(*refs)


def tall(width, tile=TILE):
    return pl.BlockSpec((tile, width), lambda i: (i, 0))


def slim(height, tile=TILE):
    return pl.BlockSpec((height, tile), lambda i: (0, i))


def fixed(height, width):
    return pl.BlockSpec((height, width), lambda i: (0, 0), pipeline_mode=pl.Buffered(1))


def column_sums(total, values):
    rows, width = values.shape
    total[...] += jnp.sum(values.reshape(rows // 8, 8, width), axis=0)


def rotate(block, cosine, sine):
    half = ROT // 2
    first = block[:, :128]
    rolled = jnp.concatenate([first[:, half:ROT], first[:, :half], first[:, ROT:]], axis=1)
    return jnp.concatenate([first * cosine + rolled * sine, block[:, 128:]], axis=1)


def rotate_back(block, cosine, sine):
    half = ROT // 2
    first = block[:, :128]
    scaled = first * sine
    rolled = jnp.concatenate([scaled[:, half:ROT], scaled[:, :half], scaled[:, ROT:]], axis=1)
    return jnp.concatenate([first * cosine + rolled, block[:, 128:]], axis=1)


class Layer:
    def __init__(self, refs):
        self.__dict__.update(refs)
        self.tokens = self.x.shape[0]
        self.length = self.tokens // N_DP
        self.tiles = self.tokens // TILE

    def clear(self):
        for total in (self.gain1, self.bias1, self.gain2, self.bias2, self.qkv_total, self.up_total):
            total[...] = jnp.zeros_like(total)

    def normalise(self, part, of):
        count = self.tokens // of
        rows = pl.ds(part * count, count)

        def body(x, n1, n2, xh):
            def some(i, carry):
                at = pl.ds(pl.multiple_of(i * 32, 32), 32)
                values = x[at, :].astype(F32)
                centred = values - jnp.mean(values, axis=1, keepdims=True)
                spread = jnp.mean(centred * centred, axis=1, keepdims=True)
                xhat = centred * lax.rsqrt(spread + NORM_EPSILON)
                xh[at, :] = xhat.astype(BF)
                n1[at, :] = (xhat * self.vec[0:1, :] + self.vec[1:2, :]).astype(BF)
                n2[at, :] = (xhat * self.vec[2:3, :] + self.vec[3:4, :]).astype(BF)
                return carry

            lax.fori_loop(0, TILE // 32, some, 0, unroll=4)

        pipe(
            body,
            count // TILE,
            [tall(D)],
            [tall(D)] * 3,
            [ref.at[rows] for ref in (self.x, self.n1, self.n2, self.xhat)],
        )

    def attend(self, seq):
        scale = 1.0 / math.sqrt(HEAD_DIM)
        length = self.length

        def project(q_refs, n1, qkv, g, dense):
            at = pl.ds(pl.multiple_of(pl.program_id(0) * TILE, TILE), TILE)
            cosine, sine = self.cos[at, :], self.sin[at, :]
            wide = jnp.dot(n1[...], qkv[...], preferred_element_type=F32) + self.qkv_bias[...]
            q_refs[0][at, :] = rotate(wide[:, :HEAD_W], cosine, sine).astype(BF)
            q_refs[1][at, :] = rotate(wide[:, HEAD_W : 2 * HEAD_W], cosine, sine).astype(BF)
            q_refs[2][at, :] = wide[:, 2 * HEAD_W :].astype(BF)
            q_refs[3][at, :] = lax.dot_general(g[...], dense[...], NT, preferred_element_type=F32).astype(BF)

        def one(q_ref, k_ref, v_ref, d_att_ref, k_total, v_total):
            base = seq * length
            rows = pl.ds(base, length)
            pipe(
                functools.partial(project, (q_ref, k_ref, v_ref, d_att_ref)),
                length // TILE,
                [tall(D), fixed(D, 3 * HEAD_W), tall(D), fixed(HEAD_W, D)],
                [],
                (self.n1.at[rows], self.qkv, self.g.at[rows], self.dense),
            )
            k_total[...] = jnp.zeros_like(k_total)
            v_total[...] = jnp.zeros_like(v_total)
            for i in range(length // TILE):
                seen = (i + 1) * TILE
                here = pl.ds(i * TILE, TILE)
                there = pl.ds(base + i * TILE, TILE)
                q, d_att = q_ref[here, :], d_att_ref[here, :]
                k, v = k_ref[:seen, :], v_ref[:seen, :]
                scores = lax.dot_general(q, k, NT, preferred_element_type=F32) * scale
                row = lax.broadcasted_iota(jnp.int32, scores.shape, 0) + i * TILE
                column = lax.broadcasted_iota(jnp.int32, scores.shape, 1)
                scores = jnp.where(row >= column, scores, MASKED)
                grown = jnp.exp(scores - jnp.max(scores, axis=1, keepdims=True))
                prob = grown * (1.0 / jnp.sum(grown, axis=1, keepdims=True))
                prob_low = prob.astype(BF)
                self.att[there, :] = jnp.dot(prob_low, v, preferred_element_type=F32).astype(BF)
                d_prob = lax.dot_general(d_att, v, NT, preferred_element_type=F32)
                inner = jnp.sum(d_prob * prob, axis=1, keepdims=True)
                d_scores = (prob * (d_prob - inner)).astype(BF)
                d_q = jnp.dot(d_scores, k, preferred_element_type=F32) * scale
                d_q = rotate_back(d_q, self.cos[here, :], self.sin[here, :]).astype(BF)
                self.d_proj[there, :HEAD_W] = d_q
                k_total[:seen, :] += lax.dot_general(d_scores, q, TN, preferred_element_type=F32)
                v_total[:seen, :] += lax.dot_general(prob_low, d_att, TN, preferred_element_type=F32)
            for i in range(length // TILE):
                here = pl.ds(i * TILE, TILE)
                there = pl.ds(base + i * TILE, TILE)
                d_k = rotate_back(k_total[here, :] * scale, self.cos[here, :], self.sin[here, :])
                self.d_proj[there, HEAD_W : 2 * HEAD_W] = d_k.astype(BF)
                self.d_proj[there, 2 * HEAD_W :] = v_total[here, :].astype(BF)
                column_sums(self.qkv_total, self.d_proj[there, :].astype(F32))

        low, wide = pltpu.VMEM((length, HEAD_W), BF), pltpu.VMEM((length, HEAD_W), F32)
        pl.run_scoped(one, low, low, low, low, wide, wide)

    def dense_gradient(self):
        def body(g, part):
            part[...] = lax.dot_general(self.att[...], g[...], TN, preferred_element_type=F32).astype(BF)

        pipe(body, D // 512, [slim(self.tokens, 512)], [slim(HEAD_W, 512)], (self.g, self.dn_part))

    def qkv_gradient(self):
        def body(n1, part):
            part[...] = lax.dot_general(n1[...], self.d_proj[...], TN, preferred_element_type=F32).astype(BF)

        pipe(body, D // WIDE, [slim(self.tokens, WIDE)], [tall(3 * HEAD_W, WIDE)], (self.n1, self.qk_part))

    def back_one(self):
        def body(qkv, xh, part):
            at = pl.ds(pl.multiple_of(pl.program_id(0) * TILE, TILE), TILE)
            d_n = lax.dot_general(self.d_proj[at, :], qkv[...], NT, preferred_element_type=F32)
            part[...] = (d_n * self.vec[0:1, :]).astype(BF)
            column_sums(self.bias1, d_n)
            column_sums(self.gain1, d_n * xh[...].astype(F32))

        pipe(body, self.tiles, [fixed(D, 3 * HEAD_W), tall(D)], [tall(D)], (self.qkv, self.xhat, self.s1))

    def expand(self):
        def body(n2, up, hidden, slope):
            for k in range(WIDE // TILE):
                at = slice(k * TILE, (k + 1) * TILE)
                pre = jnp.dot(n2[at, :], up[...], preferred_element_type=F32) + self.up_bias[...]
                value, rise = gelu_parts(pre)
                hidden[at, :] = value.astype(BF)
                slope[at, :] = rise.astype(BF)

        pipe(
            body,
            self.tokens // WIDE,
            [tall(D, WIDE), fixed(D, HID_W)],
            [tall(HID_W, WIDE)] * 2,
            (self.n2, self.up, self.hidden, self.slope),
        )

    def down_gradient(self):
        def body(g, hidden, part):
            part[...] = lax.dot_general(g[...], hidden[...], TN, preferred_element_type=F32).astype(BF)

        pipe(
            body,
            D // WIDE,
            [slim(self.tokens, WIDE), fixed(self.tokens, HID_W)],
            [tall(HID_W, WIDE)],
            (self.g, self.hidden, self.wt_part),
        )

    def contract_back(self):
        def body(g, wt, slope, d_pre):
            d_hidden = jnp.dot(g[...], wt[...], preferred_element_type=F32)
            low = (d_hidden * slope[...].astype(F32)).astype(BF)
            d_pre[...] = low
            column_sums(self.up_total, low.astype(F32))

        pipe(
            body,
            self.tokens // WIDE,
            [tall(D, WIDE), fixed(D, HID_W), tall(HID_W, WIDE)],
            [tall(HID_W, WIDE)],
            (self.g, self.wt, self.slope, self.d_pre),
        )

    def up_gradient(self):
        def body(n2, d_pre, part):
            part[...] = lax.dot_general(n2[...], d_pre[...], TN, preferred_element_type=F32).astype(BF)

        pipe(
            body,
            D // WIDE,
            [slim(self.tokens, WIDE), fixed(self.tokens, HID_W)],
            [tall(HID_W, WIDE)],
            (self.n2, self.d_pre, self.up_part),
        )

    def back_two(self):
        def body(d_pre, up, xh, s1, part):
            d_n = lax.dot_general(d_pre[...], up[...], NT, preferred_element_type=F32)
            part[...] = (s1[...].astype(F32) + d_n * self.vec[2:3, :]).astype(BF)
            column_sums(self.bias2, d_n)
            column_sums(self.gain2, d_n * xh[...].astype(F32))

        pipe(
            body,
            self.tiles,
            [tall(HID_W), fixed(D, HID_W), tall(D), tall(D)],
            [tall(D)],
            (self.d_pre, self.up, self.xhat, self.s1, self.tok_parts),
        )

    def output(self):
        def body(hidden, dense, wt, part):
            at = pl.ds(pl.multiple_of(pl.program_id(0) * TILE, TILE), TILE)
            total = jnp.dot(self.att[at, :], dense[...], preferred_element_type=F32)
            total = total + lax.dot_general(hidden[...], wt[...], NT, preferred_element_type=F32)
            part[...] = total.astype(BF)

        pipe(
            body,
            self.tiles,
            [tall(HID_W), fixed(HEAD_W, D), fixed(D, HID_W)],
            [tall(D)],
            (self.hidden, self.dense, self.wt, self.out_parts),
        )


def any_spec(count):
    return [pl.BlockSpec(memory_space=pl.ANY)] * count


def slots_needed(n_zero):
    return 28 * n_zero + 160


INPUTS = ("x_own", "g_own", "dn_low", "qk_low", "up_low", "wt_low", "vec_own", "out_bias", "cos", "sin")
RESULTS = ("out_sum", "tok_sum", "dn_home", "qk_home", "up_home", "wt_home", "vec_all", "vec_sums")
TOTALS = (("gain1", D), ("bias1", D), ("gain2", D), ("bias2", D), ("qkv_total", 3 * HEAD_W), ("up_total", HID_W))
HALF_W = HID_W // 2
WIDTHS = (HEAD_W, 3 * HEAD_W, HALF_W, HALF_W, HALF_W, HALF_W)


def buffers(tokens):
    square = ("x", "g", "n1", "n2", "xhat", "s1", "tok_parts", "out_parts")
    shapes = {name: (tokens, D) for name in square}
    shapes.update({name: (tokens, HID_W) for name in ("hidden", "slope", "d_pre")})
    shapes.update(dense=(HEAD_W, D), dn_part=(HEAD_W, D), dn_all=(D, HEAD_W), dn_cols=(D, HEAD_W))
    shapes.update(qkv=(D, 3 * HEAD_W), qk_part=(D, 3 * HEAD_W))
    shapes.update({name: (D, HID_W) for name in ("up", "wt", "up_part", "wt_part")})
    return shapes


VEC_ROWS = 16
CHUNK = 128


class VectorGather:
    def __init__(self, wire, place, own, whole):
        self.wire, self.place, self.own, self.whole = wire, place, own, whole
        self.slots = [wire.slot() for _ in range(1, N_SEQ)]
        self.line = LineGather(wire, place, whole, N_SEQ)

    def target(self, s):
        return self.whole.at[pl.ds(self.place.z * N_SEQ + s, 1)]

    def start(self, local_sem):
        p = self.place
        for step in range(1, N_SEQ):
            self.wire.send(self.slots[step - 1], self.own, self.target(p.s), {"seq": lax.rem(p.s + step, N_SEQ)})
        self.copied = pltpu.make_async_copy(self.own, self.target(p.s), local_sem)
        self.copied.start()

    def wait(self):
        p = self.place
        for step in range(1, N_SEQ):
            source = lax.rem(p.s - step + N_SEQ, N_SEQ)
            self.wire.receive(self.slots[step - 1], self.target(source), {"seq": source})
        self.copied.wait()


def lay_out_vectors(layer, place):
    rows = layer.vec_all.shape[1]


    def piece(q):
        shard, row = (q // rows, q % rows) if isinstance(q, int) else (lax.div(q, rows), lax.rem(q, rows))
        return layer.vec_all[shard, pl.ds(row, 1), :]

    count = D // CHUNK
    for row, first in enumerate((0, count, 6 * count, 7 * count)):
        for i in range(count):
            layer.vec[row : row + 1, i * CHUNK : (i + 1) * CHUNK] = piece(first + i)
    each = HEAD_W // CHUNK
    for t in range(3):
        for i in range(each):
            at = t * HEAD_W + i * CHUNK
            layer.qkv_bias[:, at : at + CHUNK] = piece((2 + t) * count + place.part * each + i)
    each = HID_W // CHUNK
    for i in range(each):
        layer.up_bias[:, i * CHUNK : (i + 1) * CHUNK] = piece(8 * count + place.part * each + i)


def partial_vectors(layer):
    fold = lambda total: jnp.sum(total[...], axis=0, keepdims=True)
    rows = [fold(total) for total in (layer.gain1, layer.bias1, layer.gain2, layer.bias2, layer.out_bias)]
    wide = jnp.concatenate(rows + [jnp.zeros((3, D), F32)], axis=0)
    for c in range(PARTS):
        layer.pieces_out[c] = wide[:, c * HEAD_W : (c + 1) * HEAD_W]


def own_vectors(layer, own):
    total = layer.pieces_in[0]
    for c in range(1, PARTS):
        total = total + layer.pieces_in[c]
    own[pl.ds(0, 8), :] = total
    qkv = jnp.sum(layer.qkv_total[...], axis=0, keepdims=True)
    up = jnp.sum(layer.up_total[...], axis=0, keepdims=True)
    cut = lambda row, count: [row[:, i * HEAD_W : (i + 1) * HEAD_W] for i in range(count)]
    rows = cut(qkv, 3) + cut(up, 4) + [jnp.zeros((1, HEAD_W), F32)]
    own[pl.ds(8, 8), :] = jnp.concatenate(rows, axis=0)


def layer_body(n_zero, rows, tokens, *refs):
    names = INPUTS + RESULTS + tuple(buffers(tokens))
    names += ("att", "d_proj", "send_sems", "recv_sems", "local_sems", "own", "total")
    names += ("vec", "qkv_bias", "up_bias", "pieces_out", "pieces_in", "vec_line", "vec_total")
    names += tuple(name for name, _ in TOTALS)
    held = dict(zip(names, refs))
    scratch = list(refs[len(names) :])
    take = lambda count: [scratch.pop(0) for _ in range(count)]
    layer = Layer(held)
    place = Place(n_zero)
    wire = Wire(layer.send_sems, layer.recv_sems)
    local = lambda index: layer.local_sems.at[index]
    block = rows * N_SEQ
    chunk = lambda c: pl.ds(pl.multiple_of(c * HEAD_W, HEAD_W), HEAD_W)

    sources = (layer.dn_low, layer.qk_low, layer.up_low, layer.wt_low)
    wholes = (layer.dn_all, layer.qkv, layer.up, layer.wt)
    exchanges = [SeqExchange(wire, place, low, whole, rows) for low, whole in zip(sources, wholes)]
    dn, qk, up, wt = [LineGather(wire, place, whole, block) for whole in wholes]
    x = PlaneGather(wire, place, layer.x_own, layer.x)
    g = PlaneGather(wire, place, layer.g_own, layer.g)
    dense_in = DenseExchange(
        wire, place, lambda c: layer.dn_all.at[chunk(c)], lambda c: layer.dense.at[:, chunk(c)]
    )
    dense_out = DenseExchange(
        wire, place, lambda c: layer.dn_part.at[:, chunk(c)], lambda c: layer.dn_cols.at[chunk(c)]
    )
    planes = []
    for k, parts in enumerate((layer.out_parts, layer.tok_parts)):
        mate, far, across, turned = take(4)
        planes.append(
            PlaneScatter(wire, place, parts, mate, far, across, turned, layer.total, layer.own, local(k))
        )
    out, tok = planes
    sums, homes = [], []
    part_half = lambda ref, k: ref.at[:, pl.ds(k * HALF_W, HALF_W)]
    parts = [layer.dn_cols, layer.qk_part]
    parts += [part_half(ref, k) for ref in (layer.up_part, layer.wt_part) for k in (0, 1)]
    results = [(layer.dn_home, 0), (layer.qk_home, 0)]
    results += [(home, k * HALF_W) for home in (layer.up_home, layer.wt_home) for k in (0, 1)]
    for k, width in enumerate(WIDTHS):
        ring, total, own = take(3)
        sums.append(LineScatter(wire, place, parts[k], ring, total, own, block, local(20 + k)))
        homes.append(Home(wire, place, total, *results[k], width, rows))

    def finish(k):
        sums[k].last()
        homes[k].start(local(26 + k))

    def store(scatter, result):
        scatter.last()
        copy = pltpu.make_async_copy(scatter.total, result, scatter.sem)
        copy.start()
        copy.wait()

    alone = layer.vec_all.shape[0] == 1
    gather = None if alone else VectorGather(wire, place, layer.vec_own, layer.vec_all)

    def vector_in_start():
        if not alone:
            gather.start(local(18))

    def vector_in_pass():
        if not alone:
            gather.wait()
            gather.line.own_from_ends()
            gather.line.own_from_middle()

    def vector_in_rest():
        if alone:
            copy = pltpu.make_async_copy(layer.vec_own, layer.vec_all, local(18))
            copy.start()
            copy.wait()
        else:
            for step in range(1, n_zero):
                gather.line.ahead(step)
        lay_out_vectors(layer, place)

    pieces = DenseExchange(
        wire, place, lambda c: layer.pieces_out.at[c], lambda c: layer.pieces_in.at[c]
    )
    vector_line = LineGather(wire, place, layer.vec_line, VEC_ROWS)
    vector_spread = DenseExchange(
        wire, place, lambda c: layer.vec_total, lambda c: layer.vec_sums.at[c]
    )

    def vector_out_start():
        partial_vectors(layer)
        pieces.start(local(18))

    def vector_out_pass():
        pieces.wait()
        own = vector_line.block(place.z)
        own_vectors(layer, own)
        vector_line.own_from_ends()
        vector_line.own_from_middle()

    def vector_out_spread():
        total = layer.vec_line[pl.ds(0, VEC_ROWS), :]
        for j in range(1, n_zero):
            total = total + layer.vec_line[pl.ds(j * VEC_ROWS, VEC_ROWS), :]
        layer.vec_total[...] = total
        vector_spread.start(local(19))

    place.barrier()
    layer.clear()
    exchanges[0].start(local(12))
    vector_in_start()
    exchanges[2].start(local(14))
    exchanges[0].wait()
    dn.own_from_ends()
    dn.own_from_middle()
    exchanges[1].start(local(13))
    vector_in_pass()
    dn.ahead(1)
    exchanges[2].wait()
    up.own_from_ends()
    x.start(local(10))
    g.start(local(11))
    up.own_from_middle()
    dn.ahead(2)
    vector_in_rest()
    exchanges[1].wait()
    qk.own_from_ends()
    up.ahead(1)
    x.turn()
    qk.own_from_middle()
    for step in range(3, n_zero):
        dn.ahead(step)
    g.turn()
    x.turn_again()
    x.wait()
    exchanges[3].start(local(15))
    up.ahead(2)
    layer.normalise(0, 2)
    g.turn_again()
    layer.normalise(1, 2)
    qk.ahead(1)
    for step in range(3, n_zero):
        up.ahead(step)
    dense_in.start(local(16))
    exchanges[3].wait()
    wt.own_from_ends()
    layer.expand()
    qk.ahead(2)
    wt.own_from_middle()
    g.wait()
    layer.down_gradient()
    sums[4].launch(0)
    sums[5].launch(0)
    for step in range(3, n_zero):
        qk.ahead(step)
    dense_in.wait()
    layer.attend(0)
    sums[4].launch(1)
    sums[5].launch(1)
    wt.ahead(1)
    layer.attend(1)
    sums[4].launch(2)
    layer.qkv_gradient()
    sums[5].launch(2)
    sums[5].advance(1)
    sums[1].launch(0)
    sums[4].advance(1)
    wt.ahead(2)
    layer.dense_gradient()
    dense_out.start(local(17))
    layer.back_one()
    for step in range(3, n_zero):
        wt.ahead(step)
    sums[5].advance(2)
    sums[1].launch(1)
    layer.contract_back()
    sums[4].advance(2)
    finish(5)
    layer.output()
    sums[1].launch(2)
    out.start()
    finish(4)
    layer.up_gradient()
    dense_out.wait()
    sums[2].launch(0)
    out.turn()
    sums[0].launch(0)
    sums[2].launch(1)
    homes[5].wait()
    sums[0].launch(1)
    sums[1].advance(1)
    layer.back_two()
    tok.start()
    out.turn_again()
    sums[1].advance(2)
    sums[3].launch(0)
    vector_out_start()
    sums[2].launch(2)
    sums[2].advance(1)
    tok.turn()
    sums[0].advance(1)
    tok.turn_again()
    sums[3].launch(1)
    sums[0].launch(2)
    finish(1)
    sums[2].advance(2)
    sums[3].advance(1)
    sums[0].advance(2)
    sums[3].launch(2)
    finish(2)
    store(out, layer.out_sum)
    homes[4].wait()
    sums[3].advance(2)
    vector_out_pass()
    finish(0)
    homes[1].wait()
    finish(3)
    homes[2].wait()
    vector_line.ahead(1)
    store(tok, layer.tok_sum)
    for step in range(2, n_zero):
        vector_line.ahead(step)
    vector_out_spread()
    homes[3].wait()
    homes[0].wait()
    vector_spread.wait()
    wire.finish()


def layer_call(n_zero, rows, tokens, *operands):
    local = tokens // PARTS
    block = rows * N_SEQ
    slots = slots_needed(n_zero)
    shards = (9 * D + FF) // (operands[6].shape[1] * CHUNK)
    vmem = lambda *dims: pltpu.VMEM(dims, BF)
    scratch = [
        vmem(tokens, HEAD_W),
        vmem(tokens, 3 * HEAD_W),
        pltpu.SemaphoreType.DMA((slots,)),
        pltpu.SemaphoreType.DMA((slots,)),
        pltpu.SemaphoreType.DMA((32,)),
        vmem(local, D),
        pltpu.VMEM((local, D), F32),
    ]
    wide = lambda *dims: pltpu.VMEM(dims, F32)
    scratch += [wide(4, D), wide(1, 3 * HEAD_W), wide(1, HID_W), wide(PARTS, 8, HEAD_W)]
    scratch += [wide(PARTS, 8, HEAD_W), wide(n_zero * VEC_ROWS, HEAD_W), wide(VEC_ROWS, HEAD_W)]
    scratch += [wide(8, width) for _, width in TOTALS]
    for _ in range(2):
        scratch += [vmem(2, 2, local, D), vmem(local, D), vmem(local, D), vmem(local, D)]
    for width in WIDTHS:
        scratch += [vmem(n_zero + 1, block, width), vmem(block, width), vmem(block, width)]
    homes = [
        jax.ShapeDtypeStruct((N_DP, N_SEQ, rows, width), BF)
        for width in (HEAD_W, 3 * HEAD_W, HID_W, HID_W)
    ]
    anywhere = pl.BlockSpec(memory_space=pl.ANY)
    vector = pl.BlockSpec(memory_space=pltpu.VMEM)
    held = buffers(tokens)
    return pl.pallas_call(
        functools.partial(layer_body, n_zero, rows, tokens),
        in_specs=[anywhere] * 7 + [vector] * 3,
        out_specs=[anywhere] * (len(RESULTS) - 2) + [vector] * 2 + [anywhere] * len(held),
        out_shape=[jax.ShapeDtypeStruct((local, D), F32)] * 2
        + homes
        + [
            jax.ShapeDtypeStruct((shards,) + operands[6].shape[1:], F32),
            jax.ShapeDtypeStruct((PARTS, VEC_ROWS, HEAD_W), F32),
        ]
        + [jax.ShapeDtypeStruct(shape, BF) for shape in held.values()],
        scratch_shapes=scratch,
        compiler_params=pltpu.CompilerParams(
            collective_id=0, has_side_effects=True, vmem_limit_bytes=62 * 1024 * 1024
        ),
        name="layer",
    )(*operands)


def update(gradient, held, results):
    param, first, second = (ref[...] for ref in held)
    for ref, value in zip(results, adam_step(param, gradient, first, second, WEIGHT_DECAY)):
        ref[...] = value
    results[3][...] = gradient


def finish_body(*refs):
    refs = list(refs)
    take = lambda count: [refs.pop(0) for _ in range(count)]
    up_home, wt_home, dn_home, *qk_homes = take(6)
    up, down, dense, qkv = (take(3) for _ in range(4))
    x, g, out_sum, tok_sum, bias = take(5)
    results = [take(4) for _ in range(4)]
    outputs, input_grad = take(2)
    update(up_home[0, 0].astype(F32), up, results[0])
    update(wt_home[0, 0].astype(F32).T, down, results[1])
    update(dn_home[0, 0].astype(F32), dense, results[2])
    columns = jnp.concatenate([home[0, 0] for home in qk_homes], axis=1)
    update(columns.astype(F32), qkv, results[3])
    tokens = x[...].astype(F32)
    outputs[...] = (tokens + out_sum[...] + bias[...]).astype(BF)
    centred = tokens - jnp.mean(tokens, axis=1, keepdims=True)
    spread = jnp.mean(centred * centred, axis=1, keepdims=True)
    rate = lax.rsqrt(spread + NORM_EPSILON)
    xhat = centred * rate
    d_xhat = tok_sum[...]
    d_tokens = rate * (
        d_xhat
        - jnp.mean(d_xhat, axis=1, keepdims=True)
        - xhat * jnp.mean(d_xhat * xhat, axis=1, keepdims=True)
    )
    input_grad[...] = (g[...].astype(F32) + d_tokens).astype(BF)


def finish_call(homes, states, x, g, out_sum, tok_sum, bias):
    up_home, wt_home, dn_home, qk_home = homes
    rows = up_home.shape[2]
    home = lambda width: pl.BlockSpec((1, 1, rows, width), lambda c: (c // N_SEQ, c % N_SEQ, 0, 0))

    def third(k):
        def at(c):
            unit = 3 * c + k
            part = unit % PARTS
            return (part // N_SEQ, part % N_SEQ, 0, unit // PARTS)

        return pl.BlockSpec((1, 1, rows, HEAD_W), at)

    columns = lambda width: pl.BlockSpec((rows, width), lambda c: (0, c))
    blocks = (columns(HID_W), pl.BlockSpec((HID_W, rows), lambda c: (c, 0)), columns(HEAD_W), columns(3 * HEAD_W))
    some = pl.BlockSpec((x.shape[0] // PARTS, D), lambda c: (c, 0))
    whole = pl.BlockSpec((1, D), lambda c: (0, 0))
    return pl.pallas_call(
        finish_body,
        grid=(PARTS,),
        in_specs=[home(HID_W), home(HID_W), home(HEAD_W)]
        + [third(k) for k in range(3)]
        + [block for block in blocks for _ in range(3)]
        + [some] * 4
        + [whole],
        out_specs=[block for block in blocks for _ in range(4)] + [some] * 2,
        out_shape=[jax.ShapeDtypeStruct(state[0].shape, F32) for state in states for _ in range(4)]
        + [jax.ShapeDtypeStruct(x.shape, BF)] * 2,
        compiler_params=pltpu.CompilerParams(vmem_limit_bytes=60 * 1024 * 1024),
        name="finish",
    )(
        up_home,
        wt_home,
        dn_home,
        qk_home,
        qk_home,
        qk_home,
        *(array for state in states for array in state),
        x,
        g,
        out_sum,
        tok_sum,
        bias,
    )


def pack_body(half, *refs):
    dense, query, key, value, up, down, g, dn_low, qk_low, up_low, wt_low, g_total = refs

    @pl.when(pl.program_id(0) == 0)
    def _():
        g_total[...] = jnp.zeros_like(g_total)

    column_sums(g_total, g[...].astype(F32))
    dn_low[0] = dense[...].astype(BF)
    qk_low[0] = jnp.concatenate([query[...], key[...], value[...]], axis=1).astype(BF)
    up_low[0] = up[...].astype(BF)
    wt_low[0] = down[...].T.astype(BF)


def pack(half, qkv_weight, dense_weight, up_weight, down_weight, g):
    rows = qkv_weight.shape[0]
    columns = lambda width, t: pl.BlockSpec((rows, width), lambda s, h: (0, t * PARTS + h[0] * N_SEQ + s))
    widths = (HEAD_W, 3 * HEAD_W, HID_W, HID_W)
    return pl.pallas_call(
        pack_body,
        grid_spec=pltpu.PrefetchScalarGridSpec(
            num_scalar_prefetch=1,
            grid=(N_SEQ,),
            in_specs=[columns(HEAD_W, 0)]
            + [columns(HEAD_W, t) for t in range(3)]
            + [columns(HID_W, 0), pl.BlockSpec((HID_W, rows), lambda s, h: (h[0] * N_SEQ + s, 0))]
            + [pl.BlockSpec((g.shape[0] // N_SEQ, D), lambda s, h: (s, 0))],
            out_specs=[pl.BlockSpec((1, rows, width), lambda s, h: (s, 0, 0)) for width in widths]
            + [pl.BlockSpec((8, D), lambda s, h: (0, 0))],
        ),
        out_shape=[jax.ShapeDtypeStruct((N_SEQ, rows, width), BF) for width in widths]
        + [jax.ShapeDtypeStruct((8, D), F32)],
        compiler_params=pltpu.CompilerParams(vmem_limit_bytes=62 * 1024 * 1024),
        name="pack",
    )(half, dense_weight, qkv_weight, qkv_weight, qkv_weight, up_weight, down_weight, g)


def rotary_rows(length):
    exponent = np.arange(ROT // 2, dtype=np.float32) * np.float32(2.0 / ROT)
    inverse = np.power(np.float32(10000.0), -exponent)
    angles = np.arange(length, dtype=np.float32)[:, None] * inverse[None, :]
    cosine, sine = np.cos(angles), np.sin(angles)
    ones = np.ones((length, 128 - ROT), np.float32)
    cosine = np.concatenate([cosine, cosine, ones], axis=1)
    sine = np.concatenate([-sine, sine, 0.0 * ones], axis=1)
    return jnp.asarray(cosine), jnp.asarray(sine)


def make_body(sizes):
    n_zero = sizes["zero"]
    everywhere = ("dp", "zero", "seq")

    def body(
        inputs,
        out_grad,
        vectors,
        qkv_weight,
        dense_weight,
        up_weight,
        down_weight,
        vectors_first,
        qkv_first,
        dense_first,
        up_first,
        down_first,
        vectors_second,
        qkv_second,
        dense_second,
        up_second,
        down_second,
    ):
        dp_i, zero_i, seq_i = (lax.axis_index(axis) for axis in everywhere)
        seqs_here, local_len = inputs.shape[0], inputs.shape[1]
        token_rows = seqs_here * local_len
        rows = qkv_weight.shape[0]

        tokens_low = inputs.reshape(token_rows, D)
        grad_low = out_grad.reshape(token_rows, D)
        dn_low, qk_low, up_low, wt_low, d_out_bias = pack(
            dp_i.astype(jnp.int32).reshape(1), qkv_weight, dense_weight, up_weight, down_weight, grad_low
        )
        tokens = N_DP * N_SEQ * token_rows
        vec_low = lax.reduce_precision(vectors, exponent_bits=8, mantissa_bits=7)
        if vectors.shape[0] % CHUNK == 0:
            vec_low = vec_low.reshape(1, -1, CHUNK)
        else:
            vec_low = lax.all_gather(vec_low, ("zero", "seq"), axis=0, tiled=True).reshape(1, -1, CHUNK)
        results = layer_call(
            n_zero,
            rows,
            tokens,
            tokens_low,
            grad_low,
            dn_low,
            qk_low,
            up_low,
            wt_low,
            vec_low,
            d_out_bias,
            *rotary_rows(tokens // N_DP),
        )
        out_sum, d_xhat, dn_home, qk_home, up_home, wt_home, vec_all, vec_sums = results[: len(RESULTS)]
        vec_flat = vec_all.reshape(-1)
        dense_bias, down_bias = vec_flat[5 * D : 6 * D], vec_flat[8 * D + FF : 9 * D + FF]

        row = lambda k: vec_sums[:, k].reshape(-1)
        vector_sum = jnp.concatenate(
            [
                row(0),
                row(1),
                vec_sums[:, 8:11].transpose(1, 0, 2).reshape(-1),
                row(4),
                row(2),
                row(3),
                vec_sums[:, 11:15].reshape(-1),
                row(4),
            ]
        )
        vectors_grad = lax.dynamic_slice_in_dim(
            vector_sum, (zero_i * N_SEQ + seq_i) * vectors.shape[0], vectors.shape[0], 0
        )

        vec_upd = adam_step(vectors, vectors_grad, vectors_first, vectors_second, 0.0) + (vectors_grad,)
        *changed, outputs, input_grad = finish_call(
            (up_home, wt_home, dn_home, qk_home),
            (
                (up_weight, up_first, up_second),
                (down_weight, down_first, down_second),
                (dense_weight, dense_first, dense_second),
                (qkv_weight, qkv_first, qkv_second),
            ),
            tokens_low,
            grad_low,
            out_sum,
            d_xhat,
            (dense_bias + down_bias).reshape(1, D),
        )
        outputs, input_grad = outputs.reshape(inputs.shape), input_grad.reshape(inputs.shape)
        up_upd, down_upd, dense_upd, qkv_upd = (tuple(changed[4 * k : 4 * k + 4]) for k in range(4))
        updates = (vec_upd, qkv_upd, dense_upd, up_upd, down_upd)
        picked = lambda k: tuple(update[k] for update in updates)
        return (outputs, input_grad) + picked(3) + picked(0) + picked(1) + picked(2)

    return body


def solution(mesh):
    wide = P(("dp", "zero"), "seq", None)
    vector = P(("zero", "seq"))
    rows = P(("zero", "seq"), None)
    columns = P(None, ("zero", "seq"))
    state = (vector, rows, rows, rows, columns)
    return jax.shard_map(
        make_body(dict(mesh.shape)),
        mesh=mesh,
        in_specs=(wide, wide) + state * 3,
        out_specs=(wide, wide) + state * 4,
        check_vma=False,
    )
```
